32 devices in a mesh: pipe: 2 (over core), dp: 4 (over y, x), rows: 4 (over z).
Axes of the slice: x: 2, y: 2, z: 4, core: 2. Of those that a mesh axis runs over, the one named last changes fastest.
Arguments:
- x_in: bfloat16 [4, 4, 8, 32, 512], P(None, 'dp', 'rows'), may hold values from -6 to 6
- pool_index: int32 [4, 4, 4, 16], P(None, 'dp', 'rows'), may hold values from 0 to 3
- task_mask: int32 [4, 4, 3], P(None, 'dp'), may hold values from 0 to 1, as said below
- task_cot: bfloat16 [3, 4, 4, 8, 32, 512], P(None, None, 'dp', 'rows'), may hold values from -8 to 8
- trunk_conv: bfloat16 [2, 2, 4608, 512], P('pipe', None, ('dp', 'rows')), may hold values from -0.09375 to 0.09375
- norm_gain: bfloat16 [2, 2, 512], P('pipe', None, ('dp', 'rows')), may hold values from 0.25 to 1.75
- norm_bias: bfloat16 [2, 2, 512], P('pipe', None, ('dp', 'rows')), may hold values from -3 to 3
- att_down: bfloat16 [2, 3, 512, 128], P('pipe', None, ('dp', 'rows')), may hold values from -0.25 to 0.25
- attention_up_weights: bfloat16 [2, 3, 128, 512], P('pipe', None, None, ('dp', 'rows')), may hold values from -1 to 1
- task_conv: bfloat16 [2, 3, 4608, 512], P('pipe', None, ('dp', 'rows')), may hold values from -0.09375 to 0.09375
Outputs:
- task_features: bfloat16 [2, 3, 4, 4, 8, 32, 512], P('pipe', None, None, 'dp', 'rows')
- input_grads: float32 [2, 4, 4, 8, 32, 512], P('pipe', None, 'dp', 'rows')
- trunk_grad: float32 [2, 2, 4608, 512], P('pipe', None, ('dp', 'rows'))
- gain_grad: float32 [2, 2, 512], P('pipe', None, ('dp', 'rows'))
- bias_grad: float32 [2, 2, 512], P('pipe', None, ('dp', 'rows'))
- down_grad: float32 [2, 3, 512, 128], P('pipe', None, ('dp', 'rows'))
- up_grad: float32 [2, 3, 128, 512], P('pipe', None, None, ('dp', 'rows'))
- task_grad: float32 [2, 3, 4608, 512], P('pipe', None, ('dp', 'rows'))
- nash_weights: float32 [3], replicated
The draws below stay inside these ranges and needn't reach their ends.
Inputs may be any that keep to these rules, and one draw needn't show every extreme that they name: `task_mask`: each sample is labelled for one or two tasks.
All inputs are finite; a program needn't handle non-finite values.
Results may differ from the reference program's by a relative error of at most 0.018.
Values may be sent and summed in bfloat16 or wider, within the bound.
No kernel may reach another device: no remote copies, remote signals or barrier semaphores. Data moves between devices by JAX's collectives and lax.ppermute only.
A program may use at most 384 MiB of HBM per device.

```python
import jax
import jax.numpy as jnp
from jax import lax

C = 512
ATT = 128
TASKS = 3
MICRO = 4
NASH_ITERS = 3
COLS = 32
BATCH = 4
HEIGHT = 8


def draw_task_mask(key, part):
    key = jax.random.fold_in(key, 11)
    subkeys = jax.random.split(key, 3)
    primary = jax.random.randint(subkeys[0], (MICRO, BATCH), 0, TASKS)
    distance = jax.random.randint(subkeys[1], (MICRO, BATCH), 1, TASKS)
    paired = jax.random.randint(subkeys[2], (MICRO, BATCH), 0, 2)
    secondary = (primary + distance) % TASKS
    labels = jnp.arange(TASKS, dtype=jnp.int32)
    first_hot = (primary[..., None] == labels).astype(jnp.int32)
    second_hot = (secondary[..., None] == labels).astype(jnp.int32)
    return first_hot + paired[..., None] * second_hot


def draw_task_cot(key, part):
    key = jax.random.fold_in(key, 17)
    subkeys = jax.random.split(key, 2)
    full_shape = (TASKS, MICRO, BATCH, HEIGHT, COLS, C)
    common = jax.random.normal(subkeys[0], (1,) + full_shape[1:], jnp.float32)
    own = jax.random.normal(subkeys[1], full_shape, jnp.float32)
    return jnp.clip(0.6 * common + 0.8 * own, -8.0, 8.0).astype(jnp.bfloat16)


def set_ends(result, key, low, largest):
    index_at = [jax.random.randint(jax.random.fold_in(key, axis), (), 0, length) for axis, length in enumerate(result.shape)]
    widest = result.shape.index(max(result.shape))
    beside = index_at[:widest] + [(index_at[widest] + 1) % result.shape[widest]] + index_at[widest + 1:]
    return result.at[tuple(index_at)].set(low).at[tuple(beside)].set(largest)


def shard_levels(own_key, shape, cuts, least, largest):
    gain, own = 1.0, jax.random.fold_in(own_key, 6)
    for axis_at, parts in cuts:
        draws = jnp.exp(jax.random.uniform(jax.random.fold_in(own, axis_at), (parts,), jnp.float32, least / len(cuts), largest / len(cuts)))
        gain = gain * jnp.repeat(draws, shape[axis_at] // parts).reshape([-1 if axis == axis_at else 1 for axis in range(len(shape))])
    return gain


def gaussian(stream_key, extent, deviation, limit, cuts=(), kind=jnp.bfloat16):
    result = jax.random.normal(stream_key, extent, jnp.float32) * deviation
    if len(cuts) > 0:
        result = shard_levels(stream_key, extent, cuts, -0.22, 0.18) * result
    return jnp.clip(result, min=-limit, max=limit).astype(kind)


def setup_inputs(seed: int = 0) -> dict:
    key_of = jax.random.split(jax.random.key(seed), 11)
    x_in = gaussian(key_of[0], (MICRO, BATCH, HEIGHT, COLS, C), 1.0, 6.0, ((1, 4), (2, 4)))
    pool_index = set_ends(jax.random.randint(key_of[1], (MICRO, BATCH, HEIGHT // 2, COLS // 2), 0, 4), jax.random.fold_in(key_of[1], 1), 0, 3).astype(jnp.int32)
    task_mask = draw_task_mask(jax.random.fold_in(key_of[10], 71), 0)
    task_cot = draw_task_cot(jax.random.fold_in(key_of[10], 71), 0)
    trunk_conv = gaussian(key_of[4], (2, 2, 9 * C, C), (9 * C) ** -0.5, 0.09375, ((0, 2), (2, 16)))
    norm_gain = jnp.clip(1.0 + 0.15 * jax.random.normal(key_of[5], (2, 2, C), jnp.float32), 0.25, 1.75).astype(jnp.bfloat16)
    norm_bias = gaussian(key_of[6], (2, 2, C), 0.5, 3.0, ((0, 2), (2, 16)))
    att_down = gaussian(key_of[7], (2, TASKS, C, ATT), C ** -0.5, 0.25, ((0, 2), (2, 16)))
    attention_up_weights = gaussian(key_of[8], (2, TASKS, ATT, C), (ATT // 4) ** -0.5, 1.0, ((0, 2), (3, 16)))
    task_conv = gaussian(key_of[9], (2, TASKS, 9 * C, C), (9 * C) ** -0.5, 0.09375, ((0, 2), (2, 16)))
    return {"x_in": x_in, "pool_index": pool_index, "task_mask": task_mask, "task_cot": task_cot, "trunk_conv": trunk_conv, "norm_gain": norm_gain, "norm_bias": norm_bias, "att_down": att_down, "attention_up_weights": attention_up_weights, "task_conv": task_conv}


@jax.custom_vjp
def low(v):
    return lax.optimization_barrier(v.astype(jnp.bfloat16)).astype(jnp.float32)

@jax.custom_vjp
def low_back(v):
    return v

def low_keep(v):
    return (low(v), None)

def low_pass(kept, grad):
    return (grad,)

def back_keep(v):
    return (v, None)

def back_low(kept, grad):
    return (low(grad),)
low.defvjp(low_keep, low_pass)
low_back.defvjp(back_keep, back_low)
eps = 1e-05

def pool_cells(field, positions):
    leading = field.shape[:-4]
    samples, rows_n, cols_n, channels = field.shape[-4:]
    blocks = field.astype(jnp.float32).reshape(leading + (samples, rows_n // 2, 2, cols_n // 2, 2, channels))
    blocks = jnp.moveaxis(blocks, -4, -3).reshape(leading + (samples, rows_n // 2, cols_n // 2, 4, channels))
    return lax.optimization_barrier(jnp.sum(blocks * positions[..., None], axis=-2))

def unpool_cells(small, positions):
    leading = small.shape[:-4]
    samples, rows_h, cols_h, channels = small.shape[-4:]
    blocks = small.astype(jnp.float32)[..., None, :] * positions[..., None]
    blocks = blocks.reshape(leading + (samples, rows_h, cols_h, 2, 2, channels))
    blocks = jnp.moveaxis(blocks, -3, -4)
    return blocks.reshape(leading + (samples, 2 * rows_h, 2 * cols_h, channels))

def conv_same(field, weight):
    channels = field.shape[-1]
    rows_n, cols_n = (field.shape[1], field.shape[2])
    padded = jnp.pad(field, ((0, 0), (1, 1), (1, 1), (0, 0)))
    summed = jnp.zeros(field.shape[:3] + (weight.shape[-1],), jnp.float32)
    for offset in range(9):
        near = padded[:, offset // 3:offset // 3 + rows_n, offset % 3:offset % 3 + cols_n, :]
        summed = summed + jnp.einsum('brwc,cd->brwd', near, weight[offset * channels:(offset + 1) * channels], precision=lax.Precision.HIGHEST)
    return summed

def trunk_pass(section_input, convs, gain_rows, bias_rows):
    hidden = section_input
    for section_layer in range(2):
        conv_out = low_back(conv_same(low(hidden), convs[section_layer]))
        center = lax.optimization_barrier(jnp.mean(conv_out, axis=(0, 1, 2)))
        spread = lax.optimization_barrier(jnp.mean((conv_out - center) ** 2, axis=(0, 1, 2)))
        normed = (conv_out - center) * lax.rsqrt(spread + eps)
        hidden = jax.nn.silu(gain_rows[section_layer] * normed + bias_rows[section_layer])
    return hidden

def task_branch(shared, carried, down, up, weight):
    mixture = low(shared + carried)
    inner_act = low_back(jnp.einsum('brwc,ca->brwa', mixture, down, precision=lax.Precision.HIGHEST))
    active_mask_flag = low(jax.nn.silu(inner_act))
    class_logits = low_back(jnp.einsum('brwa,ac->brwc', active_mask_flag, up, precision=lax.Precision.HIGHEST))
    gating = jax.nn.sigmoid(class_logits)
    return low_back(conv_same(low(gating * shared), weight))

def one_batch(params, x_block, positions, probe_x, probe_in):
    convs, gain_rows, bias_rows, downs, ups, task_maps = params
    shared = low(trunk_pass(x_block, convs[0], gain_rows[0], bias_rows[0]))
    encoder_features = [task_branch(shared, 0.0, downs[0, task_index], ups[0, task_index], task_maps[0, task_index]) for task_index in range(TASKS)]
    outgoing = low_back(pool_cells(shared, positions))
    carried = [low_back(pool_cells(low(feature), positions)) for feature in encoder_features]
    dec_input = unpool_cells(outgoing, positions) + probe_in
    shared_dec = low(trunk_pass(dec_input, convs[1], gain_rows[1], bias_rows[1]))
    dec_feats = [task_branch(shared_dec + probe_x[task_index], unpool_cells(carried[task_index], positions), downs[1, task_index], ups[1, task_index], task_maps[1, task_index]) for task_index in range(TASKS)]
    return jnp.stack([jnp.stack(encoder_features), jnp.stack(dec_feats)])

def solve_small(matrix, right_side):
    cofactor = [[matrix[1, 1] * matrix[2, 2] - matrix[1, 2] * matrix[2, 1], matrix[1, 2] * matrix[2, 0] - matrix[1, 0] * matrix[2, 2], matrix[1, 0] * matrix[2, 1] - matrix[1, 1] * matrix[2, 0]], [matrix[0, 2] * matrix[2, 1] - matrix[0, 1] * matrix[2, 2], matrix[0, 0] * matrix[2, 2] - matrix[0, 2] * matrix[2, 0], matrix[0, 1] * matrix[2, 0] - matrix[0, 0] * matrix[2, 1]], [matrix[0, 1] * matrix[1, 2] - matrix[0, 2] * matrix[1, 1], matrix[0, 2] * matrix[1, 0] - matrix[0, 0] * matrix[1, 2], matrix[0, 0] * matrix[1, 1] - matrix[0, 1] * matrix[1, 0]]]
    determinant = matrix[0, 0] * cofactor[0][0] + matrix[0, 1] * cofactor[0][1] + matrix[0, 2] * cofactor[0][2]
    answer = [(cofactor[0][col_index] * right_side[0] + cofactor[1][col_index] * right_side[1] + cofactor[2][col_index] * right_side[2]) / determinant for col_index in range(3)]
    return jnp.stack(answer)

def nash_solve(gram_sum):
    trace_mean = (gram_sum[0, 0] + gram_sum[1, 1] + gram_sum[2, 2]) / 3.0 + 1e-06
    normalized = gram_sum / trace_mean
    diagonal = jnp.stack([normalized[0, 0], normalized[1, 1], normalized[2, 2]])
    nash_alpha = lax.rsqrt(diagonal + 1e-06)
    for sweep_index in range(NASH_ITERS):
        residual = lax.optimization_barrier(jnp.sum(normalized * nash_alpha[None, :], axis=1)) - 1.0 / nash_alpha
        curvature = normalized + jnp.diag(1.0 / (nash_alpha * nash_alpha))
        update = solve_small(curvature, residual)
        nash_alpha = nash_alpha * jnp.exp(-0.5 * jnp.tanh(update / nash_alpha))
    return nash_alpha

def inner_products(flattened):
    rows_list = []
    for first_task in range(TASKS):
        entries = [jnp.sum(flattened[first_task] * flattened[second_task]) for second_task in range(TASKS)]
        rows_list.append(jnp.stack(entries))
    return jnp.stack(rows_list)

def reference(x_in, pool_index, task_mask, task_cot, trunk_conv, norm_gain, norm_bias, att_down, attention_up_weights, task_conv):
    params = tuple((weight.astype(jnp.float32) for weight in (trunk_conv, norm_gain, norm_bias, att_down, attention_up_weights, task_conv)))
    inputs = x_in.astype(jnp.float32)
    positions = (pool_index[..., None] == jnp.arange(4, dtype=jnp.int32)).astype(jnp.float32)
    probe_x = jnp.zeros((MICRO, TASKS) + x_in.shape[1:], jnp.float32)
    probe_in = jnp.zeros(x_in.shape, jnp.float32)

    def network(params, inputs, probe_x, probe_in):

        def per_batch(pieces):
            return one_batch(params, pieces[0], pieces[1], pieces[2], pieces[3])
        return lax.map(jax.checkpoint(per_batch), (inputs, positions, probe_x, probe_in))
    features, pullback = jax.vjp(network, params, inputs, probe_x, probe_in)
    mask_weights = jnp.transpose(task_mask, (0, 2, 1)).astype(jnp.float32)
    plain_cot = jnp.transpose(task_cot, (1, 0, 2, 3, 4, 5)).astype(jnp.float32) * mask_weights[:, :, :, None, None, None]
    zero_cot = jnp.zeros_like(plain_cot)
    probe_pass = pullback(jnp.stack([zero_cot, plain_cot], axis=1))
    flattened = jnp.transpose(probe_pass[2], (1, 0, 2, 3, 4, 5)).reshape(TASKS, -1)
    gram_sum = inner_products(flattened)
    nash_alpha = nash_solve(gram_sum)
    weighted = nash_alpha[None, :, None, None, None, None] * plain_cot
    final_pass = pullback(jnp.stack([zero_cot, weighted], axis=1))
    grads = final_pass[0]
    task_features = jnp.transpose(features, (1, 2, 0, 3, 4, 5, 6)).astype(jnp.bfloat16)
    input_grads = jnp.stack([final_pass[1], final_pass[3]])
    return (task_features, input_grads, grads[0], grads[1], grads[2], grads[3], grads[4], grads[5], nash_alpha)
```

```python
import functools

import jax
import jax.numpy as jnp
from jax import lax
from jax.experimental import pallas as pl
from jax.experimental.pallas import tpu as pltpu
from jax.sharding import PartitionSpec as P

NASH_ITERS = 3


eps = 1e-05


def extended_2(array, sides, width):
    for axis, dim in sides:
        peers, length = (lax.axis_size(axis), array.shape[dim])
        up = [(i, (i + 1) % peers) for i in range(peers - 1)]
        down = [(j, i) for i, j in up]
        last = lax.slice_in_dim(array, length - width, length, axis=dim)
        first = lax.slice_in_dim(array, 0, width, axis=dim)
        before = lax.ppermute(last, axis, up)
        after = lax.ppermute(first, axis, down)
        array = jnp.concatenate([before, array, after], axis=dim)
    return array


def from_behind(array, axis, by):
    peers = lax.axis_size(axis)
    pairs = [(i, i + by) for i in range(peers) if 0 <= i + by < peers]
    return lax.ppermute(array, axis, pairs)


def silu_slope(preact):
    sigmoid_val = jax.nn.sigmoid(preact)
    return sigmoid_val * (1.0 + preact * (1.0 - sigmoid_val))


def choose_side(condition, when_true, when_false):

    def either(true_leaf, false_leaf):
        return jnp.where(condition, true_leaf, false_leaf)

    return jax.tree.map(either, when_true, when_false)


def pool_cells(field, positions):
    leading = field.shape[:-4]
    samples, rows_n, cols_n, channels = field.shape[-4:]
    blocks = field.astype(jnp.float32).reshape(
        leading + (samples, rows_n // 2, 2, cols_n // 2, 2, channels)
    )
    blocks = jnp.moveaxis(blocks, -4, -3).reshape(
        leading + (samples, rows_n // 2, cols_n // 2, 4, channels)
    )
    return jnp.sum(blocks * positions[..., None], axis=-2)


def unpool_cells(small, positions):
    leading = small.shape[:-4]
    samples, rows_h, cols_h, channels = small.shape[-4:]
    blocks = small.astype(jnp.float32)[..., None, :] * positions[..., None]
    blocks = blocks.reshape(leading + (samples, rows_h, cols_h, 2, 2, channels))
    blocks = jnp.moveaxis(blocks, -3, -4)
    return blocks.reshape(leading + (samples, 2 * rows_h, 2 * cols_h, channels))


def gather_taps(padded, rows_n, cols_n):
    stencil = [
        padded[:, :, offset // 3 : offset // 3 + rows_n, offset % 3 : offset % 3 + cols_n, :]
        for offset in range(9)
    ]
    return jnp.concatenate(stencil, axis=-1)


def conv_forward(field, weight):
    extended = extended_2(field, (("rows", 2),), 1)
    padded = jnp.pad(extended, ((0, 0), (0, 0), (0, 0), (1, 1), (0, 0)))
    stencil = gather_taps(padded, field.shape[2], field.shape[3])
    conv_out = jnp.einsum("ksrwq,kqd->ksrwd", stencil, weight, preferred_element_type=jnp.float32)
    return (conv_out, padded)


def conv_backward(padded, grad_out, weight, wanted):
    rows_n, cols_n = (grad_out.shape[2], grad_out.shape[3])
    extended = extended_2(grad_out, (("rows", 2),), 1)
    beside_all = jnp.pad(extended, ((0, 0), (0, 0), (0, 0), (1, 1), (0, 0)))
    flipped = jnp.stack(
        [
            beside_all[
                :,
                :,
                2 - offset // 3 : 2 - offset // 3 + rows_n,
                2 - offset % 3 : 2 - offset % 3 + cols_n,
                :,
            ]
            for offset in range(9)
        ],
        axis=-2,
    )
    kernel = weight.reshape(weight.shape[0], 9, weight.shape[2], weight.shape[2])
    grad_in = jnp.einsum("ksrwtd,ktcd->ksrwc", flipped, kernel, preferred_element_type=jnp.float32)
    weight_grad = None
    if wanted:
        weight_grad = jnp.einsum(
            "ksrwq,ksrwd->kqd",
            gather_taps(padded, rows_n, cols_n),
            grad_out,
            preferred_element_type=jnp.float32,
        )
    return (grad_in, weight_grad)


def norm_moments(conv_out, pixel_count):
    center = lax.psum(jnp.sum(conv_out, axis=(0, 1, 2, 3)), ("dp", "rows")) / pixel_count
    spread = (
        lax.psum(jnp.sum(jnp.square(conv_out - center), axis=(0, 1, 2, 3)), ("dp", "rows"))
        / pixel_count
    )
    return (center, lax.rsqrt(spread + eps))


def section_forward(section_input, carried, positions, params, stats, pixel_count):
    trunk_maps, gain_rows, bias_rows, down_maps, upward_maps, task_maps = params
    hidden = section_input[None]
    layers = []
    moments = []
    for section_layer in range(2):
        conv_out, padded = conv_forward(hidden, trunk_maps[section_layer][None])
        if stats is None:
            center, inverse_std = norm_moments(conv_out, pixel_count)
        else:
            center, inverse_std = stats[section_layer]
        normed = (conv_out - center) * inverse_std
        preact = gain_rows[section_layer] * normed + bias_rows[section_layer]
        layers.append((padded, normed, preact))
        moments.append((center, inverse_std))
        hidden = jax.nn.silu(preact).astype(jnp.bfloat16)
    mixture = (hidden.astype(jnp.float32) + carried.astype(jnp.float32)).astype(jnp.bfloat16)
    inner_act = jnp.einsum(
        "tsrwc,tca->tsrwa", mixture, down_maps, preferred_element_type=jnp.float32
    )
    active_mask_flag = jax.nn.silu(inner_act).astype(jnp.bfloat16)
    class_logits = jnp.einsum(
        "zfhpv,zvm->zfhpm", active_mask_flag, upward_maps, preferred_element_type=jnp.float32
    )
    gating = jax.nn.sigmoid(class_logits)
    product = (gating * hidden.astype(jnp.float32)).astype(jnp.bfloat16)
    features, padded_task = conv_forward(product, task_maps)
    return {
        "layers": layers,
        "moments": moments,
        "shared": hidden,
        "mixture": mixture,
        "inner_act": inner_act,
        "active": active_mask_flag,
        "gating": gating,
        "padded_task": padded_task,
        "features": features,
        "section_input": section_input,
        "carried": carried,
        "positions": positions,
    }


def heads_backward(saved_record, grad_feats, params, wanted):
    down_maps, upward_maps, task_maps = (params[3], params[4], params[5])
    task_back, task_slope = conv_backward(
        saved_record["padded_task"], grad_feats, task_maps, wanted
    )
    shared = saved_record["shared"].astype(jnp.float32)
    gating = saved_record["gating"]
    logits_gradient = (task_back * shared * gating * (1.0 - gating)).astype(jnp.bfloat16)
    grad_active = jnp.einsum(
        "qubef,qxf->qubex", logits_gradient, upward_maps, preferred_element_type=jnp.float32
    )
    grad_inner = (grad_active * silu_slope(saved_record["inner_act"])).astype(jnp.bfloat16)
    grad_mixture = jnp.einsum(
        "tsrwa,tca->tsrwc", grad_inner, down_maps, preferred_element_type=jnp.float32
    )
    through = task_back * gating + grad_mixture
    slopes = None
    if wanted:
        slope_up = jnp.einsum(
            "munfg,munfq->mgq",
            saved_record["active"],
            logits_gradient,
            preferred_element_type=jnp.float32,
        )
        slope_down = jnp.einsum(
            "tsrwc,tsrwa->tca",
            saved_record["mixture"],
            grad_inner,
            preferred_element_type=jnp.float32,
        )
        slopes = (slope_down, slope_up, task_slope)
    return (through, grad_mixture, slopes)


def trunk_backward(saved_record, grad_shared, params, pixel_count):
    trunk_maps, gain_rows = (params[0], params[1])
    grad_hidden = grad_shared
    conv_grads = [None, None]
    gain_grads = [None, None]
    bias_grads = [None, None]
    for section_layer in (1, 0):
        padded, normed, preact = saved_record["layers"][section_layer]
        inverse_std = saved_record["moments"][section_layer][1]
        grad_pre = grad_hidden * silu_slope(preact)
        bias_part = jnp.sum(grad_pre, axis=(0, 1, 2, 3))
        gain_part = jnp.sum(grad_pre * normed, axis=(0, 1, 2, 3))
        bias_total, gain_total = lax.psum((bias_part, gain_part), ("dp", "rows"))
        grad_conv = (
            inverse_std
            * gain_rows[section_layer]
            * (grad_pre - bias_total / pixel_count - normed * gain_total / pixel_count)
        )
        grad_hidden, weight_grad = conv_backward(
            padded, grad_conv.astype(jnp.bfloat16), trunk_maps[section_layer][None], True
        )
        conv_grads[section_layer] = weight_grad[0]
        gain_grads[section_layer] = gain_part
        bias_grads[section_layer] = bias_part
    return (grad_hidden, jnp.stack(conv_grads), jnp.stack(gain_grads), jnp.stack(bias_grads))


def solve_small(matrix, right_side):
    cofactor = [
        [
            matrix[1, 1] * matrix[2, 2] - matrix[1, 2] * matrix[2, 1],
            matrix[1, 2] * matrix[2, 0] - matrix[1, 0] * matrix[2, 2],
            matrix[1, 0] * matrix[2, 1] - matrix[1, 1] * matrix[2, 0],
        ],
        [
            matrix[0, 2] * matrix[2, 1] - matrix[0, 1] * matrix[2, 2],
            matrix[0, 0] * matrix[2, 2] - matrix[0, 2] * matrix[2, 0],
            matrix[0, 1] * matrix[2, 0] - matrix[0, 0] * matrix[2, 1],
        ],
        [
            matrix[0, 1] * matrix[1, 2] - matrix[0, 2] * matrix[1, 1],
            matrix[0, 2] * matrix[1, 0] - matrix[0, 0] * matrix[1, 2],
            matrix[0, 0] * matrix[1, 1] - matrix[0, 1] * matrix[1, 0],
        ],
    ]
    determinant = (
        matrix[0, 0] * cofactor[0][0]
        + matrix[0, 1] * cofactor[0][1]
        + matrix[0, 2] * cofactor[0][2]
    )
    answer = [
        (
            cofactor[0][col_index] * right_side[0]
            + cofactor[1][col_index] * right_side[1]
            + cofactor[2][col_index] * right_side[2]
        )
        / determinant
        for col_index in range(3)
    ]
    return jnp.stack(answer)


def nash_solve(gram_sum):
    trace_mean = (gram_sum[0, 0] + gram_sum[1, 1] + gram_sum[2, 2]) / 3.0 + 1e-06
    normalized = gram_sum / trace_mean
    diagonal = jnp.stack([normalized[0, 0], normalized[1, 1], normalized[2, 2]])
    nash_alpha = lax.rsqrt(diagonal + 1e-06)
    for sweep_index in range(NASH_ITERS):
        residual = jnp.sum(normalized * nash_alpha[None, :], axis=1) - 1.0 / nash_alpha
        curvature = normalized + jnp.diag(1.0 / (nash_alpha * nash_alpha))
        update = solve_small(curvature, residual)
        nash_alpha = nash_alpha * jnp.exp(-0.5 * jnp.tanh(update / nash_alpha))
    return nash_alpha


def on_device(
    x_in,
    pool_index,
    task_mask,
    task_cot,
    trunk_conv,
    norm_gain,
    norm_bias,
    att_down,
    attention_up_weights,
    task_conv,
):
    micro_count = x_in.shape[0]
    tasks_n = task_cot.shape[0]
    decoder_side = lax.axis_index("pipe") == 1
    pixel_count = (
        x_in.shape[1] * x_in.shape[2] * x_in.shape[3] * lax.axis_size("dp") * lax.axis_size("rows")
    )
    pieces = (
        lax.all_gather(trunk_conv, ("dp", "rows"), axis=2, tiled=True),
        lax.all_gather(norm_gain, ("dp", "rows"), axis=2, tiled=True),
        lax.all_gather(norm_bias, ("dp", "rows"), axis=2, tiled=True),
        lax.all_gather(att_down, ("dp", "rows"), axis=2, tiled=True),
        lax.all_gather(attention_up_weights, ("dp", "rows"), axis=3, tiled=True),
        lax.all_gather(task_conv, ("dp", "rows"), axis=2, tiled=True),
    )
    params = (
        pieces[0][0],
        pieces[1][0].astype(jnp.float32),
        pieces[2][0].astype(jnp.float32),
        pieces[3][0],
        pieces[4][0],
        pieces[5][0],
    )
    onehot = (pool_index[..., None] == jnp.arange(4, dtype=jnp.int32)).astype(jnp.float32)
    mask_weights = jnp.transpose(task_mask, (0, 2, 1)).astype(jnp.float32)
    no_carry = jnp.zeros((tasks_n,) + x_in.shape[1:], jnp.bfloat16)
    incoming = jnp.zeros(
        (tasks_n + 1, x_in.shape[1], x_in.shape[2] // 2, x_in.shape[3] // 2, x_in.shape[4]),
        jnp.bfloat16,
    )
    records = []
    for period in range(micro_count + 1):
        enc_index = min(period, micro_count - 1)
        dec_index = max(period - 1, 0)
        positions = jnp.where(decoder_side, onehot[dec_index], onehot[enc_index])
        section_input = jnp.where(
            decoder_side, unpool_cells(incoming[0], positions).astype(jnp.bfloat16), x_in[enc_index]
        )
        carried = jnp.where(
            decoder_side, unpool_cells(incoming[1:], positions).astype(jnp.bfloat16), no_carry
        )
        saved_record = section_forward(section_input, carried, positions, params, None, pixel_count)
        records.append(saved_record)
        if period < micro_count:
            outgoing = jnp.concatenate(
                [
                    pool_cells(saved_record["shared"], positions),
                    pool_cells(saved_record["features"].astype(jnp.bfloat16), positions),
                ],
                axis=0,
            )
            incoming = from_behind(outgoing.astype(jnp.bfloat16), "pipe", 1)
    kept_records = []
    gram_sum = jnp.zeros((tasks_n, tasks_n), jnp.float32)
    for micro_index in range(micro_count):
        source_input = choose_side(decoder_side, records[micro_index + 1], records[micro_index])
        chosen = section_forward(
            source_input["section_input"],
            source_input["carried"],
            source_input["positions"],
            params,
            source_input["moments"],
            pixel_count,
        )
        kept_records.append(chosen)
        plain_cot = task_cot[:, micro_index] * mask_weights[micro_index][:, :, None, None, None]
        through, unused_mixture, unused_slopes = heads_backward(
            chosen, plain_cot.astype(jnp.bfloat16), params, False
        )
        flattened = through.reshape(tasks_n, -1)
        partial_gram = jnp.dot(flattened, flattened.T, precision=lax.Precision.HIGHEST)
        gram_sum = gram_sum + jnp.where(decoder_side, partial_gram, 0.0)
    gram_sum = lax.psum(gram_sum, ("pipe", "dp", "rows"))
    nash_alpha = nash_solve(gram_sum)
    returning = jnp.zeros_like(incoming)
    start_grads = []
    trunk_sum, gain_sum, bias_sum = (0.0, 0.0, 0.0)
    down_sum, up_sum, task_sum = (0.0, 0.0, 0.0)
    for period in range(micro_count + 1):
        dec_index = max(micro_count - 1 - period, 0)
        enc_index = min(micro_count - period, micro_count - 1)
        active_flag = 1.0 if period < micro_count else 0.0
        chosen = choose_side(decoder_side, kept_records[dec_index], kept_records[enc_index])
        positions = chosen["positions"]
        weighted = (
            nash_alpha[:, None, None, None, None]
            * mask_weights[dec_index][:, :, None, None, None]
            * task_cot[:, dec_index].astype(jnp.float32)
            * active_flag
        )
        grad_feats = jnp.where(
            decoder_side, weighted, unpool_cells(returning[1:], positions)
        ).astype(jnp.bfloat16)
        through, grad_mixture, slopes = heads_backward(chosen, grad_feats, params, True)
        down_sum = down_sum + slopes[0]
        up_sum = up_sum + slopes[1]
        task_sum = task_sum + slopes[2]
        pooled_back = jnp.where(decoder_side, 0.0, unpool_cells(returning[0:1], positions))
        grad_shared = jnp.sum(through, axis=0, keepdims=True) + pooled_back
        grad_start, conv_grads, gain_grads, bias_grads = trunk_backward(
            chosen, grad_shared, params, pixel_count
        )
        start_grads.append(grad_start[0])
        trunk_sum = trunk_sum + conv_grads
        gain_sum = gain_sum + gain_grads
        bias_sum = bias_sum + bias_grads
        if period < micro_count:
            outgoing = jnp.concatenate(
                [pool_cells(grad_start, positions), pool_cells(grad_mixture, positions)], axis=0
            )
            returning = from_behind(outgoing.astype(jnp.bfloat16), "pipe", -1)
    features_out = jnp.stack(
        [
            jnp.where(
                decoder_side, records[micro_index + 1]["features"], records[micro_index]["features"]
            )
            for micro_index in range(micro_count)
        ],
        axis=1,
    ).astype(jnp.bfloat16)
    grads_out = jnp.stack(
        [
            jnp.where(
                decoder_side,
                start_grads[micro_count - 1 - micro_index],
                start_grads[micro_count - micro_index],
            )
            for micro_index in range(micro_count)
        ],
        axis=0,
    )
    shares = (
        lax.psum_scatter(trunk_sum[None], ("dp", "rows"), scatter_dimension=2, tiled=True),
        lax.psum_scatter(gain_sum[None], ("dp", "rows"), scatter_dimension=2, tiled=True),
        lax.psum_scatter(bias_sum[None], ("dp", "rows"), scatter_dimension=2, tiled=True),
        lax.psum_scatter(down_sum[None], ("dp", "rows"), scatter_dimension=2, tiled=True),
        lax.psum_scatter(up_sum[None], ("dp", "rows"), scatter_dimension=3, tiled=True),
        lax.psum_scatter(task_sum[None], ("dp", "rows"), scatter_dimension=2, tiled=True),
    )
    return (
        features_out[None],
        grads_out[None],
        shares[0],
        shares[1],
        shares[2],
        shares[3],
        shares[4],
        shares[5],
        nash_alpha,
    )


BF = jnp.bfloat16
F32 = jnp.float32
LANES = 128
TAPS = 9
VMEM_BYTES = 56 * 1024 * 1024


class Line:
    def __init__(self, ids):
        self.ids = ids
        self.last = None


def on_section(body, only):
    if only is None:
        return body

    def gated(ids_ref, *refs):
        @pl.when(ids_ref[2] == only)
        def _():
            body(ids_ref, *refs)

    return gated


def unread(body, count, first):
    def whole(*refs):
        body(*refs[:first], *refs[first + count :])

    return whole


LIGHT = pl.CostEstimate(flops=300_000_000, bytes_accessed=1, transcendentals=0)


def kernel_call(body, outs, line, vmem, name, scratch=(), only=None, smem=(), after=()):
    extra = list(after) + ([] if line.last is None else [line.last])
    first = 1 + len(smem) + len(vmem)
    results = pl.pallas_call(
        unread(on_section(body, only), len(extra), first),
        out_shape=[jax.ShapeDtypeStruct(shape, dtype) for shape, dtype in outs],
        in_specs=[pl.BlockSpec(memory_space=pltpu.SMEM)] * (1 + len(smem))
        + [pl.BlockSpec(memory_space=pltpu.VMEM)] * len(vmem)
        + [pl.BlockSpec(memory_space=pl.ANY)] * len(extra),
        out_specs=[pl.BlockSpec(memory_space=pltpu.VMEM)] * len(outs),
        scratch_shapes=list(scratch),
        compiler_params=pltpu.CompilerParams(vmem_limit_bytes=VMEM_BYTES),
        cost_estimate=LIGHT,
        name=name,
    )(line.ids, *smem, *vmem, *extra)
    line.last = results[-1]
    return results


def stepped_call(body, outs, line, vmem, name, scratch=(), only=None, fixed=()):
    extra = [] if line.last is None else [line.last]
    steps = outs[0][0][0]

    def block(shape):
        rest = len(shape) - 1
        return pl.BlockSpec(
            (1,) + tuple(shape[1:]),
            lambda t, ids: (t if only is None else jnp.where(ids[2] == only, t, 0),) + (0,) * rest,
        )

    def same(shape):
        return pl.BlockSpec(shape, lambda t, ids: (0,) * len(shape))

    results = pl.pallas_call(
        unread(on_section(body, only), len(extra), 1 + len(vmem)),
        grid_spec=pltpu.PrefetchScalarGridSpec(
            num_scalar_prefetch=1,
            grid=(steps,),
            in_specs=[same(a.shape) if k in fixed else block(a.shape) for k, a in enumerate(vmem)]
            + [pl.BlockSpec(memory_space=pl.ANY)] * len(extra),
            out_specs=[block(shape) for shape, _ in outs],
            scratch_shapes=list(scratch),
        ),
        out_shape=[jax.ShapeDtypeStruct(shape, dtype) for shape, dtype in outs],
        compiler_params=pltpu.CompilerParams(vmem_limit_bytes=VMEM_BYTES),
        cost_estimate=LIGHT,
        name=name,
    )(line.ids, *vmem, *extra)
    line.last = results[-1]
    return results


class Parts:
    def __init__(self, given, held, given_sems, results, kept, result_sems, split_in, split_out):
        self.given = [self.copies(a, b, given_sems, k, k in split_in) for k, (a, b) in enumerate(zip(given, held))]
        self.results = [
            self.copies(b, a, result_sems, k, k in split_out) for k, (a, b) in enumerate(zip(results, kept))
        ]
        self.waiting = []

    def copies(self, source, target, sems, k, split):
        if not split:
            return [pltpu.make_async_copy(source, target, sems.at[k, 0])]
        return [
            pltpu.make_async_copy(source.at[p], target.at[p], sems.at[k, p])
            for p in range(source.shape[0])
        ]

    def begin(self):
        for p in range(3):
            for copies in self.given:
                if p < len(copies):
                    copies[p].start()

    def need(self, k, p=0):
        self.given[k][p].wait()

    def send(self, k, p=0):
        self.results[k][p].start()
        self.waiting.append(self.results[k][p])

    def finish(self):
        for copy in self.waiting:
            copy.wait()


def section_call(
    body, outs, line, vmem, name, scratch=(), only=None, other=None, paired=(), split_in=(), split_out=(), smem=()
):
    other, paired = dict(other or {}), dict(paired)
    n_in, n_out = len(vmem), len(outs)
    passed, swapped = list(other.values()), list(paired.values())
    extra = [] if line.last is None else [line.last]

    def whole(*refs):
        scalars, refs = refs[: 1 + len(smem)], refs[1 + len(smem) :]
        ids_ref = scalars[0]
        given, refs = refs[:n_in], refs[n_in:]
        passed_refs, refs = refs[: len(passed)], refs[len(passed) :]
        swapped_refs, refs = refs[: len(swapped)], refs[len(swapped) + len(extra) :]
        results, refs = refs[:n_out], refs[n_out:]
        held, refs = refs[:n_in], refs[n_in:]
        kept, refs = refs[:n_out], refs[n_out:]
        given_sems, result_sems, refs = refs[0], refs[1], refs[2:]

        def run(sources):
            parts = Parts(sources, held, given_sems, results, kept, result_sems, split_in, split_out)
            parts.begin()
            for k in range(n_in):
                if k not in split_in:
                    parts.need(k)
            if split_in or split_out:
                body(*scalars, *held, *kept, *refs, parts=parts)
            else:
                body(*scalars, *held, *kept, *refs)
            for k in range(n_out):
                if k not in split_out:
                    parts.send(k)
            parts.finish()

        def hand_out():
            for source, target in ((passed_refs, kept), (kept, results)):
                copies = []
                for at, k in enumerate(other):
                    first = source[at] if source is passed_refs else source[k]
                    copies.append(pltpu.make_async_copy(first, target[k], result_sems.at[k, 0]))
                for copy in copies:
                    copy.start()
                for copy in copies:
                    copy.wait()

        if only is not None:
            pl.when(ids_ref[2] == only)(lambda: run(given))
            if passed:
                pl.when(ids_ref[2] != only)(hand_out)
        elif paired:
            mixed = list(given)
            for k, ref in zip(paired, swapped_refs):
                mixed[k] = ref
            pl.when(ids_ref[2] == 0)(lambda: run(given))
            pl.when(ids_ref[2] == 1)(lambda: run(mixed))
        else:
            run(given)

    results = pl.pallas_call(
        whole,
        out_shape=[jax.ShapeDtypeStruct(shape, dtype) for shape, dtype in outs],
        in_specs=[pl.BlockSpec(memory_space=pltpu.SMEM)] * (1 + len(smem))
        + [pl.BlockSpec(memory_space=pl.ANY)] * (n_in + len(passed) + len(swapped) + len(extra)),
        out_specs=[pl.BlockSpec(memory_space=pl.ANY)] * n_out,
        scratch_shapes=[pltpu.VMEM(a.shape, a.dtype) for a in vmem]
        + [pltpu.VMEM(shape, dtype) for shape, dtype in outs]
        + [pltpu.SemaphoreType.DMA((n_in, 3)), pltpu.SemaphoreType.DMA((n_out, 3))]
        + list(scratch),
        compiler_params=pltpu.CompilerParams(vmem_limit_bytes=VMEM_BYTES),
        cost_estimate=LIGHT,
        name=name,
    )(line.ids, *smem, *vmem, *passed, *swapped, *extra)
    line.last = results[-1]
    return results


def anchor(line, arrays, name):
    def body(*refs):
        refs[-1][...] = jnp.zeros((8, LANES), F32)

    line.last = pl.pallas_call(
        body,
        out_shape=jax.ShapeDtypeStruct((8, LANES), F32),
        in_specs=[pl.BlockSpec(memory_space=pl.ANY)] * (len(arrays) + 1),
        out_specs=pl.BlockSpec(memory_space=pltpu.VMEM),
        cost_estimate=LIGHT,
        name=name,
    )(*arrays, line.last)


def trade(pieces, axis, sections):
    count = lax.axis_size(axis)
    taken = [pieces[0]]
    for j in range(1, count):
        pairs = [(p * count + i, p * count + (i ^ j)) for p in sections for i in range(count)]
        taken.append(lax.ppermute(pieces[j], ("pipe", axis), pairs))
    return taken


def swap_sections(pieces):
    count = lax.axis_size("dp")
    return [
        lax.ppermute(
            pieces[j],
            ("pipe", "dp"),
            [(p * count + i, (1 - p) * count + (i ^ j)) for p in range(2) for i in range(count)],
        )
        for j in range(len(pieces))
    ]


def span(index, size):
    return pl.ds(pl.multiple_of(index * size, size), size)


def dot(a, b):
    return jnp.dot(a, b, preferred_element_type=F32)


def dot_nt(a, b):
    return lax.dot_general(a, b, (((1,), (1,)), ((), ())), preferred_element_type=F32)


def dot_tn(a, b):
    return lax.dot_general(a, b, (((0,), (0,)), ((), ())), preferred_element_type=F32)


def column_of(shape, cols):
    return lax.broadcasted_iota(jnp.int32, shape, 0) % cols


def fold_taps(taps, cols):
    size = taps.shape[0]
    blank = jnp.zeros((cols, LANES), F32)
    sums = []
    for b in range(3):
        first = taps[:, b * LANES : (b + 1) * LANES]
        second = taps[:, (3 + b) * LANES : (4 + b) * LANES]
        third = taps[:, (6 + b) * LANES : (7 + b) * LANES]
        sums.append(
            second
            + jnp.concatenate([blank, first[: size - cols]], axis=0)
            + jnp.concatenate([third[cols:], blank], axis=0)
        )
    column = column_of((size, LANES), cols)
    left = jnp.where(column == 0, 0.0, pltpu.roll(sums[0], 1, 0))
    right = jnp.where(column == cols - 1, 0.0, pltpu.roll(sums[2], size - 1, 0))
    return sums[1] + left + right


def spread_taps(grad, cols):
    size = grad.shape[0]
    column = column_of((size, LANES), cols)
    moved = [
        jnp.where(column == cols - 1, 0.0, pltpu.roll(grad, size - 1, 0)).astype(BF),
        grad.astype(BF),
        jnp.where(column == 0, 0.0, pltpu.roll(grad, 1, 0)).astype(BF),
    ]
    blank = jnp.zeros((cols, LANES), BF)
    above = [jnp.concatenate([m[cols:], blank], axis=0) for m in moved]
    below = [jnp.concatenate([blank, m[: size - cols]], axis=0) for m in moved]
    return jnp.concatenate(above + moved + below, axis=1)


def cut_weights(line, arrays, name):
    depth = arrays[0][0].shape[1]
    count = sum(len(layers) for _, layers in arrays)

    def body(ids_ref, *refs):
        given, outs = refs[: len(arrays)], refs[len(arrays) :]
        for j in range(4):
            cut = span(ids_ref[0] ^ j, LANES)
            row = 0
            for ref, (_, layers) in zip(given, arrays):
                for n in layers:
                    outs[j][row * depth : (row + 1) * depth, :] = ref[n, :, cut]
                    row += 1

    return kernel_call(
        body, [((count * depth, LANES), BF)] * 4, line, [a for a, _ in arrays], name
    )


def stack_weights(line, pieces, groups, extra, name):
    depth = pieces[0].shape[0] // sum(len(group) for group in groups)
    more = [a for arrays in extra for a in arrays]

    def body(ids_ref, *refs):
        given, more_in, outs = refs[:4], list(refs[4 : 4 + len(more)]), refs[4 + len(more) :]
        for k, group in enumerate(groups):
            for at, n in enumerate(group):
                for j in range(4):
                    rows = span(4 * at + (ids_ref[0] ^ j), depth)
                    outs[k][rows, :] = given[j][n * depth : (n + 1) * depth, :]
            at = 4 * len(group) * depth
            for array in extra[k]:
                outs[k][at : at + array.shape[0], :] = more_in.pop(0)[...]
                at += array.shape[0]

    sizes = [
        4 * len(group) * depth + sum(a.shape[0] for a in extra[k])
        for k, group in enumerate(groups)
    ]
    return kernel_call(
        body, [((n, LANES), BF) for n in sizes], line, list(pieces) + more, name
    )


def place_weights(line, gathered, count, depth, name, norm_rows=0, tail_rows=0):
    whole = 16 * depth
    channels = whole // TAPS
    end = 4 * count * depth
    apart = norm_rows > 0

    def body(ids_ref, g_ref, *rest):
        flat = rest[-1]
        for n in range(count):
            for r in range(4):
                for p in range(4):
                    rows = slice((4 * n + p) * depth, (4 * n + p + 1) * depth)
                    flat[(p * 4 + r) * depth : (p * 4 + r + 1) * depth, :] = g_ref[r, rows, :]
            for tap in range(TAPS):
                lanes = slice(tap * LANES, (tap + 1) * LANES)
                value = flat[tap * channels : (tap + 1) * channels, :]
                if apart:
                    rest[n][0, :, lanes] = value
                else:
                    rest[0][n, :, lanes] = value
        if apart:
            own = [g_ref[r, end : end + norm_rows, :].astype(F32) for r in range(4)]
            rest[count][...] = (own[0] + own[1]) + (own[2] + own[3])
            rest[count + 1][...] = g_ref[:, end + norm_rows : end + norm_rows + tail_rows, :]

    if apart:
        outs = [((1, channels, TAPS * LANES), BF)] * count
        outs += [((norm_rows, LANES), F32), ((4, tail_rows, LANES), BF)]
    else:
        outs = [((count, channels, TAPS * LANES), BF)]
    return kernel_call(
        body, outs, line, [gathered], name, scratch=[pltpu.VMEM((whole, LANES), BF)]
    )


def place_attention(line, pieces, maps, part):
    def body(ids_ref, *refs):
        given, out = refs[:4], refs[4]
        for j in range(4):
            for r in range(4):
                chunk = (ids_ref[0] ^ j) * 4 + r
                for t in range(maps):
                    out[t, span(chunk, part), :] = given[j][r, t * part : (t + 1) * part, :]

    return kernel_call(
        body, [((maps, 16 * part, LANES), BF)], line, list(pieces), "place_attention"
    )[0]


def trunk_layer(
    line, pieces, weight, norms, layer, cols, eps_value, form, last, masked, name, only=None
):
    channels = weight.shape[1]
    size = {"images": 1, "slices": 0.25, "cells": 1}[form]
    size = int(pieces[0].shape[0] * size)
    pixels = 4 * size
    whole_images = form == "images"

    def body(ids_ref, *refs):
        given, (w_ref, norm_ref) = refs[:4], refs[4:6]
        at = 6
        if masked is not None and not whole_images:
            mask_ref = refs[6]
            at = 7
        outs, v_ref, pairs_ref = refs[at:-2], refs[-2], refs[-1]
        field = outs[0]
        for j in range(4):
            peer = ids_ref[0] ^ j
            if whole_images:
                field[span(peer, size), :] = given[j][:, :channels]
                outs[4][span(peer, size), :] = given[j][:, channels:]
            elif form == "cells":
                cells = spread_pairs(given[j][...].astype(F32), pairs_ref, cols)
                field[:, span(peer, LANES)] = cells.astype(BF) * mask_ref[...]
            else:
                field[:, span(peer, LANES)] = given[j][...]
        for i in range(4):
            part = slice(i * size, (i + 1) * size)
            v_ref[part, :] = fold_taps(dot(field[part, :], w_ref[0]), cols)
        conv_out = v_ref[...]
        center = jnp.sum(conv_out, axis=0, keepdims=True) / pixels
        moved = conv_out - center
        spread = jnp.sum(moved * moved, axis=0, keepdims=True) / pixels
        inverse = lax.rsqrt(spread + eps_value)
        normed = moved * inverse
        outs[1][...] = normed
        outs[2][...] = jnp.broadcast_to(inverse, (8, LANES))
        preact = norm_ref[layer : layer + 1, :] * normed + norm_ref[2 + layer : 3 + layer, :]
        hidden = (preact * jax.nn.sigmoid(preact)).astype(BF)
        outs[3][...] = hidden
        if last and masked is not None:
            kept = hidden.astype(F32) * mask_ref[...].astype(F32)
            outs[4][...] = pool_pairs(kept, pairs_ref, cols).astype(BF)

    outs = [((pixels, channels), BF), ((pixels, LANES), F32), ((8, LANES), F32)]
    outs.append(((pixels, LANES), BF))
    if last and masked is not None:
        outs.append(((size, LANES), BF))
    elif whole_images:
        outs.append(((pixels, LANES), BF))
    extra = [masked] if masked is not None and not whole_images else []
    return kernel_call(
        body,
        outs,
        line,
        list(pieces) + [weight, norms] + extra,
        name,
        scratch=[pltpu.VMEM((pixels, LANES), F32), pltpu.VMEM((pixels // 2, LANES), F32)],
        only=only,
    )


def pool_pairs(value, pairs_ref, cols):
    size = value.shape[0]
    halves = value.reshape(size // (2 * cols), 2, cols, LANES)
    pairs_ref[: size // 2, :] = (halves[:, 0] + halves[:, 1]).reshape(size // 2, LANES)
    return pairs_ref[pl.ds(0, size // 4, stride=2), :] + pairs_ref[pl.ds(1, size // 4, stride=2), :]


def spread_pairs(small, pairs_ref, cols):
    size = 4 * small.shape[0]
    pairs_ref[pl.ds(0, size // 4, stride=2), :] = small
    pairs_ref[pl.ds(1, size // 4, stride=2), :] = small
    rows = pairs_ref[: size // 2, :].reshape(size // (2 * cols), 1, cols, LANES)
    return jnp.broadcast_to(rows, (size // (2 * cols), 2, cols, LANES)).reshape(size, LANES)


def attend(x, mixture, down, up_t):
    inner = dot(mixture, down)
    active = (inner * jax.nn.sigmoid(inner)).astype(BF)
    gate = jax.nn.sigmoid(dot_nt(active, up_t))
    return inner, active, gate


def label_at(label_ref, ids_ref, device, t):
    return label_ref[(device * 4 + ids_ref[1]) * 3 + t]


def slot_of(label_ref, ids_ref, device, t):
    return sum([label_at(label_ref, ids_ref, device, k) for k in range(t)], jnp.int32(0))


def section_tasks(line, labels, x_slices, att, weights, mask, cots, cols):
    pixels = x_slices[0].shape[0]
    size = pixels // 4
    tasks_n, channels, _ = weights.shape
    down, up_t = att[:tasks_n], att[tasks_n:]

    def body(ids_ref, label_ref, *refs):
        x_in, down_ref, up_ref, w_ref, mask_ref, cot_in = refs[:4], *refs[4:8], refs[8:12]
        fields, feats, cells, du = refs[12:16], refs[16:20], refs[20], refs[21:25]
        x_ref, pairs_ref = refs[25:]
        t = pl.program_id(0)

        @pl.when(ids_ref[2] == 0)
        def _():
            @pl.when(t == 0)
            def _():
                for j in range(4):
                    x_ref[:, span(ids_ref[0] ^ j, LANES)] = x_in[j][...]

            for j in range(4):
                rows = span(ids_ref[0] ^ j, size)
                x = x_ref[rows, :]
                _, _, gate = attend(x, x, down_ref[0], up_ref[0])
                u = (gate * x.astype(F32)).astype(BF)
                fields[j][0] = u
                value = fold_taps(dot(u, w_ref[0]), cols)
                feats[j][0] = value.astype(BF)
                kept = value * mask_ref[rows, :].astype(F32)
                cells[0, span(ids_ref[0] ^ j, size // 4), :] = pool_pairs(
                    kept, pairs_ref, cols
                ).astype(BF)

        @pl.when(ids_ref[2] == 1)
        def _():
            for j in range(4):
                device = ids_ref[0] ^ j
                before = jnp.where(t > 0, label_at(label_ref, ids_ref, device, 0), 0)
                before += jnp.where(t > 1, label_at(label_ref, ids_ref, device, 1), 0)

                @pl.when(t == 0)
                def _(j=j):
                    du[j][...] = jnp.zeros_like(du[j])

                @pl.when(label_at(label_ref, ids_ref, device, t) == 1)
                def _(j=j, before=before):
                    taps = spread_taps(cot_in[j][0].astype(F32), cols)
                    du[j][before] = dot_nt(taps, w_ref[0]).astype(BF)

    def step(shape, only=None):
        return pl.BlockSpec(
            (1,) + shape[1:],
            lambda t, ids, _: (t if only is None else jnp.where(ids[2] == only, t, 0),)
            + (0,) * (len(shape) - 1),
        )

    def same(shape):
        return pl.BlockSpec(shape, lambda t, ids, _: (0,) * len(shape))

    outs = [(tasks_n, size, channels)] * 4 + [(tasks_n, size, LANES)] * 5 + [(2, size, channels)] * 4
    args = list(x_slices) + [down, up_t, weights, mask] + list(cots)
    results = pl.pallas_call(
        unread(body, 1, 2 + len(args)),
        grid_spec=pltpu.PrefetchScalarGridSpec(
            num_scalar_prefetch=2,
            grid=(tasks_n,),
            in_specs=[same(a.shape) for a in x_slices]
            + [step(down.shape, 0), step(up_t.shape, 0), step(weights.shape), same(mask.shape)]
            + [step(a.shape, 1) for a in cots]
            + [pl.BlockSpec(memory_space=pl.ANY)],
            out_specs=[step(shape, 0) for shape in outs[:9]] + [same(shape) for shape in outs[9:]],
            scratch_shapes=[pltpu.VMEM((pixels, channels), BF), pltpu.VMEM((size // 2, LANES), F32)],
        ),
        out_shape=[jax.ShapeDtypeStruct(shape, BF) for shape in outs],
        compiler_params=pltpu.CompilerParams(vmem_limit_bytes=VMEM_BYTES),
        cost_estimate=LIGHT,
        name="section_tasks",
    )(line.ids, labels, *args, line.last)
    line.last = results[-1]
    return results[:4], results[4:8], results[8], results[9:]


def grads_of_taps(field, grad_at, taps_ref, flat, out_at, cols, depth):
    size = taps_ref.shape[0] // 4
    for i in range(4 if grad_at is not None else 0):
        taps_ref[i * size : (i + 1) * size, :] = spread_taps(grad_at(i).astype(F32), cols)
    channels = field.shape[1]
    for row in range(3):
        whole = dot_tn(field, taps_ref[:, row * 3 * LANES : (row + 1) * 3 * LANES])
        for b in range(3):
            tap = 3 * row + b
            flat[tap * channels : (tap + 1) * channels, :] = whole[
                :, b * LANES : (b + 1) * LANES
            ].astype(BF)
    for r in range(4):
        out = out_at(r)
        for p in range(4):
            chunk = p * 4 + r
            out[p] = flat[chunk * depth : (chunk + 1) * depth, :]


def trunk_grads(line, enc_pairs, dec_pairs, depth, cols, name):
    count = len(enc_pairs)
    pixels, channels = enc_pairs[0][0].shape
    size = pixels // 4
    enc_in = [a for pair in enc_pairs for a in pair]
    dec_in = [a for pair in dec_pairs for a in pair]

    def body(ids_ref, *refs):
        given, out, taps_ref, flat = refs[: 2 * count], *refs[2 * count :]
        for n in range(count):
            h_ref, g_ref = given[2 * n], given[2 * n + 1]
            grads_of_taps(
                h_ref[...],
                lambda i: g_ref[i * size : (i + 1) * size, :],
                taps_ref,
                flat,
                lambda r: out.at[r, n],
                cols,
                depth,
            )

    return section_call(
        body,
        [((4, count, 4, depth, LANES), BF)],
        line,
        enc_in,
        name,
        scratch=[
            pltpu.VMEM((pixels, TAPS * LANES), BF),
            pltpu.VMEM((TAPS * channels, LANES), BF),
        ],
        paired=enumerate(dec_in),
    )[0]


def dec_task_grads(line, dec_xs, q_cells, mask, att, cots, depth, cols):
    tasks_n, size, _ = q_cells[0].shape
    pixels, channels = 4 * size, att.shape[1]

    def body(ids_ref, *refs, parts):
        x_in, q_in, mask_ref, att_ref, cot_in = refs[:4], refs[4:8], refs[8], refs[9], refs[10:14]
        u_ref, out, taps_ref, flat, x_ref, s_ref, pairs_ref = refs[14:]
        for j in range(4):
            x_ref[:, span(ids_ref[0] ^ j, LANES)] = x_in[j][...]
        for t in range(tasks_n):
            for i in range(4):
                image = ids_ref[0] ^ i
                rows = span(image, size)
                x_low = x_ref[rows, :]
                x = x_low.astype(F32)
                own = mask_ref[rows, :]
                for j in range(4):
                    kept = q_in[j][t, span(image, size // 4), :].astype(F32)
                    cells = spread_pairs(kept, pairs_ref, cols)
                    s_ref[:, span(ids_ref[0] ^ j, LANES)] = cells.astype(BF) * own
                mixture = (x + s_ref[...].astype(F32)).astype(BF)
                _, _, gate = attend(x_low, mixture, att_ref[t], att_ref[tasks_n + t])
                u_ref[t, i * size : (i + 1) * size, :] = (gate * x).astype(BF)
            parts.send(0, t)
            grads_of_taps(
                u_ref[t],
                lambda i: cot_in[i][t],
                taps_ref,
                flat,
                lambda r: out.at[r, t],
                cols,
                depth,
            )

    return section_call(
        body,
        [((tasks_n, pixels, channels), BF), ((4, tasks_n, 4, depth, LANES), BF)],
        line,
        list(dec_xs) + list(q_cells) + [mask, att] + list(cots),
        "dec_task_grads",
        scratch=[
            pltpu.VMEM((pixels, TAPS * LANES), BF),
            pltpu.VMEM((TAPS * channels, LANES), BF),
            pltpu.VMEM((pixels, channels), BF),
            pltpu.VMEM((size, channels), BF),
            pltpu.VMEM((size // 2, LANES), F32),
        ],
        only=1,
        split_out=(0,),
    )


def enc_tasks_reverse(line, labels, grad_pieces, fields, weights, mask, dec_grads, depth, cols):
    tasks_n, given_size, _ = grad_pieces[0].shape
    channels = weights.shape[1]
    size = 4 * given_size
    pixels = 4 * size

    def body(ids_ref, label_ref, *refs, parts):
        given, u_in, w_ref, mask_ref, outs = refs[:4], refs[4:8], refs[8], refs[9], refs[10:14]
        grads, pairs_ref, taps_ref, flat, whole = refs[14:]
        for j in range(4):
            outs[j][1] = jnp.zeros((size, channels), BF)
        for t in range(tasks_n):
            parts.need(8, t)
            for j in range(4):
                rows = slice(j * size, (j + 1) * size)
                cells = spread_pairs(given[j][t].astype(F32), pairs_ref, cols)
                grad = cells.astype(BF) * mask_ref[span(ids_ref[0] ^ j, size), :]
                taps_ref[rows, :] = spread_taps(grad.astype(F32), cols)
                device = ids_ref[0] ^ j

                @pl.when(label_at(label_ref, ids_ref, device, t) == 1)
                def _(t=t, j=j, rows=rows, device=device):
                    slot = slot_of(label_ref, ids_ref, device, t)
                    outs[j][slot] = dot_nt(taps_ref[rows, :], w_ref[t]).astype(BF)

                parts.need(4 + j, t)
                whole[rows, :] = u_in[j][t]
            grads_of_taps(whole[...], None, taps_ref, flat, lambda r: grads.at[r, t], cols, depth)

    return section_call(
        body,
        [((2, size, channels), BF)] * 4 + [((4, tasks_n, 4, depth, LANES), BF)],
        line,
        list(grad_pieces) + list(fields) + [weights, mask],
        "enc_tasks_back",
        scratch=[
            pltpu.VMEM((size // 2, LANES), F32),
            pltpu.VMEM((pixels, TAPS * LANES), BF),
            pltpu.VMEM((TAPS * channels, LANES), BF),
            pltpu.VMEM((pixels, channels), BF),
        ],
        only=0,
        other={4: dec_grads},
        split_in=range(4, 9),
        smem=[labels],
    )


def dec_task_layer(line, fields, weights, enc_feats, cols, name):
    tasks_n, channels, _ = weights.shape
    size = fields.shape[1] // 4

    def body(ids_ref, u_ref, w_ref, *outs, parts):
        for t in range(tasks_n):
            parts.need(1, t)
            parts.need(0, t)
            for j in range(4):
                value = dot(u_ref[t, j * size : (j + 1) * size, :], w_ref[t])
                outs[j][t] = fold_taps(value, cols).astype(BF)

    return section_call(
        body,
        [((tasks_n, size, LANES), BF)] * 4,
        line,
        [fields, weights],
        name,
        only=1,
        other=enumerate(enc_feats),
        split_in=(0, 1),
    )


def heads_reverse(line, labels, x_pieces, carried, mask, du_pieces, att, cols, name, only, other=None):
    size = x_pieces[0].shape[0] // 4
    channels = att.shape[1]
    tasks_n = att.shape[0] // 2
    carry = carried is not None

    def body(ids_ref, label_ref, *refs):
        x_in, rest = refs[:4], refs[4:]
        if carry:
            q_in, mask_ref, rest = rest[:4], rest[4], rest[5:]
        du_in, att_ref, rest = rest[:4], rest[4], rest[5:]
        outs, (x_ref, s_ref, ds_ref, da_ref, pairs_ref) = rest[:-5], rest[-5:]
        dx_ref, g_ref, grads = outs[0], outs[1], outs[2:6]
        for j in range(4):
            x_ref[:, span(ids_ref[0] ^ j, LANES)] = x_in[j][span(ids_ref[0], size), :]

        def task(t):
            x_low = x_ref[...]
            x = x_low.astype(F32)
            slot = slot_of(label_ref, ids_ref, ids_ref[0], t)
            if carry:
                own = mask_ref[span(ids_ref[0], size), :]
                for j in range(4):
                    kept = q_in[j][t, span(ids_ref[0], size // 4), :].astype(F32)
                    cells = spread_pairs(kept, pairs_ref, cols)
                    s_ref[:, span(ids_ref[0] ^ j, LANES)] = cells.astype(BF) * own
                mixture = (x + s_ref[...].astype(F32)).astype(BF)
            else:
                mixture = x_low
            inner, active, gate = attend(x, mixture, att_ref[t], att_ref[tasks_n + t])
            du = (
                (du_in[0][slot].astype(F32) + du_in[1][slot].astype(F32))
                + (du_in[2][slot].astype(F32) + du_in[3][slot].astype(F32))
            )
            gated = du * gate
            do = (gated * x * (1.0 - gate)).astype(BF)
            sig = jax.nn.sigmoid(inner)
            dk = (dot(do, att_ref[tasks_n + t]) * (sig * (1.0 + inner * (1.0 - sig)))).astype(BF)
            ds = dot_nt(dk, att_ref[t])
            dx_ref[t] = gated + ds
            if carry:
                ds_ref[...] = ds
                for j in range(4):
                    kept = ds_ref[:, span(ids_ref[0] ^ j, LANES)] * own.astype(F32)
                    outs[6 + j][t] = pool_pairs(kept, pairs_ref, cols).astype(BF)
            for row, value in ((t, dot_tn(mixture, dk)), (tasks_n + t, dot_tn(do, active))):
                da_ref[...] = value
                for j in range(4):
                    grads[j][row] = da_ref[span(ids_ref[0] ^ j, LANES), :].astype(BF)

        def no_task(t):
            dx_ref[t] = jnp.zeros((size, channels), F32)
            for j in range(4):
                if carry:
                    outs[6 + j][t] = jnp.zeros((size // 4, LANES), BF)
                grads[j][t] = jnp.zeros((LANES, LANES), BF)
                grads[j][tasks_n + t] = jnp.zeros((LANES, LANES), BF)

        for t in range(tasks_n):
            label = label_at(label_ref, ids_ref, ids_ref[0], t)
            pl.when(label == 1)(functools.partial(task, t))
            pl.when(label != 1)(functools.partial(no_task, t))
        row = 0
        g_ref[...] = jnp.zeros_like(g_ref)
        for a in range(tasks_n):
            for b in range(a, tasks_n):
                line_sum = jnp.sum(dx_ref[a] * dx_ref[b], axis=0, keepdims=True)
                folded = line_sum[:, :LANES]
                for part in range(1, channels // LANES):
                    folded = folded + line_sum[:, part * LANES : (part + 1) * LANES]
                g_ref[row : row + 1, :] = folded
                row += 1

    outs = [((tasks_n, size, channels), F32), ((8, LANES), F32)]
    outs += [((2 * tasks_n, LANES, LANES), BF)] * 4
    if carry:
        outs += [((tasks_n, size // 4, LANES), BF)] * 4
    return section_call(
        body,
        outs,
        line,
        list(x_pieces) + (list(carried) + [mask] if carry else []) + list(du_pieces) + [att],
        name,
        scratch=[
            pltpu.VMEM((size, channels), BF),
            pltpu.VMEM((size, channels), BF),
            pltpu.VMEM((size, channels), F32),
            pltpu.VMEM((channels, LANES), F32),
            pltpu.VMEM((size // 2, LANES), F32),
        ],
        only=only,
        other=other,
        smem=[labels],
    )


def nash_values(lines, tasks_n):
    def full(row):
        return jnp.broadcast_to(jnp.sum(lines[row : row + 1, :], axis=1, keepdims=True), (8, LANES))

    gram = [[None] * tasks_n for _ in range(tasks_n)]
    row = 0
    for a in range(tasks_n):
        for b in range(a, tasks_n):
            gram[a][b] = gram[b][a] = full(row)
            row += 1
    trace_mean = (gram[0][0] + gram[1][1] + gram[2][2]) / 3.0 + 1e-06
    norm = [[gram[a][b] / trace_mean for b in range(3)] for a in range(3)]
    alpha = [lax.rsqrt(norm[a][a] + 1e-06) for a in range(3)]
    for _ in range(NASH_ITERS):
        right = [
            norm[a][0] * alpha[0] + norm[a][1] * alpha[1] + norm[a][2] * alpha[2] - 1.0 / alpha[a]
            for a in range(3)
        ]
        matrix = [
            [norm[a][b] + 1.0 / (alpha[a] * alpha[a]) if a == b else norm[a][b] for b in range(3)]
            for a in range(3)
        ]
        cof = [[None] * 3 for _ in range(3)]
        for a in range(3):
            for b in range(3):
                a1, a2, b1, b2 = (a + 1) % 3, (a + 2) % 3, (b + 1) % 3, (b + 2) % 3
                cof[a][b] = matrix[a1][b1] * matrix[a2][b2] - matrix[a1][b2] * matrix[a2][b1]
        determinant = (
            matrix[0][0] * cof[0][0] + matrix[0][1] * cof[0][1] + matrix[0][2] * cof[0][2]
        )
        update = [
            (cof[0][b] * right[0] + cof[1][b] * right[1] + cof[2][b] * right[2]) / determinant
            for b in range(3)
        ]
        alpha = [alpha[a] * jnp.exp(-0.5 * jnp.tanh(update[a] / alpha[a])) for a in range(3)]
    return alpha


def weigh(line, dx, w_or_lines, solve, name):
    tasks_n, size, channels = dx.shape

    def body(ids_ref, *refs):
        given, dx_ref, outs, total = refs[: len(w_or_lines)], refs[len(w_or_lines)], refs[-6:-1], refs[-1]
        if solve:
            lines = (given[0][0] + given[0][1]) + (given[0][2] + given[0][3])
            alpha = nash_values(lines, tasks_n)
            outs[0][...] = jnp.concatenate(
                [alpha[t][:1] for t in range(3)] + [jnp.zeros((5, LANES), F32)], axis=0
            )
        else:
            outs[0][...] = given[0][...]
        acc = None
        for t in range(tasks_n):
            scale = jnp.tile(outs[0][t : t + 1, :], (1, channels // LANES))
            term = dx_ref[t] * scale
            acc = term if acc is None else acc + term
        total[...] = acc
        for j in range(4):
            outs[1 + j][...] = total[:, span(ids_ref[0] ^ j, LANES)].astype(BF)

    return kernel_call(
        body,
        [((8, LANES), F32)] + [((size, LANES), BF)] * 4,
        line,
        list(w_or_lines) + [dx],
        name,
        scratch=[pltpu.VMEM((size, channels), F32)],
    )


def trunk_reverse(
    line, pieces, by_image, cells, mask, normed, inverse, norms, layer, weight, cols, parts, other, name, only
):
    pixels = normed.shape[0]
    size = pixels // 4
    channels = weight.shape[1]
    takes, gives = cells is not None, "cells" in parts
    shapes = {"slices": (pixels, LANES), "images": (size, channels), "cells": (size, LANES)}

    def body(ids_ref, *refs):
        given, rest = refs[:4], refs[4:]
        if takes:
            cells_in, rest = rest[:4], rest[4:]
        if takes or gives:
            mask_ref, rest = rest[0], rest[1:]
        (n_ref, inv_ref, norm_ref, w_ref), rest = rest[:4], rest[4:]
        if other is not None:
            other_in, rest = rest[:4], rest[4:]
        outs, (acc_ref, back_ref, pairs_ref) = rest[:-3], rest[-3:]
        gain = norm_ref[layer : layer + 1, :]

        @pl.when(ids_ref[2] == only)
        def _():
            if by_image:
                for j in range(4):
                    acc_ref[span(ids_ref[0] ^ j, size), :] = given[j][...].astype(F32)
            else:
                acc_ref[...] = (given[0][...].astype(F32) + given[1][...].astype(F32)) + (
                    given[2][...].astype(F32) + given[3][...].astype(F32)
                )
            grad = acc_ref[...]
            if takes:
                start = (cells_in[0][...].astype(F32) + cells_in[1][...].astype(F32)) + (
                    cells_in[2][...].astype(F32) + cells_in[3][...].astype(F32)
                )
                start = start.astype(BF).astype(F32)
                grad = grad + spread_pairs(start, pairs_ref, cols) * mask_ref[...].astype(F32)
            normed_value = n_ref[...]
            preact = gain * normed_value + norm_ref[2 + layer : 3 + layer, :]
            sig = jax.nn.sigmoid(preact)
            dp = grad * (sig * (1.0 + preact * (1.0 - sig)))
            bias_total = jnp.sum(dp, axis=0, keepdims=True)
            gain_total = jnp.sum(dp * normed_value, axis=0, keepdims=True)
            outs[1][...] = jnp.concatenate(
                [gain_total, bias_total, jnp.zeros((6, LANES), F32)], axis=0
            )
            scale = inv_ref[0:1, :] * gain
            dv = scale * (dp - bias_total / pixels - normed_value * (gain_total / pixels))
            outs[0][...] = dv.astype(BF)
            acc_ref[...] = dv.astype(BF).astype(F32)
            for i in range(4):
                part = slice(i * size, (i + 1) * size)
                back_ref[part, :] = dot_nt(spread_taps(acc_ref[part, :], cols), w_ref[0])
            for at, kind in enumerate(parts):
                for j in range(4):
                    peer = ids_ref[0] ^ j
                    out = outs[2 + 4 * at + j]
                    if kind == "images":
                        out[...] = back_ref[span(peer, size), :].astype(BF)
                    elif kind == "slices":
                        out[...] = back_ref[:, span(peer, LANES)].astype(BF)
                    else:
                        kept = back_ref[:, span(peer, LANES)] * mask_ref[...].astype(F32)
                        out[...] = pool_pairs(kept, pairs_ref, cols).astype(BF)

        if other is not None:

            @pl.when(ids_ref[2] != only)
            def _():
                for j in range(4):
                    outs[2 + 4 * parts.index("images") + j][...] = other_in[j][...]

    outs = [((pixels, LANES), BF), ((8, LANES), F32)]
    for kind in parts:
        outs += [(shapes[kind], BF)] * 4
    extra = list(cells) if takes else []
    if takes or gives:
        extra.append(mask)
    return kernel_call(
        body,
        outs,
        line,
        list(pieces) + extra + [normed, inverse, norms, weight] + list(other or []),
        name,
        scratch=[
            pltpu.VMEM((pixels, LANES), F32),
            pltpu.VMEM((pixels, channels), F32),
            pltpu.VMEM((pixels // 2, LANES), F32),
        ],
    )


def plane_device(
    x_in,
    pool_index,
    task_mask,
    task_cot,
    trunk_conv,
    norm_gain,
    norm_bias,
    att_down,
    attention_up_weights,
    task_conv,
):
    micro_count, _, rows_n, cols, channels = x_in.shape
    tasks_n = task_cot.shape[0]
    strip = rows_n * cols
    size = strip * micro_count
    depth = trunk_conv.shape[2]
    part = att_down.shape[2]
    section = lax.axis_index("pipe")
    decoder = section == 1
    row_at = lax.axis_index("rows")
    line = Line(jnp.stack([lax.axis_index("dp"), row_at, section]).astype(jnp.int32))
    ENC, DEC, BOTH = (0,), (1,), (0, 1)

    norm_own = jnp.concatenate([norm_gain[0], norm_bias[0]], axis=0)
    own_lanes = jnp.arange(LANES) // part == row_at
    norm_own = jnp.where(own_lanes[None], jnp.tile(norm_own, (1, LANES // part)), 0).astype(BF)
    norm_own = jnp.pad(norm_own, ((0, 12), (0, 0)))
    att_own = jnp.concatenate(
        [att_down[0], jnp.swapaxes(attention_up_weights[0], 1, 2)], axis=0
    ).reshape(2 * tasks_n * part, LANES)

    trunk_cut = trade(cut_weights(line, [(trunk_conv[0], [0, 1])], "cut_trunk"), "dp", BOTH)

    labels = lax.all_gather(task_mask, "dp").reshape(-1)

    picked = pool_index[:, 0, :, None, :, None]
    place = jnp.arange(2)[:, None, None] * 2 + jnp.arange(2)[None, None, :]
    cells = (picked == place[None, None]).astype(BF)
    cells = jnp.broadcast_to(cells.reshape(micro_count, strip, 1), (micro_count, strip, LANES))
    strips = x_in.reshape(micro_count, strip, channels)

    def cut_input(ids_ref, x_ref, m_ref, *outs):
        for j in range(4):
            outs[j][:, :channels] = x_ref[ids_ref[1] ^ j]
            outs[j][:, channels:] = m_ref[ids_ref[1] ^ j]

    strips = kernel_call(
        cut_input, [((strip, channels + LANES), BF)] * 4, line, [strips, cells], "cut_input"
    )
    strips = trade(strips, "rows", BOTH)

    trunk_block = stack_weights(line, trunk_cut, [[0, 1]], [[norm_own, att_own]], "stack_trunk")[0]
    trunk_all = lax.all_gather(trunk_block, "rows")

    def place_input(ids_ref, a, b, c, e, o_ref):
        for j, piece in enumerate((a, b, c, e)):
            o_ref[span(ids_ref[1] ^ j, strip), :] = piece[...]

    x_image = kernel_call(
        place_input, [((size, channels + LANES), BF)], line, strips, "place_input"
    )[0]
    x_images = trade([x_image] * 4, "dp", ENC)
    task_cut = trade(
        cut_weights(line, [(task_conv[0], range(tasks_n))], "cut_tasks"), "dp", BOTH
    )
    anchor(line, x_images, "input_there")
    task_block = stack_weights(line, task_cut, [list(range(tasks_n))], [[]], "stack_tasks")[0]
    task_all = lax.all_gather(task_block, "rows")

    half = channels // 2

    def cut_cot(ids_ref, mask_ref, c_ref, *outs):
        for j in range(4):
            micro = ids_ref[1] ^ j
            for t in range(tasks_n):
                labelled = mask_ref[micro * tasks_n + t].astype(F32)
                value = c_ref[t, micro, :, span(ids_ref[2], half)].astype(F32)
                outs[j][t] = (value * labelled).astype(BF)

    cot_strips = kernel_call(
        cut_cot,
        [((tasks_n, strip, half), BF)] * 4,
        line,
        [task_cot.reshape(tasks_n, micro_count, strip, channels)],
        "cut_cotangents",
        smem=[task_mask.reshape(-1)],
    )
    cot_strips = trade(cot_strips, "rows", BOTH)

    def place_cot(ids_ref, _, a, b, c, e, o_ref):
        for j, piece in enumerate((a, b, c, e)):
            for t in range(tasks_n):
                o_ref[t, span(ids_ref[1] ^ j, strip), :] = piece[t]

    cot_half = kernel_call(
        place_cot, [((tasks_n, size, half), BF)], line, cot_strips, "place_cotangents", smem=[labels]
    )[0]
    cot_other = swap_sections([cot_half])[0]

    def slice_cot(ids_ref, own_ref, other_ref, *rest):
        outs, image = rest[:4], rest[4]
        image[:, :, :half] = other_ref[...]
        image[:, :, half:] = own_ref[...]
        for j in range(4):
            outs[j][...] = image[:, :, span(ids_ref[0] ^ j, LANES)]

    cots = kernel_call(
        slice_cot,
        [((tasks_n, size, LANES), BF)] * 4,
        line,
        [cot_half, cot_other],
        "slice_cotangents",
        scratch=[pltpu.VMEM((tasks_n, size, channels), BF)],
    )
    cots = trade(cots, "dp", BOTH)
    first_w, second_w, norms, att_rows = place_weights(
        line, trunk_all, 2, depth, "place_trunk", norm_own.shape[0], att_own.shape[0]
    )
    enc_h0, enc_n1, enc_i1, enc_h, mask = trunk_layer(
        line, x_images, first_w, norms, 0, cols, eps, "images", False, None, "enc_layer1", 0
    )
    enc_hs = trade([enc_h] * 4, "dp", ENC)
    dec_mask = swap_sections([mask])[0]
    att = place_attention(line, trade([att_rows] * 4, "dp", BOTH), 2 * tasks_n, part)
    enc_h1, enc_n2, enc_i2, enc_x, z = trunk_layer(
        line, enc_hs, second_w, norms, 1, cols, eps, "slices", True, mask, "enc_layer2", 0
    )
    z_pieces = swap_sections([z] * 4)
    enc_xs = trade([enc_x] * 4, "dp", ENC)

    dec_h0, dec_n1, dec_i1, dec_h = trunk_layer(
        line, z_pieces, first_w, norms, 0, cols, eps, "cells", False, dec_mask, "dec_layer1", 1
    )
    dec_hs = trade([dec_h] * 4, "dp", DEC)

    dec_h1, dec_n2, dec_i2, dec_x = trunk_layer(
        line, dec_hs, second_w, norms, 1, cols, eps, "slices", True, None, "dec_layer2", 1
    )
    dec_xs = trade([dec_x] * 4, "dp", BOTH)

    task_w = place_weights(line, task_all, tasks_n, depth, "place_tasks")[0]
    enc_us, enc_feats, kept, du = section_tasks(
        line, labels, enc_xs, att, task_w, mask, cots, cols
    )
    anchor(line, dec_xs, "decoder_there")
    dec_du = trade(du, "dp", DEC)
    q_cells = swap_sections([kept] * 4)

    dec_dx, lines, *rest = heads_reverse(
        line, labels, dec_xs, q_cells, dec_mask, dec_du, att, cols, "dec_heads", 1
    )
    dec_att, ds = rest[:4], rest[4:]
    ds = swap_sections(ds)
    lines = jnp.sum(lax.all_gather(lines, "dp"), axis=0)
    terms = lax.all_gather(lines, "rows")
    dec_w, *dh = weigh(line, dec_dx, [terms], True, "bargain")
    dh = trade(dh, "dp", BOTH)
    enc_w = swap_sections([dec_w])[0]
    nash_w = jnp.where(decoder, dec_w, enc_w)

    dec_dv2, dec_s2, *dh = trunk_reverse(
        line, dh, True, None, None, dec_n2, dec_i2, norms, 1, second_w, cols, ["slices"], None, "dec_back2", 1
    )
    dh = trade(dh, "dp", DEC)
    dec_u, dec_dw = dec_task_grads(line, dec_xs, q_cells, dec_mask, att, cots, depth, cols)
    dec_dv1, dec_s1, *rest = trunk_reverse(
        line, dh, False, None, dec_mask, dec_n1, dec_i1, norms, 0, first_w, cols, ["cells", "images"], None, "dec_back1", 1
    )
    dec_start, dec_dz = swap_sections(rest[:4]), rest[4:]
    *du, task_dw = enc_tasks_reverse(
        line, labels, ds, enc_us, task_w, mask, dec_dw, depth, cols
    )
    enc_du = trade(du, "dp", ENC)
    task_dw = lax.psum_scatter(task_dw, "rows", scatter_dimension=0, tiled=True)
    enc_dx, _, *att_parts = heads_reverse(
        line, labels, enc_xs, None, None, enc_du, att, cols, "enc_heads_back", 0, {k + 2: a for k, a in enumerate(dec_att)}
    )
    _, *dh = weigh(line, enc_dx, [enc_w], False, "enc_weigh")
    dh = trade(dh, "dp", BOTH)
    att_parts = trade(att_parts, "dp", BOTH)

    feats = dec_task_layer(line, dec_u, task_w, enc_feats, cols, "dec_tasks")
    feats = trade(feats, "dp", BOTH)
    enc_dv2, enc_s2, *dh = trunk_reverse(
        line, dh, True, dec_start, mask, enc_n2, enc_i2, norms, 1, second_w, cols, ["slices"], None, "enc_back2", 0
    )
    dh = trade(dh, "dp", ENC)

    enc_dv1, enc_s1, *dz = trunk_reverse(
        line, dh, False, None, None, enc_n1, enc_i1, norms, 0, first_w, cols, ["images"], dec_dz, "enc_back1", 0
    )
    dz = trade(dz, "dp", BOTH)
    trunk_dw = trunk_grads(
        line,
        [(enc_h0, enc_dv1), (enc_h1, enc_dv2)],
        [(dec_h0, dec_dv1), (dec_h1, dec_dv2)],
        depth,
        cols,
        "trunk_grads",
    )
    trunk_dw = lax.psum_scatter(trunk_dw, "rows", scatter_dimension=0, tiled=True)


    def share(sums, name):
        counts = [a.shape[1] for a in sums]

        def cut(ids_ref, *refs):
            outs = refs[len(sums) :]
            for j in range(4):
                row = 0
                for ref, count in zip(refs, counts):
                    for n in range(count):
                        outs[j][row] = ref[0, n, ids_ref[0] ^ j]
                        row += 1

        pieces = kernel_call(cut, [((sum(counts), depth, LANES), BF)] * 4, line, sums, name)
        return trade(pieces, "dp", BOTH)

    def join(layers, scale, name):
        counts = [pieces[0].shape[0] for pieces in layers]

        def body(ids_ref, *refs):
            o_ref, at = refs[-1], 0
            for m, count in enumerate(counts):
                for n in range(count):
                    for j in range(4):
                        value = refs[4 * m + j][n].astype(F32)
                        if scale is not None:
                            value = value * refs[4 * len(counts)][n : n + 1, :]
                        o_ref[at, :, span(ids_ref[0] ^ j, LANES)] = value
                    at += 1

        return kernel_call(
            body,
            [((sum(counts), depth, channels), F32)],
            line,
            [piece for pieces in layers for piece in pieces] + ([] if scale is None else [scale]),
            name,
        )[0]

    def cut_att(ids_ref, a, b, c, e, *rest):
        outs, total = rest[:4], rest[4]
        total[...] = (a[...].astype(F32) + b[...].astype(F32)) + (
            c[...].astype(F32) + e[...].astype(F32)
        )
        for j in range(4):
            outs[j][...] = total[:, span(ids_ref[1] ^ j, part), :].astype(BF)

    att_parts = kernel_call(
        cut_att,
        [((2 * tasks_n, part, LANES), BF)] * 4,
        line,
        att_parts,
        "cut_attention",
        scratch=[pltpu.VMEM((2 * tasks_n, LANES, LANES), F32)],
    )
    att_parts = trade(att_parts, "rows", BOTH)

    def cut_feats(ids_ref, a, b, c, e, *rest):
        outs, image = rest[:4], rest[4]
        for j, piece in enumerate((a, b, c, e)):
            image[:, :, span(ids_ref[0] ^ j, LANES)] = piece[...]
        for j in range(4):
            outs[j][...] = image[:, span(ids_ref[1] ^ j, strip), :]

    feats = kernel_call(
        cut_feats,
        [((tasks_n, strip, channels), BF)] * 4,
        line,
        feats,
        "cut_features",
        scratch=[pltpu.VMEM((tasks_n, size, channels), BF)],
    )
    feats = trade(feats, "rows", BOTH)

    sums = jnp.where(
        decoder, jnp.concatenate([dec_s1, dec_s2]), jnp.concatenate([enc_s1, enc_s2])
    )
    sums = trade([sums] * 4, "rows", BOTH)
    sums = (sums[0] + sums[1]) + (sums[2] + sums[3])
    sums = lax.dynamic_slice_in_dim(sums, row_at * part, part, axis=1)
    gain_out = jnp.stack([sums[0], sums[8]])
    bias_out = jnp.stack([sums[1], sums[9]])

    def cut_start(ids_ref, a, b, c, e, *rest):
        outs, image = rest[:4], rest[4]
        image[...] = (a[...].astype(F32) + b[...].astype(F32)) + (
            c[...].astype(F32) + e[...].astype(F32)
        )
        for j in range(4):
            outs[j][...] = image[span(ids_ref[1] ^ j, strip), :].astype(BF)

    starts = kernel_call(
        cut_start,
        [((strip, channels), BF)] * 4,
        line,
        dz,
        "cut_start",
        scratch=[pltpu.VMEM((size, channels), F32)],
    )
    starts = trade(starts, "rows", BOTH)

    task_parts = share([task_dw], "share_tasks")
    trunk_parts = share([trunk_dw], "share_trunk")

    def place_feats(ids_ref, a, b, c, e, o_ref):
        for j, piece in enumerate((a, b, c, e)):
            for t in range(tasks_n):
                o_ref[t, ids_ref[1] ^ j] = piece[t]

    feats_out = kernel_call(
        place_feats, [((tasks_n, micro_count, strip, channels), BF)], line, feats, "place_features"
    )[0]

    def join_att(ids_ref, a, b, c, e, w_ref, o_ref):
        total = (a[...].astype(F32) + b[...].astype(F32)) + (
            c[...].astype(F32) + e[...].astype(F32)
        )
        for t in range(2 * tasks_n):
            at = t % tasks_n
            o_ref[t] = total[t] * w_ref[at : at + 1, :]

    att_out = kernel_call(
        join_att,
        [((2 * tasks_n, part, LANES), F32)],
        line,
        att_parts + [nash_w],
        "join_attention",
    )[0]

    def place_start(ids_ref, a, b, c, e, o_ref):
        for j, piece in enumerate((a, b, c, e)):
            o_ref[ids_ref[1] ^ j] = piece[...].astype(F32)

    start_out = kernel_call(
        place_start, [((micro_count, strip, channels), F32)], line, starts, "place_start"
    )[0]
    task_out = join([task_parts], nash_w, "join_tasks")
    trunk_out = join([trunk_parts], None, "join_trunk")

    return (
        feats_out.reshape(1, tasks_n, micro_count, 1, rows_n, cols, channels),
        start_out.reshape(1, micro_count, 1, rows_n, cols, channels),
        trunk_out[None],
        gain_out[None],
        bias_out[None],
        att_out[:tasks_n][None],
        jnp.swapaxes(att_out[tasks_n:], 1, 2)[None],
        task_out[None],
        nash_w[:3, 0],
    )


def by_planes(x_in, task_cot):
    peers, planes = lax.axis_size("dp"), lax.axis_size("rows")
    micro, samples, _, _, channels = x_in.shape
    return (
        peers == 4
        and planes == 4
        and micro == planes
        and samples == 1
        and channels == peers * LANES
        and task_cot.shape[0] == 3
    )


def section_device(*arrays):
    if by_planes(arrays[0], arrays[3]):
        return plane_device(*arrays)
    return on_device(*arrays)


def solution(mesh):
    in_specs = (
        P(None, "dp", "rows", None, None),
        P(None, "dp", "rows", None),
        P(None, "dp", None),
        P(None, None, "dp", "rows", None, None),
        P("pipe", None, ("dp", "rows"), None),
        P("pipe", None, ("dp", "rows")),
        P("pipe", None, ("dp", "rows")),
        P("pipe", None, ("dp", "rows"), None),
        P("pipe", None, None, ("dp", "rows")),
        P("pipe", None, ("dp", "rows"), None),
    )
    out_specs = (
        P("pipe", None, None, "dp", "rows", None, None),
        P("pipe", None, "dp", "rows", None, None),
        P("pipe", None, ("dp", "rows"), None),
        P("pipe", None, ("dp", "rows")),
        P("pipe", None, ("dp", "rows")),
        P("pipe", None, ("dp", "rows"), None),
        P("pipe", None, None, ("dp", "rows")),
        P("pipe", None, ("dp", "rows"), None),
        P(),
    )
    return jax.shard_map(
        section_device, mesh=mesh, in_specs=in_specs, out_specs=out_specs, check_vma=False
    )
```

```python
import functools

import jax
import jax.numpy as jnp
from jax import lax
from jax.experimental import pallas as pl
from jax.experimental.pallas import tpu as pltpu
from jax.sharding import PartitionSpec as P

NASH_ITERS = 3


eps = 1e-05


def extended_2(array, sides, width):
    for axis, dim in sides:
        peers, length = (lax.axis_size(axis), array.shape[dim])
        up = [(i, (i + 1) % peers) for i in range(peers - 1)]
        down = [(j, i) for i, j in up]
        last = lax.slice_in_dim(array, length - width, length, axis=dim)
        first = lax.slice_in_dim(array, 0, width, axis=dim)
        before = lax.ppermute(last, axis, up)
        after = lax.ppermute(first, axis, down)
        array = jnp.concatenate([before, array, after], axis=dim)
    return array


def from_behind(array, axis, by):
    peers = lax.axis_size(axis)
    pairs = [(i, i + by) for i in range(peers) if 0 <= i + by < peers]
    return lax.ppermute(array, axis, pairs)


def silu_slope(preact):
    sigmoid_val = jax.nn.sigmoid(preact)
    return sigmoid_val * (1.0 + preact * (1.0 - sigmoid_val))


def choose_side(condition, when_true, when_false):

    def either(true_leaf, false_leaf):
        return jnp.where(condition, true_leaf, false_leaf)

    return jax.tree.map(either, when_true, when_false)


def pool_cells(field, positions):
    leading = field.shape[:-4]
    samples, rows_n, cols_n, channels = field.shape[-4:]
    blocks = field.astype(jnp.float32).reshape(
        leading + (samples, rows_n // 2, 2, cols_n // 2, 2, channels)
    )
    blocks = jnp.moveaxis(blocks, -4, -3).reshape(
        leading + (samples, rows_n // 2, cols_n // 2, 4, channels)
    )
    return jnp.sum(blocks * positions[..., None], axis=-2)


def unpool_cells(small, positions):
    leading = small.shape[:-4]
    samples, rows_h, cols_h, channels = small.shape[-4:]
    blocks = small.astype(jnp.float32)[..., None, :] * positions[..., None]
    blocks = blocks.reshape(leading + (samples, rows_h, cols_h, 2, 2, channels))
    blocks = jnp.moveaxis(blocks, -3, -4)
    return blocks.reshape(leading + (samples, 2 * rows_h, 2 * cols_h, channels))


def gather_taps(padded, rows_n, cols_n):
    stencil = [
        padded[:, :, offset // 3 : offset // 3 + rows_n, offset % 3 : offset % 3 + cols_n, :]
        for offset in range(9)
    ]
    return jnp.concatenate(stencil, axis=-1)


def conv_forward(field, weight):
    extended = extended_2(field, (("rows", 2),), 1)
    padded = jnp.pad(extended, ((0, 0), (0, 0), (0, 0), (1, 1), (0, 0)))
    stencil = gather_taps(padded, field.shape[2], field.shape[3])
    conv_out = jnp.einsum("ksrwq,kqd->ksrwd", stencil, weight, preferred_element_type=jnp.float32)
    return (conv_out, padded)


def conv_backward(padded, grad_out, weight, wanted):
    rows_n, cols_n = (grad_out.shape[2], grad_out.shape[3])
    extended = extended_2(grad_out, (("rows", 2),), 1)
    beside_all = jnp.pad(extended, ((0, 0), (0, 0), (0, 0), (1, 1), (0, 0)))
    flipped = jnp.stack(
        [
            beside_all[
                :,
                :,
                2 - offset // 3 : 2 - offset // 3 + rows_n,
                2 - offset % 3 : 2 - offset % 3 + cols_n,
                :,
            ]
            for offset in range(9)
        ],
        axis=-2,
    )
    kernel = weight.reshape(weight.shape[0], 9, weight.shape[2], weight.shape[2])
    grad_in = jnp.einsum("ksrwtd,ktcd->ksrwc", flipped, kernel, preferred_element_type=jnp.float32)
    weight_grad = None
    if wanted:
        weight_grad = jnp.einsum(
            "ksrwq,ksrwd->kqd",
            gather_taps(padded, rows_n, cols_n),
            grad_out,
            preferred_element_type=jnp.float32,
        )
    return (grad_in, weight_grad)


def norm_moments(conv_out, pixel_count):
    center = lax.psum(jnp.sum(conv_out, axis=(0, 1, 2, 3)), ("dp", "rows")) / pixel_count
    spread = (
        lax.psum(jnp.sum(jnp.square(conv_out - center), axis=(0, 1, 2, 3)), ("dp", "rows"))
        / pixel_count
    )
    return (center, lax.rsqrt(spread + eps))


def section_forward(section_input, carried, positions, params, stats, pixel_count):
    trunk_maps, gain_rows, bias_rows, down_maps, upward_maps, task_maps = params
    hidden = section_input[None]
    layers = []
    moments = []
    for section_layer in range(2):
        conv_out, padded = conv_forward(hidden, trunk_maps[section_layer][None])
        if stats is None:
            center, inverse_std = norm_moments(conv_out, pixel_count)
        else:
            center, inverse_std = stats[section_layer]
        normed = (conv_out - center) * inverse_std
        preact = gain_rows[section_layer] * normed + bias_rows[section_layer]
        layers.append((padded, normed, preact))
        moments.append((center, inverse_std))
        hidden = jax.nn.silu(preact).astype(jnp.bfloat16)
    mixture = (hidden.astype(jnp.float32) + carried.astype(jnp.float32)).astype(jnp.bfloat16)
    inner_act = jnp.einsum(
        "tsrwc,tca->tsrwa", mixture, down_maps, preferred_element_type=jnp.float32
    )
    active_mask_flag = jax.nn.silu(inner_act).astype(jnp.bfloat16)
    class_logits = jnp.einsum(
        "zfhpv,zvm->zfhpm", active_mask_flag, upward_maps, preferred_element_type=jnp.float32
    )
    gating = jax.nn.sigmoid(class_logits)
    product = (gating * hidden.astype(jnp.float32)).astype(jnp.bfloat16)
    features, padded_task = conv_forward(product, task_maps)
    return {
        "layers": layers,
        "moments": moments,
        "shared": hidden,
        "mixture": mixture,
        "inner_act": inner_act,
        "active": active_mask_flag,
        "gating": gating,
        "padded_task": padded_task,
        "features": features,
        "section_input": section_input,
        "carried": carried,
        "positions": positions,
    }


def heads_backward(saved_record, grad_feats, params, wanted):
    down_maps, upward_maps, task_maps = (params[3], params[4], params[5])
    task_back, task_slope = conv_backward(
        saved_record["padded_task"], grad_feats, task_maps, wanted
    )
    shared = saved_record["shared"].astype(jnp.float32)
    gating = saved_record["gating"]
    logits_gradient = (task_back * shared * gating * (1.0 - gating)).astype(jnp.bfloat16)
    grad_active = jnp.einsum(
        "qubef,qxf->qubex", logits_gradient, upward_maps, preferred_element_type=jnp.float32
    )
    grad_inner = (grad_active * silu_slope(saved_record["inner_act"])).astype(jnp.bfloat16)
    grad_mixture = jnp.einsum(
        "tsrwa,tca->tsrwc", grad_inner, down_maps, preferred_element_type=jnp.float32
    )
    through = task_back * gating + grad_mixture
    slopes = None
    if wanted:
        slope_up = jnp.einsum(
            "munfg,munfq->mgq",
            saved_record["active"],
            logits_gradient,
            preferred_element_type=jnp.float32,
        )
        slope_down = jnp.einsum(
            "tsrwc,tsrwa->tca",
            saved_record["mixture"],
            grad_inner,
            preferred_element_type=jnp.float32,
        )
        slopes = (slope_down, slope_up, task_slope)
    return (through, grad_mixture, slopes)


def trunk_backward(saved_record, grad_shared, params, pixel_count):
    trunk_maps, gain_rows = (params[0], params[1])
    grad_hidden = grad_shared
    conv_grads = [None, None]
    gain_grads = [None, None]
    bias_grads = [None, None]
    for section_layer in (1, 0):
        padded, normed, preact = saved_record["layers"][section_layer]
        inverse_std = saved_record["moments"][section_layer][1]
        grad_pre = grad_hidden * silu_slope(preact)
        bias_part = jnp.sum(grad_pre, axis=(0, 1, 2, 3))
        gain_part = jnp.sum(grad_pre * normed, axis=(0, 1, 2, 3))
        bias_total, gain_total = lax.psum((bias_part, gain_part), ("dp", "rows"))
        grad_conv = (
            inverse_std
            * gain_rows[section_layer]
            * (grad_pre - bias_total / pixel_count - normed * gain_total / pixel_count)
        )
        grad_hidden, weight_grad = conv_backward(
            padded, grad_conv.astype(jnp.bfloat16), trunk_maps[section_layer][None], True
        )
        conv_grads[section_layer] = weight_grad[0]
        gain_grads[section_layer] = gain_part
        bias_grads[section_layer] = bias_part
    return (grad_hidden, jnp.stack(conv_grads), jnp.stack(gain_grads), jnp.stack(bias_grads))


def solve_small(matrix, right_side):
    cofactor = [
        [
            matrix[1, 1] * matrix[2, 2] - matrix[1, 2] * matrix[2, 1],
            matrix[1, 2] * matrix[2, 0] - matrix[1, 0] * matrix[2, 2],
            matrix[1, 0] * matrix[2, 1] - matrix[1, 1] * matrix[2, 0],
        ],
        [
            matrix[0, 2] * matrix[2, 1] - matrix[0, 1] * matrix[2, 2],
            matrix[0, 0] * matrix[2, 2] - matrix[0, 2] * matrix[2, 0],
            matrix[0, 1] * matrix[2, 0] - matrix[0, 0] * matrix[2, 1],
        ],
        [
            matrix[0, 1] * matrix[1, 2] - matrix[0, 2] * matrix[1, 1],
            matrix[0, 2] * matrix[1, 0] - matrix[0, 0] * matrix[1, 2],
            matrix[0, 0] * matrix[1, 1] - matrix[0, 1] * matrix[1, 0],
        ],
    ]
    determinant = (
        matrix[0, 0] * cofactor[0][0]
        + matrix[0, 1] * cofactor[0][1]
        + matrix[0, 2] * cofactor[0][2]
    )
    answer = [
        (
            cofactor[0][col_index] * right_side[0]
            + cofactor[1][col_index] * right_side[1]
            + cofactor[2][col_index] * right_side[2]
        )
        / determinant
        for col_index in range(3)
    ]
    return jnp.stack(answer)


def nash_solve(gram_sum):
    trace_mean = (gram_sum[0, 0] + gram_sum[1, 1] + gram_sum[2, 2]) / 3.0 + 1e-06
    normalized = gram_sum / trace_mean
    diagonal = jnp.stack([normalized[0, 0], normalized[1, 1], normalized[2, 2]])
    nash_alpha = lax.rsqrt(diagonal + 1e-06)
    for sweep_index in range(NASH_ITERS):
        residual = jnp.sum(normalized * nash_alpha[None, :], axis=1) - 1.0 / nash_alpha
        curvature = normalized + jnp.diag(1.0 / (nash_alpha * nash_alpha))
        update = solve_small(curvature, residual)
        nash_alpha = nash_alpha * jnp.exp(-0.5 * jnp.tanh(update / nash_alpha))
    return nash_alpha


def on_device(
    x_in,
    pool_index,
    task_mask,
    task_cot,
    trunk_conv,
    norm_gain,
    norm_bias,
    att_down,
    attention_up_weights,
    task_conv,
):
    micro_count = x_in.shape[0]
    tasks_n = task_cot.shape[0]
    decoder_side = lax.axis_index("pipe") == 1
    pixel_count = (
        x_in.shape[1] * x_in.shape[2] * x_in.shape[3] * lax.axis_size("dp") * lax.axis_size("rows")
    )
    pieces = (
        lax.all_gather(trunk_conv, ("dp", "rows"), axis=2, tiled=True),
        lax.all_gather(norm_gain, ("dp", "rows"), axis=2, tiled=True),
        lax.all_gather(norm_bias, ("dp", "rows"), axis=2, tiled=True),
        lax.all_gather(att_down, ("dp", "rows"), axis=2, tiled=True),
        lax.all_gather(attention_up_weights, ("dp", "rows"), axis=3, tiled=True),
        lax.all_gather(task_conv, ("dp", "rows"), axis=2, tiled=True),
    )
    params = (
        pieces[0][0],
        pieces[1][0].astype(jnp.float32),
        pieces[2][0].astype(jnp.float32),
        pieces[3][0],
        pieces[4][0],
        pieces[5][0],
    )
    onehot = (pool_index[..., None] == jnp.arange(4, dtype=jnp.int32)).astype(jnp.float32)
    mask_weights = jnp.transpose(task_mask, (0, 2, 1)).astype(jnp.float32)
    no_carry = jnp.zeros((tasks_n,) + x_in.shape[1:], jnp.bfloat16)
    incoming = jnp.zeros(
        (tasks_n + 1, x_in.shape[1], x_in.shape[2] // 2, x_in.shape[3] // 2, x_in.shape[4]),
        jnp.bfloat16,
    )
    records = []
    for period in range(micro_count + 1):
        enc_index = min(period, micro_count - 1)
        dec_index = max(period - 1, 0)
        positions = jnp.where(decoder_side, onehot[dec_index], onehot[enc_index])
        section_input = jnp.where(
            decoder_side, unpool_cells(incoming[0], positions).astype(jnp.bfloat16), x_in[enc_index]
        )
        carried = jnp.where(
            decoder_side, unpool_cells(incoming[1:], positions).astype(jnp.bfloat16), no_carry
        )
        saved_record = section_forward(section_input, carried, positions, params, None, pixel_count)
        records.append(saved_record)
        if period < micro_count:
            outgoing = jnp.concatenate(
                [
                    pool_cells(saved_record["shared"], positions),
                    pool_cells(saved_record["features"].astype(jnp.bfloat16), positions),
                ],
                axis=0,
            )
            incoming = from_behind(outgoing.astype(jnp.bfloat16), "pipe", 1)
    kept_records = []
    gram_sum = jnp.zeros((tasks_n, tasks_n), jnp.float32)
    for micro_index in range(micro_count):
        source_input = choose_side(decoder_side, records[micro_index + 1], records[micro_index])
        chosen = section_forward(
            source_input["section_input"],
            source_input["carried"],
            source_input["positions"],
            params,
            source_input["moments"],
            pixel_count,
        )
        kept_records.append(chosen)
        plain_cot = task_cot[:, micro_index] * mask_weights[micro_index][:, :, None, None, None]
        through, unused_mixture, unused_slopes = heads_backward(
            chosen, plain_cot.astype(jnp.bfloat16), params, False
        )
        flattened = through.reshape(tasks_n, -1)
        partial_gram = jnp.dot(flattened, flattened.T, precision=lax.Precision.HIGHEST)
        gram_sum = gram_sum + jnp.where(decoder_side, partial_gram, 0.0)
    gram_sum = lax.psum(gram_sum, ("pipe", "dp", "rows"))
    nash_alpha = nash_solve(gram_sum)
    returning = jnp.zeros_like(incoming)
    start_grads = []
    trunk_sum, gain_sum, bias_sum = (0.0, 0.0, 0.0)
    down_sum, up_sum, task_sum = (0.0, 0.0, 0.0)
    for period in range(micro_count + 1):
        dec_index = max(micro_count - 1 - period, 0)
        enc_index = min(micro_count - period, micro_count - 1)
        active_flag = 1.0 if period < micro_count else 0.0
        chosen = choose_side(decoder_side, kept_records[dec_index], kept_records[enc_index])
        positions = chosen["positions"]
        weighted = (
            nash_alpha[:, None, None, None, None]
            * mask_weights[dec_index][:, :, None, None, None]
            * task_cot[:, dec_index].astype(jnp.float32)
            * active_flag
        )
        grad_feats = jnp.where(
            decoder_side, weighted, unpool_cells(returning[1:], positions)
        ).astype(jnp.bfloat16)
        through, grad_mixture, slopes = heads_backward(chosen, grad_feats, params, True)
        down_sum = down_sum + slopes[0]
        up_sum = up_sum + slopes[1]
        task_sum = task_sum + slopes[2]
        pooled_back = jnp.where(decoder_side, 0.0, unpool_cells(returning[0:1], positions))
        grad_shared = jnp.sum(through, axis=0, keepdims=True) + pooled_back
        grad_start, conv_grads, gain_grads, bias_grads = trunk_backward(
            chosen, grad_shared, params, pixel_count
        )
        start_grads.append(grad_start[0])
        trunk_sum = trunk_sum + conv_grads
        gain_sum = gain_sum + gain_grads
        bias_sum = bias_sum + bias_grads
        if period < micro_count:
            outgoing = jnp.concatenate(
                [pool_cells(grad_start, positions), pool_cells(grad_mixture, positions)], axis=0
            )
            returning = from_behind(outgoing.astype(jnp.bfloat16), "pipe", -1)
    features_out = jnp.stack(
        [
            jnp.where(
                decoder_side, records[micro_index + 1]["features"], records[micro_index]["features"]
            )
            for micro_index in range(micro_count)
        ],
        axis=1,
    ).astype(jnp.bfloat16)
    grads_out = jnp.stack(
        [
            jnp.where(
                decoder_side,
                start_grads[micro_count - 1 - micro_index],
                start_grads[micro_count - micro_index],
            )
            for micro_index in range(micro_count)
        ],
        axis=0,
    )
    shares = (
        lax.psum_scatter(trunk_sum[None], ("dp", "rows"), scatter_dimension=2, tiled=True),
        lax.psum_scatter(gain_sum[None], ("dp", "rows"), scatter_dimension=2, tiled=True),
        lax.psum_scatter(bias_sum[None], ("dp", "rows"), scatter_dimension=2, tiled=True),
        lax.psum_scatter(down_sum[None], ("dp", "rows"), scatter_dimension=2, tiled=True),
        lax.psum_scatter(up_sum[None], ("dp", "rows"), scatter_dimension=3, tiled=True),
        lax.psum_scatter(task_sum[None], ("dp", "rows"), scatter_dimension=2, tiled=True),
    )
    return (
        features_out[None],
        grads_out[None],
        shares[0],
        shares[1],
        shares[2],
        shares[3],
        shares[4],
        shares[5],
        nash_alpha,
    )


BF = jnp.bfloat16
F32 = jnp.float32
LANES = 128
TAPS = 9
VMEM_BYTES = 56 * 1024 * 1024


class Line:
    def __init__(self, ids):
        self.ids = ids
        self.last = None


def on_section(body, only):
    if only is None:
        return body

    def gated(ids_ref, *refs):
        @pl.when(ids_ref[2] == only)
        def _():
            body(ids_ref, *refs)

    return gated


def unread(body, count, first):
    def whole(*refs):
        body(*refs[:first], *refs[first + count :])

    return whole


LIGHT = pl.CostEstimate(flops=300_000_000, bytes_accessed=1, transcendentals=0)


def kernel_call(body, outs, line, vmem, name, scratch=(), only=None, smem=(), after=()):
    extra = list(after) + ([] if line.last is None else [line.last])
    first = 1 + len(smem) + len(vmem)
    results = pl.pallas_call(
        unread(on_section(body, only), len(extra), first),
        out_shape=[jax.ShapeDtypeStruct(shape, dtype) for shape, dtype in outs],
        in_specs=[pl.BlockSpec(memory_space=pltpu.SMEM)] * (1 + len(smem))
        + [pl.BlockSpec(memory_space=pltpu.VMEM)] * len(vmem)
        + [pl.BlockSpec(memory_space=pl.ANY)] * len(extra),
        out_specs=[pl.BlockSpec(memory_space=pltpu.VMEM)] * len(outs),
        scratch_shapes=list(scratch),
        compiler_params=pltpu.CompilerParams(vmem_limit_bytes=VMEM_BYTES),
        cost_estimate=LIGHT,
        name=name,
    )(line.ids, *smem, *vmem, *extra)
    line.last = results[-1]
    return results


def stepped_call(body, outs, line, vmem, name, scratch=(), only=None, fixed=()):
    extra = [] if line.last is None else [line.last]
    steps = outs[0][0][0]

    def block(shape):
        rest = len(shape) - 1
        return pl.BlockSpec(
            (1,) + tuple(shape[1:]),
            lambda t, ids: (t if only is None else jnp.where(ids[2] == only, t, 0),) + (0,) * rest,
        )

    def same(shape):
        return pl.BlockSpec(shape, lambda t, ids: (0,) * len(shape))

    results = pl.pallas_call(
        unread(on_section(body, only), len(extra), 1 + len(vmem)),
        grid_spec=pltpu.PrefetchScalarGridSpec(
            num_scalar_prefetch=1,
            grid=(steps,),
            in_specs=[same(a.shape) if k in fixed else block(a.shape) for k, a in enumerate(vmem)]
            + [pl.BlockSpec(memory_space=pl.ANY)] * len(extra),
            out_specs=[block(shape) for shape, _ in outs],
            scratch_shapes=list(scratch),
        ),
        out_shape=[jax.ShapeDtypeStruct(shape, dtype) for shape, dtype in outs],
        compiler_params=pltpu.CompilerParams(vmem_limit_bytes=VMEM_BYTES),
        cost_estimate=LIGHT,
        name=name,
    )(line.ids, *vmem, *extra)
    line.last = results[-1]
    return results


class Parts:
    def __init__(self, given, held, given_sems, results, kept, result_sems, split_in, split_out):
        self.given = [self.copies(a, b, given_sems, k, k in split_in) for k, (a, b) in enumerate(zip(given, held))]
        self.results = [
            self.copies(b, a, result_sems, k, k in split_out) for k, (a, b) in enumerate(zip(results, kept))
        ]
        self.waiting = []

    def copies(self, source, target, sems, k, split):
        if not split:
            return [pltpu.make_async_copy(source, target, sems.at[k, 0])]
        return [
            pltpu.make_async_copy(source.at[p], target.at[p], sems.at[k, p])
            for p in range(source.shape[0])
        ]

    def begin(self):
        for p in range(3):
            for copies in self.given:
                if p < len(copies):
                    copies[p].start()

    def need(self, k, p=0):
        self.given[k][p].wait()

    def send(self, k, p=0):
        self.results[k][p].start()
        self.waiting.append(self.results[k][p])

    def finish(self):
        for copy in self.waiting:
            copy.wait()


def section_call(
    body, outs, line, vmem, name, scratch=(), only=None, other=None, paired=(), split_in=(), split_out=(), smem=()
):
    other, paired = dict(other or {}), dict(paired)
    n_in, n_out = len(vmem), len(outs)
    passed, swapped = list(other.values()), list(paired.values())
    extra = [] if line.last is None else [line.last]

    def whole(*refs):
        scalars, refs = refs[: 1 + len(smem)], refs[1 + len(smem) :]
        ids_ref = scalars[0]
        given, refs = refs[:n_in], refs[n_in:]
        passed_refs, refs = refs[: len(passed)], refs[len(passed) :]
        swapped_refs, refs = refs[: len(swapped)], refs[len(swapped) + len(extra) :]
        results, refs = refs[:n_out], refs[n_out:]
        held, refs = refs[:n_in], refs[n_in:]
        kept, refs = refs[:n_out], refs[n_out:]
        given_sems, result_sems, refs = refs[0], refs[1], refs[2:]

        def run(sources):
            parts = Parts(sources, held, given_sems, results, kept, result_sems, split_in, split_out)
            parts.begin()
            for k in range(n_in):
                if k not in split_in:
                    parts.need(k)
            if split_in or split_out:
                body(*scalars, *held, *kept, *refs, parts=parts)
            else:
                body(*scalars, *held, *kept, *refs)
            for k in range(n_out):
                if k not in split_out:
                    parts.send(k)
            parts.finish()

        def hand_out():
            for source, target in ((passed_refs, kept), (kept, results)):
                copies = []
                for at, k in enumerate(other):
                    first = source[at] if source is passed_refs else source[k]
                    copies.append(pltpu.make_async_copy(first, target[k], result_sems.at[k, 0]))
                for copy in copies:
                    copy.start()
                for copy in copies:
                    copy.wait()

        if only is not None:
            pl.when(ids_ref[2] == only)(lambda: run(given))
            if passed:
                pl.when(ids_ref[2] != only)(hand_out)
        elif paired:
            mixed = list(given)
            for k, ref in zip(paired, swapped_refs):
                mixed[k] = ref
            pl.when(ids_ref[2] == 0)(lambda: run(given))
            pl.when(ids_ref[2] == 1)(lambda: run(mixed))
        else:
            run(given)

    results = pl.pallas_call(
        whole,
        out_shape=[jax.ShapeDtypeStruct(shape, dtype) for shape, dtype in outs],
        in_specs=[pl.BlockSpec(memory_space=pltpu.SMEM)] * (1 + len(smem))
        + [pl.BlockSpec(memory_space=pl.ANY)] * (n_in + len(passed) + len(swapped) + len(extra)),
        out_specs=[pl.BlockSpec(memory_space=pl.ANY)] * n_out,
        scratch_shapes=[pltpu.VMEM(a.shape, a.dtype) for a in vmem]
        + [pltpu.VMEM(shape, dtype) for shape, dtype in outs]
        + [pltpu.SemaphoreType.DMA((n_in, 3)), pltpu.SemaphoreType.DMA((n_out, 3))]
        + list(scratch),
        compiler_params=pltpu.CompilerParams(vmem_limit_bytes=VMEM_BYTES),
        cost_estimate=LIGHT,
        name=name,
    )(line.ids, *smem, *vmem, *passed, *swapped, *extra)
    line.last = results[-1]
    return results


def anchor(line, arrays, name):
    def body(*refs):
        refs[-1][...] = jnp.zeros((8, LANES), F32)

    line.last = pl.pallas_call(
        body,
        out_shape=jax.ShapeDtypeStruct((8, LANES), F32),
        in_specs=[pl.BlockSpec(memory_space=pl.ANY)] * (len(arrays) + 1),
        out_specs=pl.BlockSpec(memory_space=pltpu.VMEM),
        cost_estimate=LIGHT,
        name=name,
    )(*arrays, line.last)


def trade(pieces, axis, sections):
    count = lax.axis_size(axis)
    taken = [pieces[0]]
    for j in range(1, count):
        pairs = [(p * count + i, p * count + (i ^ j)) for p in sections for i in range(count)]
        taken.append(lax.ppermute(pieces[j], ("pipe", axis), pairs))
    return taken


def swap_sections(pieces):
    count = lax.axis_size("dp")
    return [
        lax.ppermute(
            pieces[j],
            ("pipe", "dp"),
            [(p * count + i, (1 - p) * count + (i ^ j)) for p in range(2) for i in range(count)],
        )
        for j in range(len(pieces))
    ]


def span(index, size):
    return pl.ds(pl.multiple_of(index * size, size), size)


def dot(a, b):
    return jnp.dot(a, b, preferred_element_type=F32)


def dot_nt(a, b):
    return lax.dot_general(a, b, (((1,), (1,)), ((), ())), preferred_element_type=F32)


def dot_tn(a, b):
    return lax.dot_general(a, b, (((0,), (0,)), ((), ())), preferred_element_type=F32)


def column_of(shape, cols):
    return lax.broadcasted_iota(jnp.int32, shape, 0) % cols


def fold_taps(taps, cols):
    size = taps.shape[0]
    blank = jnp.zeros((cols, LANES), F32)
    sums = []
    for b in range(3):
        first = taps[:, b * LANES : (b + 1) * LANES]
        second = taps[:, (3 + b) * LANES : (4 + b) * LANES]
        third = taps[:, (6 + b) * LANES : (7 + b) * LANES]
        sums.append(
            second
            + jnp.concatenate([blank, first[: size - cols]], axis=0)
            + jnp.concatenate([third[cols:], blank], axis=0)
        )
    column = column_of((size, LANES), cols)
    left = jnp.where(column == 0, 0.0, pltpu.roll(sums[0], 1, 0))
    right = jnp.where(column == cols - 1, 0.0, pltpu.roll(sums[2], size - 1, 0))
    return sums[1] + left + right


def spread_taps(grad, cols):
    size = grad.shape[0]
    column = column_of((size, LANES), cols)
    moved = [
        jnp.where(column == cols - 1, 0.0, pltpu.roll(grad, size - 1, 0)).astype(BF),
        grad.astype(BF),
        jnp.where(column == 0, 0.0, pltpu.roll(grad, 1, 0)).astype(BF),
    ]
    blank = jnp.zeros((cols, LANES), BF)
    above = [jnp.concatenate([m[cols:], blank], axis=0) for m in moved]
    below = [jnp.concatenate([blank, m[: size - cols]], axis=0) for m in moved]
    return jnp.concatenate(above + moved + below, axis=1)


def cut_weights(line, arrays, name):
    depth = arrays[0][0].shape[1]
    count = sum(len(layers) for _, layers in arrays)

    def body(ids_ref, *refs):
        given, outs = refs[: len(arrays)], refs[len(arrays) :]
        for j in range(4):
            cut = span(ids_ref[0] ^ j, LANES)
            row = 0
            for ref, (_, layers) in zip(given, arrays):
                for n in layers:
                    outs[j][row * depth : (row + 1) * depth, :] = ref[n, :, cut]
                    row += 1

    return kernel_call(
        body, [((count * depth, LANES), BF)] * 4, line, [a for a, _ in arrays], name
    )


def stack_weights(line, pieces, groups, extra, name):
    depth = pieces[0].shape[0] // sum(len(group) for group in groups)
    more = [a for arrays in extra for a in arrays]

    def body(ids_ref, *refs):
        given, more_in, outs = refs[:4], list(refs[4 : 4 + len(more)]), refs[4 + len(more) :]
        for k, group in enumerate(groups):
            for at, n in enumerate(group):
                for j in range(4):
                    rows = span(4 * at + (ids_ref[0] ^ j), depth)
                    outs[k][rows, :] = given[j][n * depth : (n + 1) * depth, :]
            at = 4 * len(group) * depth
            for array in extra[k]:
                outs[k][at : at + array.shape[0], :] = more_in.pop(0)[...]
                at += array.shape[0]

    sizes = [
        4 * len(group) * depth + sum(a.shape[0] for a in extra[k])
        for k, group in enumerate(groups)
    ]
    return kernel_call(
        body, [((n, LANES), BF) for n in sizes], line, list(pieces) + more, name
    )


def place_weights(line, gathered, count, depth, name, norm_rows=0, tail_rows=0):
    whole = 16 * depth
    channels = whole // TAPS
    end = 4 * count * depth
    apart = norm_rows > 0

    def body(ids_ref, g_ref, *rest):
        flat = rest[-1]
        for n in range(count):
            for r in range(4):
                for p in range(4):
                    rows = slice((4 * n + p) * depth, (4 * n + p + 1) * depth)
                    flat[(p * 4 + r) * depth : (p * 4 + r + 1) * depth, :] = g_ref[r, rows, :]
            for tap in range(TAPS):
                lanes = slice(tap * LANES, (tap + 1) * LANES)
                value = flat[tap * channels : (tap + 1) * channels, :]
                if apart:
                    rest[n][0, :, lanes] = value
                else:
                    rest[0][n, :, lanes] = value
        if apart:
            own = [g_ref[r, end : end + norm_rows, :].astype(F32) for r in range(4)]
            rest[count][...] = (own[0] + own[1]) + (own[2] + own[3])
            rest[count + 1][...] = g_ref[:, end + norm_rows : end + norm_rows + tail_rows, :]

    if apart:
        outs = [((1, channels, TAPS * LANES), BF)] * count
        outs += [((norm_rows, LANES), F32), ((4, tail_rows, LANES), BF)]
    else:
        outs = [((count, channels, TAPS * LANES), BF)]
    return kernel_call(
        body, outs, line, [gathered], name, scratch=[pltpu.VMEM((whole, LANES), BF)]
    )


def place_attention(line, pieces, maps, part):
    def body(ids_ref, *refs):
        given, out = refs[:4], refs[4]
        for j in range(4):
            for r in range(4):
                chunk = (ids_ref[0] ^ j) * 4 + r
                for t in range(maps):
                    out[t, span(chunk, part), :] = given[j][r, t * part : (t + 1) * part, :]

    return kernel_call(
        body, [((maps, 16 * part, LANES), BF)], line, list(pieces), "place_attention"
    )[0]


def trunk_layer(
    line, pieces, weight, norms, layer, cols, eps_value, form, last, masked, name, only=None
):
    channels = weight.shape[1]
    size = {"images": 1, "slices": 0.25, "cells": 1}[form]
    size = int(pieces[0].shape[0] * size)
    pixels = 4 * size
    whole_images = form == "images"

    def body(ids_ref, *refs):
        given, (w_ref, norm_ref) = refs[:4], refs[4:6]
        at = 6
        if masked is not None and not whole_images:
            mask_ref = refs[6]
            at = 7
        outs, v_ref, pairs_ref = refs[at:-2], refs[-2], refs[-1]
        field = outs[0]
        for j in range(4):
            peer = ids_ref[0] ^ j
            if whole_images:
                field[span(peer, size), :] = given[j][:, :channels]
                outs[4][span(peer, size), :] = given[j][:, channels:]
            elif form == "cells":
                cells = spread_pairs(given[j][...].astype(F32), pairs_ref, cols)
                field[:, span(peer, LANES)] = cells.astype(BF) * mask_ref[...]
            else:
                field[:, span(peer, LANES)] = given[j][...]
        for i in range(4):
            part = slice(i * size, (i + 1) * size)
            v_ref[part, :] = fold_taps(dot(field[part, :], w_ref[0]), cols)
        conv_out = v_ref[...]
        center = jnp.sum(conv_out, axis=0, keepdims=True) / pixels
        moved = conv_out - center
        spread = jnp.sum(moved * moved, axis=0, keepdims=True) / pixels
        inverse = lax.rsqrt(spread + eps_value)
        normed = moved * inverse
        outs[1][...] = normed
        outs[2][...] = jnp.broadcast_to(inverse, (8, LANES))
        preact = norm_ref[layer : layer + 1, :] * normed + norm_ref[2 + layer : 3 + layer, :]
        hidden = (preact * jax.nn.sigmoid(preact)).astype(BF)
        outs[3][...] = hidden
        if last and masked is not None:
            kept = hidden.astype(F32) * mask_ref[...].astype(F32)
            outs[4][...] = pool_pairs(kept, pairs_ref, cols).astype(BF)

    outs = [((pixels, channels), BF), ((pixels, LANES), F32), ((8, LANES), F32)]
    outs.append(((pixels, LANES), BF))
    if last and masked is not None:
        outs.append(((size, LANES), BF))
    elif whole_images:
        outs.append(((pixels, LANES), BF))
    extra = [masked] if masked is not None and not whole_images else []
    return kernel_call(
        body,
        outs,
        line,
        list(pieces) + [weight, norms] + extra,
        name,
        scratch=[pltpu.VMEM((pixels, LANES), F32), pltpu.VMEM((pixels // 2, LANES), F32)],
        only=only,
    )


def pool_pairs(value, pairs_ref, cols):
    size = value.shape[0]
    halves = value.reshape(size // (2 * cols), 2, cols, LANES)
    pairs_ref[: size // 2, :] = (halves[:, 0] + halves[:, 1]).reshape(size // 2, LANES)
    return pairs_ref[pl.ds(0, size // 4, stride=2), :] + pairs_ref[pl.ds(1, size // 4, stride=2), :]


def spread_pairs(small, pairs_ref, cols):
    size = 4 * small.shape[0]
    pairs_ref[pl.ds(0, size // 4, stride=2), :] = small
    pairs_ref[pl.ds(1, size // 4, stride=2), :] = small
    rows = pairs_ref[: size // 2, :].reshape(size // (2 * cols), 1, cols, LANES)
    return jnp.broadcast_to(rows, (size // (2 * cols), 2, cols, LANES)).reshape(size, LANES)


def attend(x, mixture, down, up_t):
    inner = dot(mixture, down)
    active = (inner * jax.nn.sigmoid(inner)).astype(BF)
    gate = jax.nn.sigmoid(dot_nt(active, up_t))
    return inner, active, gate


def label_at(label_ref, ids_ref, device, t):
    return label_ref[(device * 4 + ids_ref[1]) * 3 + t]


def slot_of(label_ref, ids_ref, device, t):
    return sum([label_at(label_ref, ids_ref, device, k) for k in range(t)], jnp.int32(0))


def section_tasks(line, labels, x_slices, att, weights, mask, cots, cols):
    pixels = x_slices[0].shape[0]
    size = pixels // 4
    tasks_n, channels, _ = weights.shape
    down, up_t = att[:tasks_n], att[tasks_n:]

    def body(ids_ref, label_ref, *refs):
        x_in, down_ref, up_ref, w_ref, mask_ref, cot_in = refs[:4], *refs[4:8], refs[8:12]
        fields, feats, cells, du = refs[12:16], refs[16:20], refs[20], refs[21:25]
        x_ref, pairs_ref = refs[25:]
        t = pl.program_id(0)

        @pl.when(ids_ref[2] == 0)
        def _():
            @pl.when(t == 0)
            def _():
                for j in range(4):
                    x_ref[:, span(ids_ref[0] ^ j, LANES)] = x_in[j][...]

            for j in range(4):
                rows = span(ids_ref[0] ^ j, size)
                x = x_ref[rows, :]
                _, _, gate = attend(x, x, down_ref[0], up_ref[0])
                u = (gate * x.astype(F32)).astype(BF)
                fields[j][0] = u
                value = fold_taps(dot(u, w_ref[0]), cols)
                feats[j][0] = value.astype(BF)
                kept = value * mask_ref[rows, :].astype(F32)
                cells[0, span(ids_ref[0] ^ j, size // 4), :] = pool_pairs(
                    kept, pairs_ref, cols
                ).astype(BF)

        @pl.when(ids_ref[2] == 1)
        def _():
            for j in range(4):
                device = ids_ref[0] ^ j
                before = jnp.where(t > 0, label_at(label_ref, ids_ref, device, 0), 0)
                before += jnp.where(t > 1, label_at(label_ref, ids_ref, device, 1), 0)

                @pl.when(t == 0)
                def _(j=j):
                    du[j][...] = jnp.zeros_like(du[j])

                @pl.when(label_at(label_ref, ids_ref, device, t) == 1)
                def _(j=j, before=before):
                    taps = spread_taps(cot_in[j][0].astype(F32), cols)
                    du[j][before] = dot_nt(taps, w_ref[0]).astype(BF)

    def step(shape, only=None):
        return pl.BlockSpec(
            (1,) + shape[1:],
            lambda t, ids, _: (t if only is None else jnp.where(ids[2] == only, t, 0),)
            + (0,) * (len(shape) - 1),
        )

    def same(shape):
        return pl.BlockSpec(shape, lambda t, ids, _: (0,) * len(shape))

    outs = [(tasks_n, size, channels)] * 4 + [(tasks_n, size, LANES)] * 5 + [(2, size, channels)] * 4
    args = list(x_slices) + [down, up_t, weights, mask] + list(cots)
    results = pl.pallas_call(
        unread(body, 1, 2 + len(args)),
        grid_spec=pltpu.PrefetchScalarGridSpec(
            num_scalar_prefetch=2,
            grid=(tasks_n,),
            in_specs=[same(a.shape) for a in x_slices]
            + [step(down.shape, 0), step(up_t.shape, 0), step(weights.shape), same(mask.shape)]
            + [step(a.shape, 1) for a in cots]
            + [pl.BlockSpec(memory_space=pl.ANY)],
            out_specs=[step(shape, 0) for shape in outs[:9]] + [same(shape) for shape in outs[9:]],
            scratch_shapes=[pltpu.VMEM((pixels, channels), BF), pltpu.VMEM((size // 2, LANES), F32)],
        ),
        out_shape=[jax.ShapeDtypeStruct(shape, BF) for shape in outs],
        compiler_params=pltpu.CompilerParams(vmem_limit_bytes=VMEM_BYTES),
        cost_estimate=LIGHT,
        name="section_tasks",
    )(line.ids, labels, *args, line.last)
    line.last = results[-1]
    return results[:4], results[4:8], results[8], results[9:]


def grads_of_taps(field, grad_at, taps_ref, flat, out_at, cols, depth):
    size = taps_ref.shape[0] // 4
    for i in range(4 if grad_at is not None else 0):
        taps_ref[i * size : (i + 1) * size, :] = spread_taps(grad_at(i).astype(F32), cols)
    channels = field.shape[1]
    for row in range(3):
        whole = dot_tn(field, taps_ref[:, row * 3 * LANES : (row + 1) * 3 * LANES])
        for b in range(3):
            tap = 3 * row + b
            flat[tap * channels : (tap + 1) * channels, :] = whole[
                :, b * LANES : (b + 1) * LANES
            ].astype(BF)
    for r in range(4):
        out = out_at(r)
        for p in range(4):
            chunk = p * 4 + r
            out[p] = flat[chunk * depth : (chunk + 1) * depth, :]


def trunk_grads(line, enc_pairs, dec_pairs, depth, cols, name):
    count = len(enc_pairs)
    pixels, channels = enc_pairs[0][0].shape
    size = pixels // 4
    enc_in = [a for pair in enc_pairs for a in pair]
    dec_in = [a for pair in dec_pairs for a in pair]

    def body(ids_ref, *refs):
        given, out, taps_ref, flat = refs[: 2 * count], *refs[2 * count :]
        for n in range(count):
            h_ref, g_ref = given[2 * n], given[2 * n + 1]
            grads_of_taps(
                h_ref[...],
                lambda i: g_ref[i * size : (i + 1) * size, :],
                taps_ref,
                flat,
                lambda r: out.at[r, n],
                cols,
                depth,
            )

    return section_call(
        body,
        [((4, count, 4, depth, LANES), BF)],
        line,
        enc_in,
        name,
        scratch=[
            pltpu.VMEM((pixels, TAPS * LANES), BF),
            pltpu.VMEM((TAPS * channels, LANES), BF),
        ],
        paired=enumerate(dec_in),
    )[0]


def dec_task_grads(line, dec_xs, q_cells, mask, att, cots, enc_grads, depth, cols):
    tasks_n, size, _ = q_cells[0].shape
    pixels, channels = 4 * size, att.shape[1]

    def body(ids_ref, *refs, parts):
        x_in, q_in, mask_ref, att_ref, cot_in = refs[:4], refs[4:8], refs[8], refs[9], refs[10:14]
        u_ref, out, taps_ref, flat, x_ref, s_ref, pairs_ref = refs[14:]
        for j in range(4):
            x_ref[:, span(ids_ref[0] ^ j, LANES)] = x_in[j][...]
        for t in range(tasks_n):
            for i in range(4):
                image = ids_ref[0] ^ i
                rows = span(image, size)
                x_low = x_ref[rows, :]
                x = x_low.astype(F32)
                own = mask_ref[rows, :]
                for j in range(4):
                    kept = q_in[j][t, span(image, size // 4), :].astype(F32)
                    cells = spread_pairs(kept, pairs_ref, cols)
                    s_ref[:, span(ids_ref[0] ^ j, LANES)] = cells.astype(BF) * own
                mixture = (x + s_ref[...].astype(F32)).astype(BF)
                _, _, gate = attend(x_low, mixture, att_ref[t], att_ref[tasks_n + t])
                u_ref[t, i * size : (i + 1) * size, :] = (gate * x).astype(BF)
            parts.send(0, t)
            grads_of_taps(
                u_ref[t],
                lambda i: cot_in[i][t],
                taps_ref,
                flat,
                lambda r: out.at[r, t],
                cols,
                depth,
            )

    return section_call(
        body,
        [((tasks_n, pixels, channels), BF), ((4, tasks_n, 4, depth, LANES), BF)],
        line,
        list(dec_xs) + list(q_cells) + [mask, att] + list(cots),
        "dec_task_grads",
        scratch=[
            pltpu.VMEM((pixels, TAPS * LANES), BF),
            pltpu.VMEM((TAPS * channels, LANES), BF),
            pltpu.VMEM((pixels, channels), BF),
            pltpu.VMEM((size, channels), BF),
            pltpu.VMEM((size // 2, LANES), F32),
        ],
        only=1,
        other={1: enc_grads},
        split_out=(0,),
    )


def enc_tasks_reverse(line, labels, grad_pieces, fields, weights, mask, depth, cols):
    tasks_n, given_size, _ = grad_pieces[0].shape
    channels = weights.shape[1]
    size = 4 * given_size
    pixels = 4 * size

    def body(ids_ref, label_ref, *refs, parts):
        given, u_in, w_ref, mask_ref, outs = refs[:4], refs[4:8], refs[8], refs[9], refs[10:14]
        grads, pairs_ref, taps_ref, flat, whole = refs[14:]
        for j in range(4):
            outs[j][1] = jnp.zeros((size, channels), BF)
        for t in range(tasks_n):
            parts.need(8, t)
            for j in range(4):
                rows = slice(j * size, (j + 1) * size)
                cells = spread_pairs(given[j][t].astype(F32), pairs_ref, cols)
                grad = cells.astype(BF) * mask_ref[span(ids_ref[0] ^ j, size), :]
                taps_ref[rows, :] = spread_taps(grad.astype(F32), cols)
                device = ids_ref[0] ^ j

                @pl.when(label_at(label_ref, ids_ref, device, t) == 1)
                def _(t=t, j=j, rows=rows, device=device):
                    slot = slot_of(label_ref, ids_ref, device, t)
                    outs[j][slot] = dot_nt(taps_ref[rows, :], w_ref[t]).astype(BF)

                parts.need(4 + j, t)
                whole[rows, :] = u_in[j][t]
            grads_of_taps(whole[...], None, taps_ref, flat, lambda r: grads.at[r, t], cols, depth)

    return section_call(
        body,
        [((2, size, channels), BF)] * 4 + [((4, tasks_n, 4, depth, LANES), BF)],
        line,
        list(grad_pieces) + list(fields) + [weights, mask],
        "enc_tasks_back",
        scratch=[
            pltpu.VMEM((size // 2, LANES), F32),
            pltpu.VMEM((pixels, TAPS * LANES), BF),
            pltpu.VMEM((TAPS * channels, LANES), BF),
            pltpu.VMEM((pixels, channels), BF),
        ],
        only=0,
        split_in=range(4, 9),
        smem=[labels],
    )


def dec_task_layer(line, fields, weights, enc_feats, cols, name):
    tasks_n, channels, _ = weights.shape
    size = fields.shape[1] // 4

    def body(ids_ref, u_ref, w_ref, *outs, parts):
        for t in range(tasks_n):
            parts.need(1, t)
            parts.need(0, t)
            for j in range(4):
                value = dot(u_ref[t, j * size : (j + 1) * size, :], w_ref[t])
                outs[j][t] = fold_taps(value, cols).astype(BF)

    return section_call(
        body,
        [((tasks_n, size, LANES), BF)] * 4,
        line,
        [fields, weights],
        name,
        only=1,
        other=enumerate(enc_feats),
        split_in=(0, 1),
    )


def heads_reverse(line, labels, x_pieces, carried, mask, du_pieces, att, cols, name, only, other=None):
    size = x_pieces[0].shape[0] // 4
    channels = att.shape[1]
    tasks_n = att.shape[0] // 2
    carry = carried is not None

    def body(ids_ref, label_ref, *refs):
        x_in, rest = refs[:4], refs[4:]
        if carry:
            q_in, mask_ref, rest = rest[:4], rest[4], rest[5:]
        du_in, att_ref, rest = rest[:4], rest[4], rest[5:]
        outs, (x_ref, s_ref, ds_ref, da_ref, pairs_ref) = rest[:-5], rest[-5:]
        dx_ref, g_ref, grads = outs[0], outs[1], outs[2:6]
        for j in range(4):
            x_ref[:, span(ids_ref[0] ^ j, LANES)] = x_in[j][span(ids_ref[0], size), :]

        def task(t):
            x_low = x_ref[...]
            x = x_low.astype(F32)
            slot = slot_of(label_ref, ids_ref, ids_ref[0], t)
            if carry:
                own = mask_ref[span(ids_ref[0], size), :]
                for j in range(4):
                    kept = q_in[j][t, span(ids_ref[0], size // 4), :].astype(F32)
                    cells = spread_pairs(kept, pairs_ref, cols)
                    s_ref[:, span(ids_ref[0] ^ j, LANES)] = cells.astype(BF) * own
                mixture = (x + s_ref[...].astype(F32)).astype(BF)
            else:
                mixture = x_low
            inner, active, gate = attend(x, mixture, att_ref[t], att_ref[tasks_n + t])
            du = (
                (du_in[0][slot].astype(F32) + du_in[1][slot].astype(F32))
                + (du_in[2][slot].astype(F32) + du_in[3][slot].astype(F32))
            )
            gated = du * gate
            do = (gated * x * (1.0 - gate)).astype(BF)
            sig = jax.nn.sigmoid(inner)
            dk = (dot(do, att_ref[tasks_n + t]) * (sig * (1.0 + inner * (1.0 - sig)))).astype(BF)
            ds = dot_nt(dk, att_ref[t])
            dx_ref[t] = gated + ds
            if carry:
                ds_ref[...] = ds
                for j in range(4):
                    kept = ds_ref[:, span(ids_ref[0] ^ j, LANES)] * own.astype(F32)
                    outs[6 + j][t] = pool_pairs(kept, pairs_ref, cols).astype(BF)
            for row, value in ((t, dot_tn(mixture, dk)), (tasks_n + t, dot_tn(do, active))):
                da_ref[...] = value
                for j in range(4):
                    grads[j][row] = da_ref[span(ids_ref[0] ^ j, LANES), :].astype(BF)

        def no_task(t):
            dx_ref[t] = jnp.zeros((size, channels), F32)
            for j in range(4):
                if carry:
                    outs[6 + j][t] = jnp.zeros((size // 4, LANES), BF)
                grads[j][t] = jnp.zeros((LANES, LANES), BF)
                grads[j][tasks_n + t] = jnp.zeros((LANES, LANES), BF)

        for t in range(tasks_n):
            label = label_at(label_ref, ids_ref, ids_ref[0], t)
            pl.when(label == 1)(functools.partial(task, t))
            pl.when(label != 1)(functools.partial(no_task, t))
        row = 0
        g_ref[...] = jnp.zeros_like(g_ref)
        for a in range(tasks_n):
            for b in range(a, tasks_n):
                line_sum = jnp.sum(dx_ref[a] * dx_ref[b], axis=0, keepdims=True)
                folded = line_sum[:, :LANES]
                for part in range(1, channels // LANES):
                    folded = folded + line_sum[:, part * LANES : (part + 1) * LANES]
                g_ref[row : row + 1, :] = folded
                row += 1

    outs = [((tasks_n, size, channels), F32), ((8, LANES), F32)]
    outs += [((2 * tasks_n, LANES, LANES), BF)] * 4
    if carry:
        outs += [((tasks_n, size // 4, LANES), BF)] * 4
    return section_call(
        body,
        outs,
        line,
        list(x_pieces) + (list(carried) + [mask] if carry else []) + list(du_pieces) + [att],
        name,
        scratch=[
            pltpu.VMEM((size, channels), BF),
            pltpu.VMEM((size, channels), BF),
            pltpu.VMEM((size, channels), F32),
            pltpu.VMEM((channels, LANES), F32),
            pltpu.VMEM((size // 2, LANES), F32),
        ],
        only=only,
        other=other,
        smem=[labels],
    )


def nash_values(lines, tasks_n):
    def full(row):
        return jnp.broadcast_to(jnp.sum(lines[row : row + 1, :], axis=1, keepdims=True), (8, LANES))

    gram = [[None] * tasks_n for _ in range(tasks_n)]
    row = 0
    for a in range(tasks_n):
        for b in range(a, tasks_n):
            gram[a][b] = gram[b][a] = full(row)
            row += 1
    trace_mean = (gram[0][0] + gram[1][1] + gram[2][2]) / 3.0 + 1e-06
    norm = [[gram[a][b] / trace_mean for b in range(3)] for a in range(3)]
    alpha = [lax.rsqrt(norm[a][a] + 1e-06) for a in range(3)]
    for _ in range(NASH_ITERS):
        right = [
            norm[a][0] * alpha[0] + norm[a][1] * alpha[1] + norm[a][2] * alpha[2] - 1.0 / alpha[a]
            for a in range(3)
        ]
        matrix = [
            [norm[a][b] + 1.0 / (alpha[a] * alpha[a]) if a == b else norm[a][b] for b in range(3)]
            for a in range(3)
        ]
        cof = [[None] * 3 for _ in range(3)]
        for a in range(3):
            for b in range(3):
                a1, a2, b1, b2 = (a + 1) % 3, (a + 2) % 3, (b + 1) % 3, (b + 2) % 3
                cof[a][b] = matrix[a1][b1] * matrix[a2][b2] - matrix[a1][b2] * matrix[a2][b1]
        determinant = (
            matrix[0][0] * cof[0][0] + matrix[0][1] * cof[0][1] + matrix[0][2] * cof[0][2]
        )
        update = [
            (cof[0][b] * right[0] + cof[1][b] * right[1] + cof[2][b] * right[2]) / determinant
            for b in range(3)
        ]
        alpha = [alpha[a] * jnp.exp(-0.5 * jnp.tanh(update[a] / alpha[a])) for a in range(3)]
    return alpha


def weigh(line, dx, w_or_lines, solve, name):
    tasks_n, size, channels = dx.shape

    def body(ids_ref, *refs):
        given, dx_ref, outs, total = refs[: len(w_or_lines)], refs[len(w_or_lines)], refs[-6:-1], refs[-1]
        if solve:
            lines = (given[0][0] + given[0][1]) + (given[0][2] + given[0][3])
            alpha = nash_values(lines, tasks_n)
            outs[0][...] = jnp.concatenate(
                [alpha[t][:1] for t in range(3)] + [jnp.zeros((5, LANES), F32)], axis=0
            )
        else:
            outs[0][...] = given[0][...]
        acc = None
        for t in range(tasks_n):
            scale = jnp.tile(outs[0][t : t + 1, :], (1, channels // LANES))
            term = dx_ref[t] * scale
            acc = term if acc is None else acc + term
        total[...] = acc
        for j in range(4):
            outs[1 + j][...] = total[:, span(ids_ref[0] ^ j, LANES)].astype(BF)

    return kernel_call(
        body,
        [((8, LANES), F32)] + [((size, LANES), BF)] * 4,
        line,
        list(w_or_lines) + [dx],
        name,
        scratch=[pltpu.VMEM((size, channels), F32)],
    )


def trunk_reverse(
    line, pieces, by_image, cells, mask, normed, inverse, norms, layer, weight, cols, parts, other, name, only
):
    pixels = normed.shape[0]
    size = pixels // 4
    channels = weight.shape[1]
    takes, gives = cells is not None, "cells" in parts
    shapes = {"slices": (pixels, LANES), "images": (size, channels), "cells": (size, LANES)}

    def body(ids_ref, *refs):
        given, rest = refs[:4], refs[4:]
        if takes:
            cells_in, rest = rest[:4], rest[4:]
        if takes or gives:
            mask_ref, rest = rest[0], rest[1:]
        (n_ref, inv_ref, norm_ref, w_ref), rest = rest[:4], rest[4:]
        if other is not None:
            other_in, rest = rest[:4], rest[4:]
        outs, (acc_ref, back_ref, pairs_ref) = rest[:-3], rest[-3:]
        gain = norm_ref[layer : layer + 1, :]

        @pl.when(ids_ref[2] == only)
        def _():
            if by_image:
                for j in range(4):
                    acc_ref[span(ids_ref[0] ^ j, size), :] = given[j][...].astype(F32)
            else:
                acc_ref[...] = (given[0][...].astype(F32) + given[1][...].astype(F32)) + (
                    given[2][...].astype(F32) + given[3][...].astype(F32)
                )
            grad = acc_ref[...]
            if takes:
                start = (cells_in[0][...].astype(F32) + cells_in[1][...].astype(F32)) + (
                    cells_in[2][...].astype(F32) + cells_in[3][...].astype(F32)
                )
                start = start.astype(BF).astype(F32)
                grad = grad + spread_pairs(start, pairs_ref, cols) * mask_ref[...].astype(F32)
            normed_value = n_ref[...]
            preact = gain * normed_value + norm_ref[2 + layer : 3 + layer, :]
            sig = jax.nn.sigmoid(preact)
            dp = grad * (sig * (1.0 + preact * (1.0 - sig)))
            bias_total = jnp.sum(dp, axis=0, keepdims=True)
            gain_total = jnp.sum(dp * normed_value, axis=0, keepdims=True)
            outs[1][...] = jnp.concatenate(
                [gain_total, bias_total, jnp.zeros((6, LANES), F32)], axis=0
            )
            scale = inv_ref[0:1, :] * gain
            dv = scale * (dp - bias_total / pixels - normed_value * (gain_total / pixels))
            outs[0][...] = dv.astype(BF)
            acc_ref[...] = dv.astype(BF).astype(F32)
            for i in range(4):
                part = slice(i * size, (i + 1) * size)
                back_ref[part, :] = dot_nt(spread_taps(acc_ref[part, :], cols), w_ref[0])
            for at, kind in enumerate(parts):
                for j in range(4):
                    peer = ids_ref[0] ^ j
                    out = outs[2 + 4 * at + j]
                    if kind == "images":
                        out[...] = back_ref[span(peer, size), :].astype(BF)
                    elif kind == "slices":
                        out[...] = back_ref[:, span(peer, LANES)].astype(BF)
                    else:
                        kept = back_ref[:, span(peer, LANES)] * mask_ref[...].astype(F32)
                        out[...] = pool_pairs(kept, pairs_ref, cols).astype(BF)

        if other is not None:

            @pl.when(ids_ref[2] != only)
            def _():
                for j in range(4):
                    outs[2 + 4 * parts.index("images") + j][...] = other_in[j][...]

    outs = [((pixels, LANES), BF), ((8, LANES), F32)]
    for kind in parts:
        outs += [(shapes[kind], BF)] * 4
    extra = list(cells) if takes else []
    if takes or gives:
        extra.append(mask)
    return kernel_call(
        body,
        outs,
        line,
        list(pieces) + extra + [normed, inverse, norms, weight] + list(other or []),
        name,
        scratch=[
            pltpu.VMEM((pixels, LANES), F32),
            pltpu.VMEM((pixels, channels), F32),
            pltpu.VMEM((pixels // 2, LANES), F32),
        ],
    )


def plane_device(
    x_in,
    pool_index,
    task_mask,
    task_cot,
    trunk_conv,
    norm_gain,
    norm_bias,
    att_down,
    attention_up_weights,
    task_conv,
):
    micro_count, _, rows_n, cols, channels = x_in.shape
    tasks_n = task_cot.shape[0]
    strip = rows_n * cols
    size = strip * micro_count
    depth = trunk_conv.shape[2]
    part = att_down.shape[2]
    section = lax.axis_index("pipe")
    decoder = section == 1
    row_at = lax.axis_index("rows")
    line = Line(jnp.stack([lax.axis_index("dp"), row_at, section]).astype(jnp.int32))
    ENC, DEC, BOTH = (0,), (1,), (0, 1)

    norm_own = jnp.concatenate([norm_gain[0], norm_bias[0]], axis=0)
    own_lanes = jnp.arange(LANES) // part == row_at
    norm_own = jnp.where(own_lanes[None], jnp.tile(norm_own, (1, LANES // part)), 0).astype(BF)
    norm_own = jnp.pad(norm_own, ((0, 12), (0, 0)))
    att_own = jnp.concatenate(
        [att_down[0], jnp.swapaxes(attention_up_weights[0], 1, 2)], axis=0
    ).reshape(2 * tasks_n * part, LANES)

    trunk_cut = trade(cut_weights(line, [(trunk_conv[0], [0, 1])], "cut_trunk"), "dp", BOTH)

    labels = lax.all_gather(task_mask, "dp").reshape(-1)

    picked = pool_index[:, 0, :, None, :, None]
    place = jnp.arange(2)[:, None, None] * 2 + jnp.arange(2)[None, None, :]
    cells = (picked == place[None, None]).astype(BF)
    cells = jnp.broadcast_to(cells.reshape(micro_count, strip, 1), (micro_count, strip, LANES))
    strips = x_in.reshape(micro_count, strip, channels)

    def cut_input(ids_ref, x_ref, m_ref, *outs):
        for j in range(4):
            outs[j][:, :channels] = x_ref[ids_ref[1] ^ j]
            outs[j][:, channels:] = m_ref[ids_ref[1] ^ j]

    strips = kernel_call(
        cut_input, [((strip, channels + LANES), BF)] * 4, line, [strips, cells], "cut_input"
    )
    strips = trade(strips, "rows", BOTH)

    trunk_block = stack_weights(line, trunk_cut, [[0, 1]], [[norm_own, att_own]], "stack_trunk")[0]
    trunk_all = lax.all_gather(trunk_block, "rows")

    def place_input(ids_ref, a, b, c, e, o_ref):
        for j, piece in enumerate((a, b, c, e)):
            o_ref[span(ids_ref[1] ^ j, strip), :] = piece[...]

    x_image = kernel_call(
        place_input, [((size, channels + LANES), BF)], line, strips, "place_input"
    )[0]
    x_images = trade([x_image] * 4, "dp", ENC)
    task_cut = trade(
        cut_weights(line, [(task_conv[0], range(tasks_n))], "cut_tasks"), "dp", BOTH
    )
    anchor(line, x_images, "input_there")
    task_block = stack_weights(line, task_cut, [list(range(tasks_n))], [[]], "stack_tasks")[0]
    task_all = lax.all_gather(task_block, "rows")

    half = channels // 2

    def cut_cot(ids_ref, mask_ref, c_ref, *outs):
        for j in range(4):
            micro = ids_ref[1] ^ j
            for t in range(tasks_n):
                labelled = mask_ref[micro * tasks_n + t].astype(F32)
                value = c_ref[t, micro, :, span(ids_ref[2], half)].astype(F32)
                outs[j][t] = (value * labelled).astype(BF)

    cot_strips = kernel_call(
        cut_cot,
        [((tasks_n, strip, half), BF)] * 4,
        line,
        [task_cot.reshape(tasks_n, micro_count, strip, channels)],
        "cut_cotangents",
        smem=[task_mask.reshape(-1)],
    )
    cot_strips = trade(cot_strips, "rows", BOTH)

    def place_cot(ids_ref, _, a, b, c, e, o_ref):
        for j, piece in enumerate((a, b, c, e)):
            for t in range(tasks_n):
                o_ref[t, span(ids_ref[1] ^ j, strip), :] = piece[t]

    cot_half = kernel_call(
        place_cot, [((tasks_n, size, half), BF)], line, cot_strips, "place_cotangents", smem=[labels]
    )[0]
    cot_other = swap_sections([cot_half])[0]

    def slice_cot(ids_ref, own_ref, other_ref, *rest):
        outs, image = rest[:4], rest[4]
        image[:, :, :half] = other_ref[...]
        image[:, :, half:] = own_ref[...]
        for j in range(4):
            outs[j][...] = image[:, :, span(ids_ref[0] ^ j, LANES)]

    cots = kernel_call(
        slice_cot,
        [((tasks_n, size, LANES), BF)] * 4,
        line,
        [cot_half, cot_other],
        "slice_cotangents",
        scratch=[pltpu.VMEM((tasks_n, size, channels), BF)],
    )
    cots = trade(cots, "dp", BOTH)
    first_w, second_w, norms, att_rows = place_weights(
        line, trunk_all, 2, depth, "place_trunk", norm_own.shape[0], att_own.shape[0]
    )
    enc_h0, enc_n1, enc_i1, enc_h, mask = trunk_layer(
        line, x_images, first_w, norms, 0, cols, eps, "images", False, None, "enc_layer1", 0
    )
    enc_hs = trade([enc_h] * 4, "dp", ENC)
    dec_mask = swap_sections([mask])[0]
    att = place_attention(line, trade([att_rows] * 4, "dp", BOTH), 2 * tasks_n, part)
    enc_h1, enc_n2, enc_i2, enc_x, z = trunk_layer(
        line, enc_hs, second_w, norms, 1, cols, eps, "slices", True, mask, "enc_layer2", 0
    )
    z_pieces = swap_sections([z] * 4)
    enc_xs = trade([enc_x] * 4, "dp", ENC)

    dec_h0, dec_n1, dec_i1, dec_h = trunk_layer(
        line, z_pieces, first_w, norms, 0, cols, eps, "cells", False, dec_mask, "dec_layer1", 1
    )
    dec_hs = trade([dec_h] * 4, "dp", DEC)

    dec_h1, dec_n2, dec_i2, dec_x = trunk_layer(
        line, dec_hs, second_w, norms, 1, cols, eps, "slices", True, None, "dec_layer2", 1
    )
    dec_xs = trade([dec_x] * 4, "dp", BOTH)

    task_w = place_weights(line, task_all, tasks_n, depth, "place_tasks")[0]
    enc_us, enc_feats, kept, du = section_tasks(
        line, labels, enc_xs, att, task_w, mask, cots, cols
    )
    anchor(line, dec_xs, "decoder_there")
    dec_du = trade(du, "dp", DEC)
    q_cells = swap_sections([kept] * 4)

    dec_dx, lines, *rest = heads_reverse(
        line, labels, dec_xs, q_cells, dec_mask, dec_du, att, cols, "dec_heads", 1
    )
    dec_att, ds = rest[:4], rest[4:]
    ds = swap_sections(ds)
    lines = jnp.sum(lax.all_gather(lines, "dp"), axis=0)
    terms = lax.all_gather(lines, "rows")
    dec_w, *dh = weigh(line, dec_dx, [terms], True, "bargain")
    dh = trade(dh, "dp", BOTH)
    enc_w = swap_sections([dec_w])[0]
    nash_w = jnp.where(decoder, dec_w, enc_w)

    anchor(line, dh, "bargain_there")
    *du, enc_dw = enc_tasks_reverse(
        line, labels, ds, enc_us, task_w, mask, depth, cols
    )
    enc_du = trade(du, "dp", ENC)
    dec_dv2, dec_s2, *dh = trunk_reverse(
        line, dh, True, None, None, dec_n2, dec_i2, norms, 1, second_w, cols, ["slices"], None, "dec_back2", 1
    )
    dh = trade(dh, "dp", DEC)
    dec_u, task_dw = dec_task_grads(
        line, dec_xs, q_cells, dec_mask, att, cots, enc_dw, depth, cols
    )
    task_dw = lax.psum_scatter(task_dw, "rows", scatter_dimension=0, tiled=True)
    dec_dv1, dec_s1, *rest = trunk_reverse(
        line, dh, False, None, dec_mask, dec_n1, dec_i1, norms, 0, first_w, cols, ["cells", "images"], None, "dec_back1", 1
    )
    dec_start, dec_dz = swap_sections(rest[:4]), rest[4:]
    enc_dx, _, *att_parts = heads_reverse(
        line, labels, enc_xs, None, None, enc_du, att, cols, "enc_heads_back", 0, {k + 2: a for k, a in enumerate(dec_att)}
    )
    _, *dh = weigh(line, enc_dx, [enc_w], False, "enc_weigh")
    dh = trade(dh, "dp", BOTH)
    att_parts = trade(att_parts, "dp", BOTH)

    feats = dec_task_layer(line, dec_u, task_w, enc_feats, cols, "dec_tasks")
    feats = trade(feats, "dp", BOTH)
    enc_dv2, enc_s2, *dh = trunk_reverse(
        line, dh, True, dec_start, mask, enc_n2, enc_i2, norms, 1, second_w, cols, ["slices"], None, "enc_back2", 0
    )
    dh = trade(dh, "dp", ENC)

    enc_dv1, enc_s1, *dz = trunk_reverse(
        line, dh, False, None, None, enc_n1, enc_i1, norms, 0, first_w, cols, ["images"], dec_dz, "enc_back1", 0
    )
    dz = trade(dz, "dp", BOTH)
    trunk_dw = trunk_grads(
        line,
        [(enc_h0, enc_dv1), (enc_h1, enc_dv2)],
        [(dec_h0, dec_dv1), (dec_h1, dec_dv2)],
        depth,
        cols,
        "trunk_grads",
    )
    trunk_dw = lax.psum_scatter(trunk_dw, "rows", scatter_dimension=0, tiled=True)


    def cut_shares(sums, name):
        count = sums.shape[1]

        def cut(ids_ref, g_ref, *outs):
            for j in range(4):
                for n in range(count):
                    outs[j][n] = g_ref[0, n, ids_ref[0] ^ j]

        return kernel_call(cut, [((count, depth, LANES), BF)] * 4, line, [sums], name)

    def join(layers, scale, name):
        counts = [pieces[0].shape[0] for pieces in layers]

        def body(ids_ref, *refs):
            o_ref, at = refs[-1], 0
            for m, count in enumerate(counts):
                for n in range(count):
                    for j in range(4):
                        value = refs[4 * m + j][n].astype(F32)
                        if scale is not None:
                            value = value * refs[4 * len(counts)][n : n + 1, :]
                        o_ref[at, :, span(ids_ref[0] ^ j, LANES)] = value
                    at += 1

        return kernel_call(
            body,
            [((sum(counts), depth, channels), F32)],
            line,
            [piece for pieces in layers for piece in pieces] + ([] if scale is None else [scale]),
            name,
        )[0]

    def cut_att(ids_ref, a, b, c, e, *rest):
        outs, total = rest[:4], rest[4]
        total[...] = (a[...].astype(F32) + b[...].astype(F32)) + (
            c[...].astype(F32) + e[...].astype(F32)
        )
        for j in range(4):
            outs[j][...] = total[:, span(ids_ref[1] ^ j, part), :].astype(BF)

    att_parts = kernel_call(
        cut_att,
        [((2 * tasks_n, part, LANES), BF)] * 4,
        line,
        att_parts,
        "cut_attention",
        scratch=[pltpu.VMEM((2 * tasks_n, LANES, LANES), F32)],
    )
    att_parts = trade(att_parts, "rows", BOTH)

    def cut_feats(ids_ref, a, b, c, e, *rest):
        outs, image = rest[:4], rest[4]
        for j, piece in enumerate((a, b, c, e)):
            image[:, :, span(ids_ref[0] ^ j, LANES)] = piece[...]
        for j in range(4):
            outs[j][...] = image[:, span(ids_ref[1] ^ j, strip), :]

    feats = kernel_call(
        cut_feats,
        [((tasks_n, strip, channels), BF)] * 4,
        line,
        feats,
        "cut_features",
        scratch=[pltpu.VMEM((tasks_n, size, channels), BF)],
    )
    feats = trade(feats, "rows", BOTH)

    sums = jnp.where(
        decoder, jnp.concatenate([dec_s1, dec_s2]), jnp.concatenate([enc_s1, enc_s2])
    )
    sums = trade([sums] * 4, "rows", BOTH)
    sums = (sums[0] + sums[1]) + (sums[2] + sums[3])
    sums = lax.dynamic_slice_in_dim(sums, row_at * part, part, axis=1)
    gain_out = jnp.stack([sums[0], sums[8]])
    bias_out = jnp.stack([sums[1], sums[9]])

    def cut_start(ids_ref, a, b, c, e, *rest):
        outs, image = rest[:4], rest[4]
        image[...] = (a[...].astype(F32) + b[...].astype(F32)) + (
            c[...].astype(F32) + e[...].astype(F32)
        )
        for j in range(4):
            outs[j][...] = image[span(ids_ref[1] ^ j, strip), :].astype(BF)

    starts = kernel_call(
        cut_start,
        [((strip, channels), BF)] * 4,
        line,
        dz,
        "cut_start",
        scratch=[pltpu.VMEM((size, channels), F32)],
    )
    starts = trade(starts, "rows", BOTH)

    task_parts = trade(cut_shares(task_dw, "share_tasks"), "dp", BOTH)
    def place_feats(ids_ref, a, b, c, e, o_ref):
        for j, piece in enumerate((a, b, c, e)):
            for t in range(tasks_n):
                o_ref[t, ids_ref[1] ^ j] = piece[t]

    feats_out = kernel_call(
        place_feats, [((tasks_n, micro_count, strip, channels), BF)], line, feats, "place_features"
    )[0]

    def join_att(ids_ref, a, b, c, e, w_ref, o_ref):
        total = (a[...].astype(F32) + b[...].astype(F32)) + (
            c[...].astype(F32) + e[...].astype(F32)
        )
        for t in range(2 * tasks_n):
            at = t % tasks_n
            o_ref[t] = total[t] * w_ref[at : at + 1, :]

    att_out = kernel_call(
        join_att,
        [((2 * tasks_n, part, LANES), F32)],
        line,
        att_parts + [nash_w],
        "join_attention",
    )[0]

    def place_start(ids_ref, a, b, c, e, o_ref):
        for j, piece in enumerate((a, b, c, e)):
            o_ref[ids_ref[1] ^ j] = piece[...].astype(F32)

    start_out = kernel_call(
        place_start, [((micro_count, strip, channels), F32)], line, starts, "place_start"
    )[0]
    task_out = join([task_parts], nash_w, "join_tasks")
    trunk_parts = trade(cut_shares(trunk_dw, "share_trunk"), "dp", BOTH)
    trunk_out = join([trunk_parts], None, "join_trunk")

    return (
        feats_out.reshape(1, tasks_n, micro_count, 1, rows_n, cols, channels),
        start_out.reshape(1, micro_count, 1, rows_n, cols, channels),
        trunk_out[None],
        gain_out[None],
        bias_out[None],
        att_out[:tasks_n][None],
        jnp.swapaxes(att_out[tasks_n:], 1, 2)[None],
        task_out[None],
        nash_w[:3, 0],
    )


def by_planes(x_in, task_cot):
    peers, planes = lax.axis_size("dp"), lax.axis_size("rows")
    micro, samples, _, _, channels = x_in.shape
    return (
        peers == 4
        and planes == 4
        and micro == planes
        and samples == 1
        and channels == peers * LANES
        and task_cot.shape[0] == 3
    )


def section_device(*arrays):
    if by_planes(arrays[0], arrays[3]):
        return plane_device(*arrays)
    return on_device(*arrays)


def solution(mesh):
    in_specs = (
        P(None, "dp", "rows", None, None),
        P(None, "dp", "rows", None),
        P(None, "dp", None),
        P(None, None, "dp", "rows", None, None),
        P("pipe", None, ("dp", "rows"), None),
        P("pipe", None, ("dp", "rows")),
        P("pipe", None, ("dp", "rows")),
        P("pipe", None, ("dp", "rows"), None),
        P("pipe", None, None, ("dp", "rows")),
        P("pipe", None, ("dp", "rows"), None),
    )
    out_specs = (
        P("pipe", None, None, "dp", "rows", None, None),
        P("pipe", None, "dp", "rows", None, None),
        P("pipe", None, ("dp", "rows"), None),
        P("pipe", None, ("dp", "rows")),
        P("pipe", None, ("dp", "rows")),
        P("pipe", None, ("dp", "rows"), None),
        P("pipe", None, None, ("dp", "rows")),
        P("pipe", None, ("dp", "rows"), None),
        P(),
    )
    return jax.shard_map(
        section_device, mesh=mesh, in_specs=in_specs, out_specs=out_specs, check_vma=False
    )
```

```python
import functools

import jax
import jax.numpy as jnp
from jax import lax
from jax.experimental import pallas as pl
from jax.experimental.pallas import tpu as pltpu
from jax.sharding import PartitionSpec as P

NASH_ITERS = 3


eps = 1e-05


def extended_2(array, sides, width):
    for axis, dim in sides:
        peers, length = (lax.axis_size(axis), array.shape[dim])
        up = [(i, (i + 1) % peers) for i in range(peers - 1)]
        down = [(j, i) for i, j in up]
        last = lax.slice_in_dim(array, length - width, length, axis=dim)
        first = lax.slice_in_dim(array, 0, width, axis=dim)
        before = lax.ppermute(last, axis, up)
        after = lax.ppermute(first, axis, down)
        array = jnp.concatenate([before, array, after], axis=dim)
    return array


def from_behind(array, axis, by):
    peers = lax.axis_size(axis)
    pairs = [(i, i + by) for i in range(peers) if 0 <= i + by < peers]
    return lax.ppermute(array, axis, pairs)


def silu_slope(preact):
    sigmoid_val = jax.nn.sigmoid(preact)
    return sigmoid_val * (1.0 + preact * (1.0 - sigmoid_val))


def choose_side(condition, when_true, when_false):

    def either(true_leaf, false_leaf):
        return jnp.where(condition, true_leaf, false_leaf)

    return jax.tree.map(either, when_true, when_false)


def pool_cells(field, positions):
    leading = field.shape[:-4]
    samples, rows_n, cols_n, channels = field.shape[-4:]
    blocks = field.astype(jnp.float32).reshape(
        leading + (samples, rows_n // 2, 2, cols_n // 2, 2, channels)
    )
    blocks = jnp.moveaxis(blocks, -4, -3).reshape(
        leading + (samples, rows_n // 2, cols_n // 2, 4, channels)
    )
    return jnp.sum(blocks * positions[..., None], axis=-2)


def unpool_cells(small, positions):
    leading = small.shape[:-4]
    samples, rows_h, cols_h, channels = small.shape[-4:]
    blocks = small.astype(jnp.float32)[..., None, :] * positions[..., None]
    blocks = blocks.reshape(leading + (samples, rows_h, cols_h, 2, 2, channels))
    blocks = jnp.moveaxis(blocks, -3, -4)
    return blocks.reshape(leading + (samples, 2 * rows_h, 2 * cols_h, channels))


def gather_taps(padded, rows_n, cols_n):
    stencil = [
        padded[:, :, offset // 3 : offset // 3 + rows_n, offset % 3 : offset % 3 + cols_n, :]
        for offset in range(9)
    ]
    return jnp.concatenate(stencil, axis=-1)


def conv_forward(field, weight):
    extended = extended_2(field, (("rows", 2),), 1)
    padded = jnp.pad(extended, ((0, 0), (0, 0), (0, 0), (1, 1), (0, 0)))
    stencil = gather_taps(padded, field.shape[2], field.shape[3])
    conv_out = jnp.einsum("ksrwq,kqd->ksrwd", stencil, weight, preferred_element_type=jnp.float32)
    return (conv_out, padded)


def conv_backward(padded, grad_out, weight, wanted):
    rows_n, cols_n = (grad_out.shape[2], grad_out.shape[3])
    extended = extended_2(grad_out, (("rows", 2),), 1)
    beside_all = jnp.pad(extended, ((0, 0), (0, 0), (0, 0), (1, 1), (0, 0)))
    flipped = jnp.stack(
        [
            beside_all[
                :,
                :,
                2 - offset // 3 : 2 - offset // 3 + rows_n,
                2 - offset % 3 : 2 - offset % 3 + cols_n,
                :,
            ]
            for offset in range(9)
        ],
        axis=-2,
    )
    kernel = weight.reshape(weight.shape[0], 9, weight.shape[2], weight.shape[2])
    grad_in = jnp.einsum("ksrwtd,ktcd->ksrwc", flipped, kernel, preferred_element_type=jnp.float32)
    weight_grad = None
    if wanted:
        weight_grad = jnp.einsum(
            "ksrwq,ksrwd->kqd",
            gather_taps(padded, rows_n, cols_n),
            grad_out,
            preferred_element_type=jnp.float32,
        )
    return (grad_in, weight_grad)


def norm_moments(conv_out, pixel_count):
    center = lax.psum(jnp.sum(conv_out, axis=(0, 1, 2, 3)), ("dp", "rows")) / pixel_count
    spread = (
        lax.psum(jnp.sum(jnp.square(conv_out - center), axis=(0, 1, 2, 3)), ("dp", "rows"))
        / pixel_count
    )
    return (center, lax.rsqrt(spread + eps))


def section_forward(section_input, carried, positions, params, stats, pixel_count):
    trunk_maps, gain_rows, bias_rows, down_maps, upward_maps, task_maps = params
    hidden = section_input[None]
    layers = []
    moments = []
    for section_layer in range(2):
        conv_out, padded = conv_forward(hidden, trunk_maps[section_layer][None])
        if stats is None:
            center, inverse_std = norm_moments(conv_out, pixel_count)
        else:
            center, inverse_std = stats[section_layer]
        normed = (conv_out - center) * inverse_std
        preact = gain_rows[section_layer] * normed + bias_rows[section_layer]
        layers.append((padded, normed, preact))
        moments.append((center, inverse_std))
        hidden = jax.nn.silu(preact).astype(jnp.bfloat16)
    mixture = (hidden.astype(jnp.float32) + carried.astype(jnp.float32)).astype(jnp.bfloat16)
    inner_act = jnp.einsum(
        "tsrwc,tca->tsrwa", mixture, down_maps, preferred_element_type=jnp.float32
    )
    active_mask_flag = jax.nn.silu(inner_act).astype(jnp.bfloat16)
    class_logits = jnp.einsum(
        "zfhpv,zvm->zfhpm", active_mask_flag, upward_maps, preferred_element_type=jnp.float32
    )
    gating = jax.nn.sigmoid(class_logits)
    product = (gating * hidden.astype(jnp.float32)).astype(jnp.bfloat16)
    features, padded_task = conv_forward(product, task_maps)
    return {
        "layers": layers,
        "moments": moments,
        "shared": hidden,
        "mixture": mixture,
        "inner_act": inner_act,
        "active": active_mask_flag,
        "gating": gating,
        "padded_task": padded_task,
        "features": features,
        "section_input": section_input,
        "carried": carried,
        "positions": positions,
    }


def heads_backward(saved_record, grad_feats, params, wanted):
    down_maps, upward_maps, task_maps = (params[3], params[4], params[5])
    task_back, task_slope = conv_backward(
        saved_record["padded_task"], grad_feats, task_maps, wanted
    )
    shared = saved_record["shared"].astype(jnp.float32)
    gating = saved_record["gating"]
    logits_gradient = (task_back * shared * gating * (1.0 - gating)).astype(jnp.bfloat16)
    grad_active = jnp.einsum(
        "qubef,qxf->qubex", logits_gradient, upward_maps, preferred_element_type=jnp.float32
    )
    grad_inner = (grad_active * silu_slope(saved_record["inner_act"])).astype(jnp.bfloat16)
    grad_mixture = jnp.einsum(
        "tsrwa,tca->tsrwc", grad_inner, down_maps, preferred_element_type=jnp.float32
    )
    through = task_back * gating + grad_mixture
    slopes = None
    if wanted:
        slope_up = jnp.einsum(
            "munfg,munfq->mgq",
            saved_record["active"],
            logits_gradient,
            preferred_element_type=jnp.float32,
        )
        slope_down = jnp.einsum(
            "tsrwc,tsrwa->tca",
            saved_record["mixture"],
            grad_inner,
            preferred_element_type=jnp.float32,
        )
        slopes = (slope_down, slope_up, task_slope)
    return (through, grad_mixture, slopes)


def trunk_backward(saved_record, grad_shared, params, pixel_count):
    trunk_maps, gain_rows = (params[0], params[1])
    grad_hidden = grad_shared
    conv_grads = [None, None]
    gain_grads = [None, None]
    bias_grads = [None, None]
    for section_layer in (1, 0):
        padded, normed, preact = saved_record["layers"][section_layer]
        inverse_std = saved_record["moments"][section_layer][1]
        grad_pre = grad_hidden * silu_slope(preact)
        bias_part = jnp.sum(grad_pre, axis=(0, 1, 2, 3))
        gain_part = jnp.sum(grad_pre * normed, axis=(0, 1, 2, 3))
        bias_total, gain_total = lax.psum((bias_part, gain_part), ("dp", "rows"))
        grad_conv = (
            inverse_std
            * gain_rows[section_layer]
            * (grad_pre - bias_total / pixel_count - normed * gain_total / pixel_count)
        )
        grad_hidden, weight_grad = conv_backward(
            padded, grad_conv.astype(jnp.bfloat16), trunk_maps[section_layer][None], True
        )
        conv_grads[section_layer] = weight_grad[0]
        gain_grads[section_layer] = gain_part
        bias_grads[section_layer] = bias_part
    return (grad_hidden, jnp.stack(conv_grads), jnp.stack(gain_grads), jnp.stack(bias_grads))


def solve_small(matrix, right_side):
    cofactor = [
        [
            matrix[1, 1] * matrix[2, 2] - matrix[1, 2] * matrix[2, 1],
            matrix[1, 2] * matrix[2, 0] - matrix[1, 0] * matrix[2, 2],
            matrix[1, 0] * matrix[2, 1] - matrix[1, 1] * matrix[2, 0],
        ],
        [
            matrix[0, 2] * matrix[2, 1] - matrix[0, 1] * matrix[2, 2],
            matrix[0, 0] * matrix[2, 2] - matrix[0, 2] * matrix[2, 0],
            matrix[0, 1] * matrix[2, 0] - matrix[0, 0] * matrix[2, 1],
        ],
        [
            matrix[0, 1] * matrix[1, 2] - matrix[0, 2] * matrix[1, 1],
            matrix[0, 2] * matrix[1, 0] - matrix[0, 0] * matrix[1, 2],
            matrix[0, 0] * matrix[1, 1] - matrix[0, 1] * matrix[1, 0],
        ],
    ]
    determinant = (
        matrix[0, 0] * cofactor[0][0]
        + matrix[0, 1] * cofactor[0][1]
        + matrix[0, 2] * cofactor[0][2]
    )
    answer = [
        (
            cofactor[0][col_index] * right_side[0]
            + cofactor[1][col_index] * right_side[1]
            + cofactor[2][col_index] * right_side[2]
        )
        / determinant
        for col_index in range(3)
    ]
    return jnp.stack(answer)


def nash_solve(gram_sum):
    trace_mean = (gram_sum[0, 0] + gram_sum[1, 1] + gram_sum[2, 2]) / 3.0 + 1e-06
    normalized = gram_sum / trace_mean
    diagonal = jnp.stack([normalized[0, 0], normalized[1, 1], normalized[2, 2]])
    nash_alpha = lax.rsqrt(diagonal + 1e-06)
    for sweep_index in range(NASH_ITERS):
        residual = jnp.sum(normalized * nash_alpha[None, :], axis=1) - 1.0 / nash_alpha
        curvature = normalized + jnp.diag(1.0 / (nash_alpha * nash_alpha))
        update = solve_small(curvature, residual)
        nash_alpha = nash_alpha * jnp.exp(-0.5 * jnp.tanh(update / nash_alpha))
    return nash_alpha


def on_device(
    x_in,
    pool_index,
    task_mask,
    task_cot,
    trunk_conv,
    norm_gain,
    norm_bias,
    att_down,
    attention_up_weights,
    task_conv,
):
    micro_count = x_in.shape[0]
    tasks_n = task_cot.shape[0]
    decoder_side = lax.axis_index("pipe") == 1
    pixel_count = (
        x_in.shape[1] * x_in.shape[2] * x_in.shape[3] * lax.axis_size("dp") * lax.axis_size("rows")
    )
    pieces = (
        lax.all_gather(trunk_conv, ("dp", "rows"), axis=2, tiled=True),
        lax.all_gather(norm_gain, ("dp", "rows"), axis=2, tiled=True),
        lax.all_gather(norm_bias, ("dp", "rows"), axis=2, tiled=True),
        lax.all_gather(att_down, ("dp", "rows"), axis=2, tiled=True),
        lax.all_gather(attention_up_weights, ("dp", "rows"), axis=3, tiled=True),
        lax.all_gather(task_conv, ("dp", "rows"), axis=2, tiled=True),
    )
    params = (
        pieces[0][0],
        pieces[1][0].astype(jnp.float32),
        pieces[2][0].astype(jnp.float32),
        pieces[3][0],
        pieces[4][0],
        pieces[5][0],
    )
    onehot = (pool_index[..., None] == jnp.arange(4, dtype=jnp.int32)).astype(jnp.float32)
    mask_weights = jnp.transpose(task_mask, (0, 2, 1)).astype(jnp.float32)
    no_carry = jnp.zeros((tasks_n,) + x_in.shape[1:], jnp.bfloat16)
    incoming = jnp.zeros(
        (tasks_n + 1, x_in.shape[1], x_in.shape[2] // 2, x_in.shape[3] // 2, x_in.shape[4]),
        jnp.bfloat16,
    )
    records = []
    for period in range(micro_count + 1):
        enc_index = min(period, micro_count - 1)
        dec_index = max(period - 1, 0)
        positions = jnp.where(decoder_side, onehot[dec_index], onehot[enc_index])
        section_input = jnp.where(
            decoder_side, unpool_cells(incoming[0], positions).astype(jnp.bfloat16), x_in[enc_index]
        )
        carried = jnp.where(
            decoder_side, unpool_cells(incoming[1:], positions).astype(jnp.bfloat16), no_carry
        )
        saved_record = section_forward(section_input, carried, positions, params, None, pixel_count)
        records.append(saved_record)
        if period < micro_count:
            outgoing = jnp.concatenate(
                [
                    pool_cells(saved_record["shared"], positions),
                    pool_cells(saved_record["features"].astype(jnp.bfloat16), positions),
                ],
                axis=0,
            )
            incoming = from_behind(outgoing.astype(jnp.bfloat16), "pipe", 1)
    kept_records = []
    gram_sum = jnp.zeros((tasks_n, tasks_n), jnp.float32)
    for micro_index in range(micro_count):
        source_input = choose_side(decoder_side, records[micro_index + 1], records[micro_index])
        chosen = section_forward(
            source_input["section_input"],
            source_input["carried"],
            source_input["positions"],
            params,
            source_input["moments"],
            pixel_count,
        )
        kept_records.append(chosen)
        plain_cot = task_cot[:, micro_index] * mask_weights[micro_index][:, :, None, None, None]
        through, unused_mixture, unused_slopes = heads_backward(
            chosen, plain_cot.astype(jnp.bfloat16), params, False
        )
        flattened = through.reshape(tasks_n, -1)
        partial_gram = jnp.dot(flattened, flattened.T, precision=lax.Precision.HIGHEST)
        gram_sum = gram_sum + jnp.where(decoder_side, partial_gram, 0.0)
    gram_sum = lax.psum(gram_sum, ("pipe", "dp", "rows"))
    nash_alpha = nash_solve(gram_sum)
    returning = jnp.zeros_like(incoming)
    start_grads = []
    trunk_sum, gain_sum, bias_sum = (0.0, 0.0, 0.0)
    down_sum, up_sum, task_sum = (0.0, 0.0, 0.0)
    for period in range(micro_count + 1):
        dec_index = max(micro_count - 1 - period, 0)
        enc_index = min(micro_count - period, micro_count - 1)
        active_flag = 1.0 if period < micro_count else 0.0
        chosen = choose_side(decoder_side, kept_records[dec_index], kept_records[enc_index])
        positions = chosen["positions"]
        weighted = (
            nash_alpha[:, None, None, None, None]
            * mask_weights[dec_index][:, :, None, None, None]
            * task_cot[:, dec_index].astype(jnp.float32)
            * active_flag
        )
        grad_feats = jnp.where(
            decoder_side, weighted, unpool_cells(returning[1:], positions)
        ).astype(jnp.bfloat16)
        through, grad_mixture, slopes = heads_backward(chosen, grad_feats, params, True)
        down_sum = down_sum + slopes[0]
        up_sum = up_sum + slopes[1]
        task_sum = task_sum + slopes[2]
        pooled_back = jnp.where(decoder_side, 0.0, unpool_cells(returning[0:1], positions))
        grad_shared = jnp.sum(through, axis=0, keepdims=True) + pooled_back
        grad_start, conv_grads, gain_grads, bias_grads = trunk_backward(
            chosen, grad_shared, params, pixel_count
        )
        start_grads.append(grad_start[0])
        trunk_sum = trunk_sum + conv_grads
        gain_sum = gain_sum + gain_grads
        bias_sum = bias_sum + bias_grads
        if period < micro_count:
            outgoing = jnp.concatenate(
                [pool_cells(grad_start, positions), pool_cells(grad_mixture, positions)], axis=0
            )
            returning = from_behind(outgoing.astype(jnp.bfloat16), "pipe", -1)
    features_out = jnp.stack(
        [
            jnp.where(
                decoder_side, records[micro_index + 1]["features"], records[micro_index]["features"]
            )
            for micro_index in range(micro_count)
        ],
        axis=1,
    ).astype(jnp.bfloat16)
    grads_out = jnp.stack(
        [
            jnp.where(
                decoder_side,
                start_grads[micro_count - 1 - micro_index],
                start_grads[micro_count - micro_index],
            )
            for micro_index in range(micro_count)
        ],
        axis=0,
    )
    shares = (
        lax.psum_scatter(trunk_sum[None], ("dp", "rows"), scatter_dimension=2, tiled=True),
        lax.psum_scatter(gain_sum[None], ("dp", "rows"), scatter_dimension=2, tiled=True),
        lax.psum_scatter(bias_sum[None], ("dp", "rows"), scatter_dimension=2, tiled=True),
        lax.psum_scatter(down_sum[None], ("dp", "rows"), scatter_dimension=2, tiled=True),
        lax.psum_scatter(up_sum[None], ("dp", "rows"), scatter_dimension=3, tiled=True),
        lax.psum_scatter(task_sum[None], ("dp", "rows"), scatter_dimension=2, tiled=True),
    )
    return (
        features_out[None],
        grads_out[None],
        shares[0],
        shares[1],
        shares[2],
        shares[3],
        shares[4],
        shares[5],
        nash_alpha,
    )


BF = jnp.bfloat16
F32 = jnp.float32
LANES = 128
TAPS = 9
VMEM_BYTES = 56 * 1024 * 1024


class Line:
    def __init__(self, ids):
        self.ids = ids
        self.last = None


def on_section(body, only):
    if only is None:
        return body

    def gated(ids_ref, *refs):
        @pl.when(ids_ref[2] == only)
        def _():
            body(ids_ref, *refs)

    return gated


def unread(body, count, first):
    def whole(*refs):
        body(*refs[:first], *refs[first + count :])

    return whole


LIGHT = pl.CostEstimate(flops=4_000_000_000, bytes_accessed=1, transcendentals=0)


def kernel_call(body, outs, line, vmem, name, scratch=(), only=None, smem=(), after=()):
    extra = list(after) + ([] if line.last is None else [line.last])
    first = 1 + len(smem) + len(vmem)
    results = pl.pallas_call(
        unread(on_section(body, only), len(extra), first),
        out_shape=[jax.ShapeDtypeStruct(shape, dtype) for shape, dtype in outs],
        in_specs=[pl.BlockSpec(memory_space=pltpu.SMEM)] * (1 + len(smem))
        + [pl.BlockSpec(memory_space=pltpu.VMEM)] * len(vmem)
        + [pl.BlockSpec(memory_space=pl.ANY)] * len(extra),
        out_specs=[pl.BlockSpec(memory_space=pltpu.VMEM)] * len(outs),
        scratch_shapes=list(scratch),
        compiler_params=pltpu.CompilerParams(vmem_limit_bytes=VMEM_BYTES),
        cost_estimate=LIGHT,
        name=name,
    )(line.ids, *smem, *vmem, *extra)
    line.last = results[-1]
    return results


def stepped_call(body, outs, line, vmem, name, scratch=(), only=None, fixed=()):
    extra = [] if line.last is None else [line.last]
    steps = outs[0][0][0]

    def block(shape):
        rest = len(shape) - 1
        return pl.BlockSpec(
            (1,) + tuple(shape[1:]),
            lambda t, ids: (t if only is None else jnp.where(ids[2] == only, t, 0),) + (0,) * rest,
        )

    def same(shape):
        return pl.BlockSpec(shape, lambda t, ids: (0,) * len(shape))

    results = pl.pallas_call(
        unread(on_section(body, only), len(extra), 1 + len(vmem)),
        grid_spec=pltpu.PrefetchScalarGridSpec(
            num_scalar_prefetch=1,
            grid=(steps,),
            in_specs=[same(a.shape) if k in fixed else block(a.shape) for k, a in enumerate(vmem)]
            + [pl.BlockSpec(memory_space=pl.ANY)] * len(extra),
            out_specs=[block(shape) for shape, _ in outs],
            scratch_shapes=list(scratch),
        ),
        out_shape=[jax.ShapeDtypeStruct(shape, dtype) for shape, dtype in outs],
        compiler_params=pltpu.CompilerParams(vmem_limit_bytes=VMEM_BYTES),
        cost_estimate=LIGHT,
        name=name,
    )(line.ids, *vmem, *extra)
    line.last = results[-1]
    return results


class Parts:
    def __init__(self, given, held, given_sems, results, kept, result_sems):
        self.given = [(a, b, given_sems, k) for k, (a, b) in enumerate(zip(given, held))]
        self.results = [(b, a, result_sems, k) for k, (a, b) in enumerate(zip(results, kept))]

    @staticmethod
    def copy(pair, p):
        source, target, sems, k = pair
        if p is None:
            return pltpu.make_async_copy(source, target, sems.at[k, 0])
        return pltpu.make_async_copy(source.at[p], target.at[p], sems.at[k, p])

    def need(self, k, p=None):
        self.copy(self.given[k], p).wait()

    def send(self, k, p=None):
        self.copy(self.results[k], p).start()


def section_call(
    body, outs, line, vmem, name, scratch=(), only=None, other=None, paired=(), split_in=(), split_out=(), smem=()
):
    other, paired = dict(other or {}), dict(paired)
    n_in, n_out = len(vmem), len(outs)
    passed, swapped = list(other.values()), list(paired.values())
    extra = [] if line.last is None else [line.last]

    def whole(*refs):
        scalars, refs = refs[: 1 + len(smem)], refs[1 + len(smem) :]
        ids_ref = scalars[0]
        given, refs = refs[:n_in], refs[n_in:]
        passed_refs, refs = refs[: len(passed)], refs[len(passed) :]
        swapped_refs, refs = refs[: len(swapped)], refs[len(swapped) + len(extra) :]
        results, refs = refs[:n_out], refs[n_out:]
        held, refs = refs[:n_in], refs[n_in:]
        kept, refs = refs[:n_out], refs[n_out:]
        given_sems, result_sems, refs = refs[0], refs[1], refs[2:]

        def run(sources):
            parts = Parts(sources, held, given_sems, results, kept, result_sems)
            for k in range(n_in):
                if k not in split_in:
                    parts.copy(parts.given[k], None).start()
            for p in range(3):
                for k in split_in:
                    parts.copy(parts.given[k], p).start()
            for k in range(n_in):
                if k not in split_in:
                    parts.need(k)
            if split_in or split_out:
                body(*scalars, *held, *kept, *refs, parts=parts)
            else:
                body(*scalars, *held, *kept, *refs)
            for k in range(n_out):
                if k not in split_out:
                    parts.send(k)
            for k in range(n_out):
                if k not in split_out:
                    parts.copy(parts.results[k], None).wait()
            for p in range(3):
                for k in split_out:
                    parts.copy(parts.results[k], p).wait()

        def hand_out():
            for source, target in ((passed_refs, kept), (kept, results)):
                copies = []
                for at, k in enumerate(other):
                    first = source[at] if source is passed_refs else source[k]
                    copies.append(pltpu.make_async_copy(first, target[k], result_sems.at[k, 0]))
                for copy in copies:
                    copy.start()
                for copy in copies:
                    copy.wait()

        if only is not None:
            pl.when(ids_ref[2] == only)(lambda: run(given))
            if passed:
                pl.when(ids_ref[2] != only)(hand_out)
        elif paired:
            mixed = list(given)
            for k, ref in zip(paired, swapped_refs):
                mixed[k] = ref
            pl.when(ids_ref[2] == 0)(lambda: run(given))
            pl.when(ids_ref[2] == 1)(lambda: run(mixed))
        else:
            run(given)

    results = pl.pallas_call(
        whole,
        out_shape=[jax.ShapeDtypeStruct(shape, dtype) for shape, dtype in outs],
        in_specs=[pl.BlockSpec(memory_space=pltpu.SMEM)] * (1 + len(smem))
        + [pl.BlockSpec(memory_space=pl.ANY)] * (n_in + len(passed) + len(swapped) + len(extra)),
        out_specs=[pl.BlockSpec(memory_space=pl.ANY)] * n_out,
        scratch_shapes=[pltpu.VMEM(a.shape, a.dtype) for a in vmem]
        + [pltpu.VMEM(shape, dtype) for shape, dtype in outs]
        + [pltpu.SemaphoreType.DMA((n_in, 3)), pltpu.SemaphoreType.DMA((n_out, 3))]
        + list(scratch),
        compiler_params=pltpu.CompilerParams(vmem_limit_bytes=VMEM_BYTES),
        cost_estimate=LIGHT,
        name=name,
    )(line.ids, *smem, *vmem, *passed, *swapped, *extra)
    line.last = results[-1]
    return results


def anchor(line, arrays, name):
    def body(*refs):
        refs[-1][...] = jnp.zeros((8, LANES), F32)

    line.last = pl.pallas_call(
        body,
        out_shape=jax.ShapeDtypeStruct((8, LANES), F32),
        in_specs=[pl.BlockSpec(memory_space=pl.ANY)] * (len(arrays) + 1),
        out_specs=pl.BlockSpec(memory_space=pltpu.VMEM),
        cost_estimate=LIGHT,
        name=name,
    )(*arrays, line.last)


def trade(pieces, axis, sections):
    count = lax.axis_size(axis)
    taken = [pieces[0]]
    for j in range(1, count):
        pairs = [(p * count + i, p * count + (i ^ j)) for p in sections for i in range(count)]
        taken.append(lax.ppermute(pieces[j], ("pipe", axis), pairs))
    return taken


def swap_sections(pieces):
    count = lax.axis_size("dp")
    return [
        lax.ppermute(
            pieces[j],
            ("pipe", "dp"),
            [(p * count + i, (1 - p) * count + (i ^ j)) for p in range(2) for i in range(count)],
        )
        for j in range(len(pieces))
    ]


def all_of(count, step):
    for i in range(count):
        step(i)


def each(count, step):
    def run(i, carry):
        step(i)
        return carry

    lax.fori_loop(0, count, run, 0)


def span(index, size):
    return pl.ds(pl.multiple_of(index * size, size), size)


def dot(a, b):
    return jnp.dot(a, b, preferred_element_type=F32)


def dot_nt(a, b):
    return lax.dot_general(a, b, (((1,), (1,)), ((), ())), preferred_element_type=F32)


def dot_tn(a, b):
    return lax.dot_general(a, b, (((0,), (0,)), ((), ())), preferred_element_type=F32)


def column_of(shape, cols):
    return lax.broadcasted_iota(jnp.int32, shape, 0) % cols


def fold_taps(taps, cols):
    size = taps.shape[0]
    blank = jnp.zeros((cols, LANES), F32)
    sums = []
    for b in range(3):
        first = taps[:, b * LANES : (b + 1) * LANES]
        second = taps[:, (3 + b) * LANES : (4 + b) * LANES]
        third = taps[:, (6 + b) * LANES : (7 + b) * LANES]
        sums.append(
            second
            + jnp.concatenate([blank, first[: size - cols]], axis=0)
            + jnp.concatenate([third[cols:], blank], axis=0)
        )
    column = column_of((size, LANES), cols)
    left = jnp.where(column == 0, 0.0, pltpu.roll(sums[0], 1, 0))
    right = jnp.where(column == cols - 1, 0.0, pltpu.roll(sums[2], size - 1, 0))
    return sums[1] + left + right


def spread_taps(grad, cols):
    size = grad.shape[0]
    column = column_of((size, LANES), cols)
    moved = [
        jnp.where(column == cols - 1, 0.0, pltpu.roll(grad, size - 1, 0)).astype(BF),
        grad.astype(BF),
        jnp.where(column == 0, 0.0, pltpu.roll(grad, 1, 0)).astype(BF),
    ]
    blank = jnp.zeros((cols, LANES), BF)
    above = [jnp.concatenate([m[cols:], blank], axis=0) for m in moved]
    below = [jnp.concatenate([blank, m[: size - cols]], axis=0) for m in moved]
    return jnp.concatenate(above + moved + below, axis=1)


def cut_weights(line, arrays, name):
    depth = arrays[0][0].shape[1]
    count = sum(len(layers) for _, layers in arrays)

    def body(ids_ref, *refs):
        given, outs = refs[: len(arrays)], refs[len(arrays) :]
        for j in range(4):
            cut = span(ids_ref[0] ^ j, LANES)
            row = 0
            for ref, (_, layers) in zip(given, arrays):
                for n in layers:
                    outs[j][row * depth : (row + 1) * depth, :] = ref[n, :, cut]
                    row += 1

    return kernel_call(
        body, [((count * depth, LANES), BF)] * 4, line, [a for a, _ in arrays], name
    )


def stack_weights(line, pieces, groups, extra, name):
    depth = pieces[0].shape[0] // sum(len(group) for group in groups)
    more = [a for arrays in extra for a in arrays]

    def body(ids_ref, *refs):
        given, more_in, outs = refs[:4], list(refs[4 : 4 + len(more)]), refs[4 + len(more) :]
        for k, group in enumerate(groups):
            for at, n in enumerate(group):
                for j in range(4):
                    rows = span(4 * at + (ids_ref[0] ^ j), depth)
                    outs[k][rows, :] = given[j][n * depth : (n + 1) * depth, :]
            at = 4 * len(group) * depth
            for array in extra[k]:
                outs[k][at : at + array.shape[0], :] = more_in.pop(0)[...]
                at += array.shape[0]

    sizes = [
        4 * len(group) * depth + sum(a.shape[0] for a in extra[k])
        for k, group in enumerate(groups)
    ]
    return kernel_call(
        body, [((n, LANES), BF) for n in sizes], line, list(pieces) + more, name
    )


def place_weights(line, gathered, count, depth, name, norm_rows=0, tail_rows=0):
    whole = 16 * depth
    channels = whole // TAPS
    end = 4 * count * depth
    apart = norm_rows > 0

    def body(ids_ref, g_ref, *rest):
        flat = rest[-1]
        for n in range(count):
            for r in range(4):
                for p in range(4):
                    rows = slice((4 * n + p) * depth, (4 * n + p + 1) * depth)
                    flat[(p * 4 + r) * depth : (p * 4 + r + 1) * depth, :] = g_ref[r, rows, :]
            for tap in range(TAPS):
                lanes = slice(tap * LANES, (tap + 1) * LANES)
                value = flat[tap * channels : (tap + 1) * channels, :]
                if apart:
                    rest[n][0, :, lanes] = value
                else:
                    rest[0][n, :, lanes] = value
        if apart:
            own = [g_ref[r, end : end + norm_rows, :].astype(F32) for r in range(4)]
            rest[count][...] = (own[0] + own[1]) + (own[2] + own[3])
            rest[count + 1][...] = g_ref[:, end + norm_rows : end + norm_rows + tail_rows, :]

    if apart:
        outs = [((1, channels, TAPS * LANES), BF)] * count
        outs += [((norm_rows, LANES), F32), ((4, tail_rows, LANES), BF)]
    else:
        outs = [((count, channels, TAPS * LANES), BF)]
    return kernel_call(
        body, outs, line, [gathered], name, scratch=[pltpu.VMEM((whole, LANES), BF)]
    )


def place_attention(line, pieces, maps, part):
    def body(ids_ref, *refs):
        given, out = refs[:4], refs[4]
        for j in range(4):
            for r in range(4):
                chunk = (ids_ref[0] ^ j) * 4 + r
                for t in range(maps):
                    out[t, span(chunk, part), :] = given[j][r, t * part : (t + 1) * part, :]

    return kernel_call(
        body, [((maps, 16 * part, LANES), BF)], line, list(pieces), "place_attention"
    )[0]


def trunk_layer(
    line, pieces, weight, norms, layer, cols, eps_value, form, last, masked, name, only=None
):
    channels = weight.shape[1]
    size = {"images": 1, "slices": 0.25, "cells": 1}[form]
    size = int(pieces[0].shape[0] * size)
    pixels = 4 * size
    whole_images = form == "images"

    def body(ids_ref, *refs):
        given, (w_ref, norm_ref) = refs[:4], refs[4:6]
        at = 6
        if masked is not None and not whole_images:
            mask_ref = refs[6]
            at = 7
        outs, v_ref, pairs_ref = refs[at:-2], refs[-2], refs[-1]
        field = outs[0]
        for j in range(4):
            peer = ids_ref[0] ^ j
            if whole_images:
                field[span(peer, size), :] = given[j][:, :channels]
                outs[4][span(peer, size), :] = given[j][:, channels:]
            elif form == "cells":
                cells = spread_pairs(given[j][...].astype(F32), pairs_ref, cols)
                field[:, span(peer, LANES)] = cells.astype(BF) * mask_ref[...]
            else:
                field[:, span(peer, LANES)] = given[j][...]

        def convolve(i):
            part = span(i, size)
            v_ref[part, :] = fold_taps(dot(field[part, :], w_ref[0]), cols)

        all_of(4, convolve)
        conv_out = v_ref[...]
        center = jnp.sum(conv_out, axis=0, keepdims=True) / pixels
        moved = conv_out - center
        spread = jnp.sum(moved * moved, axis=0, keepdims=True) / pixels
        inverse = lax.rsqrt(spread + eps_value)
        normed = moved * inverse
        outs[1][...] = normed
        outs[2][...] = jnp.broadcast_to(inverse, (8, LANES))
        preact = norm_ref[layer : layer + 1, :] * normed + norm_ref[2 + layer : 3 + layer, :]
        hidden = (preact * jax.nn.sigmoid(preact)).astype(BF)
        outs[3][...] = hidden
        if last and masked is not None:
            kept = hidden.astype(F32) * mask_ref[...].astype(F32)
            outs[4][...] = pool_pairs(kept, pairs_ref, cols).astype(BF)

    outs = [((pixels, channels), BF), ((pixels, LANES), F32), ((8, LANES), F32)]
    outs.append(((pixels, LANES), BF))
    if last and masked is not None:
        outs.append(((size, LANES), BF))
    elif whole_images:
        outs.append(((pixels, LANES), BF))
    extra = [masked] if masked is not None and not whole_images else []
    return kernel_call(
        body,
        outs,
        line,
        list(pieces) + [weight, norms] + extra,
        name,
        scratch=[pltpu.VMEM((pixels, LANES), F32), pltpu.VMEM((pixels // 2, LANES), F32)],
        only=only,
    )


def pool_pairs(value, pairs_ref, cols):
    size = value.shape[0]
    halves = value.reshape(size // (2 * cols), 2, cols, LANES)
    pairs_ref[: size // 2, :] = (halves[:, 0] + halves[:, 1]).reshape(size // 2, LANES)
    return pairs_ref[pl.ds(0, size // 4, stride=2), :] + pairs_ref[pl.ds(1, size // 4, stride=2), :]


def spread_pairs(small, pairs_ref, cols):
    size = 4 * small.shape[0]
    pairs_ref[pl.ds(0, size // 4, stride=2), :] = small
    pairs_ref[pl.ds(1, size // 4, stride=2), :] = small
    rows = pairs_ref[: size // 2, :].reshape(size // (2 * cols), 1, cols, LANES)
    return jnp.broadcast_to(rows, (size // (2 * cols), 2, cols, LANES)).reshape(size, LANES)


def attend(x, mixture, down, up_t):
    inner = dot(mixture, down)
    active = (inner * jax.nn.sigmoid(inner)).astype(BF)
    gate = jax.nn.sigmoid(dot_nt(active, up_t))
    return inner, active, gate


def label_at(label_ref, ids_ref, device, t):
    return label_ref[(device * 4 + ids_ref[1]) * 3 + t]


def slot_of(label_ref, ids_ref, device, t):
    first = jnp.where(t > 0, label_at(label_ref, ids_ref, device, 0), 0)
    return first + jnp.where(t > 1, label_at(label_ref, ids_ref, device, 1), 0)


def section_tasks(line, labels, x_slices, att, gathered, depth, mask, cots, cols):
    pixels = x_slices[0].shape[0]
    size = pixels // 4
    tasks_n, channels = gathered.shape[1], att.shape[1]
    down, up_t = att[:tasks_n], att[tasks_n:]

    def body(ids_ref, label_ref, *refs):
        x_in, down_ref, up_ref, g_ref, mask_ref, cot_in = refs[:4], *refs[4:8], refs[8:12]
        fields, feats, cells, du, w_ref = refs[12:16], refs[16:20], refs[20], refs[21:25], refs[25]
        x_ref, pairs_ref, flat, u_ref, f_ref, c_ref = refs[26:]
        t = pl.program_id(0)
        for r in range(4):
            for p in range(4):
                flat[(p * 4 + r) * depth : (p * 4 + r + 1) * depth, :] = g_ref[
                    r, 0, p * depth : (p + 1) * depth, :
                ]
        for tap in range(TAPS):
            w_ref[0, :, tap * LANES : (tap + 1) * LANES] = flat[
                tap * channels : (tap + 1) * channels, :
            ]

        @pl.when(ids_ref[2] == 0)
        def _():
            @pl.when(t == 0)
            def _():
                for j in range(4):
                    x_ref[:, span(ids_ref[0] ^ j, LANES)] = x_in[j][...]

            def one_image(i):
                rows = span(ids_ref[0] ^ i, size)
                x = x_ref[rows, :]
                _, _, gate = attend(x, x, down_ref[0], up_ref[0])
                u = (gate * x.astype(F32)).astype(BF)
                u_ref[i] = u
                value = fold_taps(dot(u, w_ref[0]), cols)
                f_ref[i] = value.astype(BF)
                kept = value * mask_ref[rows, :].astype(F32)
                cells[0, span(ids_ref[0] ^ i, size // 4), :] = pool_pairs(
                    kept, pairs_ref, cols
                ).astype(BF)

            all_of(4, one_image)
            for j in range(4):
                fields[j][0] = u_ref[j]
                feats[j][0] = f_ref[j]

        @pl.when(ids_ref[2] == 1)
        def _():
            for j in range(4):
                c_ref[j] = cot_in[j][0]

            def one_image(i):
                @pl.when(label_at(label_ref, ids_ref, ids_ref[0] ^ i, t) == 1)
                def _():
                    u_ref[i] = dot_nt(spread_taps(c_ref[i].astype(F32), cols), w_ref[0]).astype(BF)

            all_of(4, one_image)
            for j in range(4):
                device = ids_ref[0] ^ j

                @pl.when(t == 0)
                def _(j=j):
                    du[j][...] = jnp.zeros_like(du[j])

                @pl.when(label_at(label_ref, ids_ref, device, t) == 1)
                def _(j=j, device=device):
                    du[j][slot_of(label_ref, ids_ref, device, t)] = u_ref[j]

    def step(shape, only=None):
        return pl.BlockSpec(
            (1,) + shape[1:],
            lambda t, ids, _: (t if only is None else jnp.where(ids[2] == only, t, 0),)
            + (0,) * (len(shape) - 1),
        )

    def same(shape):
        return pl.BlockSpec(shape, lambda t, ids, _: (0,) * len(shape))

    outs = [(tasks_n, size, channels)] * 4 + [(tasks_n, size, LANES)] * 5 + [(2, size, channels)] * 4
    outs.append((tasks_n, channels, TAPS * LANES))
    args = list(x_slices) + [down, up_t, gathered, mask] + list(cots)
    results = pl.pallas_call(
        unread(body, 1, 2 + len(args)),
        grid_spec=pltpu.PrefetchScalarGridSpec(
            num_scalar_prefetch=2,
            grid=(tasks_n,),
            in_specs=[same(a.shape) for a in x_slices]
            + [step(down.shape, 0), step(up_t.shape, 0)]
            + [pl.BlockSpec((4, 1, 4 * depth, LANES), lambda t, ids, _: (0, t, 0, 0)), same(mask.shape)]
            + [step(a.shape, 1) for a in cots]
            + [pl.BlockSpec(memory_space=pl.ANY)],
            out_specs=[step(shape, 0) for shape in outs[:9]]
            + [same(shape) for shape in outs[9:13]]
            + [step(outs[13])],
            scratch_shapes=[
                pltpu.VMEM((pixels, channels), BF),
                pltpu.VMEM((size // 2, LANES), F32),
                pltpu.VMEM((TAPS * channels, LANES), BF),
                pltpu.VMEM((4, size, channels), BF),
                pltpu.VMEM((4, size, LANES), BF),
                pltpu.VMEM((4, size, LANES), BF),
            ],
        ),
        out_shape=[jax.ShapeDtypeStruct(shape, BF) for shape in outs],
        compiler_params=pltpu.CompilerParams(vmem_limit_bytes=VMEM_BYTES),
        cost_estimate=LIGHT,
        name="section_tasks",
    )(line.ids, labels, *args, line.last)
    line.last = results[-1]
    return results[:4], results[4:8], results[8], results[9:13], results[13]


def grads_of_taps(field, grad_ref, taps_ref, flat, out_at, cols, depth):
    size = taps_ref.shape[0] // 4
    channels = field.shape[1]

    def spread(i):
        part = span(i, size)
        taps_ref[part, :] = spread_taps(grad_ref[part, :].astype(F32), cols)

    if grad_ref is not None:
        all_of(4, spread)

    def row_of_taps(row):
        whole = dot_tn(field[...], taps_ref[:, span(row, 3 * LANES)])
        for b in range(3):
            flat[span(3 * row + b, channels), :] = whole[:, b * LANES : (b + 1) * LANES].astype(BF)

    all_of(3, row_of_taps)

    def keep(r):
        out = out_at(r)
        for p in range(4):
            out[p] = flat[span(p * 4 + r, depth), :]

    all_of(4, keep)


def trunk_grads(line, enc_pairs, dec_pairs, depth, cols, name):
    count = len(enc_pairs)
    pixels, channels = enc_pairs[0][0].shape
    enc_in = [a for pair in enc_pairs for a in pair]
    dec_in = [a for pair in dec_pairs for a in pair]

    def body(ids_ref, *refs):
        given, out, taps_ref, flat = refs[: 2 * count], *refs[2 * count :]
        for n in range(count):
            h_ref, g_ref = given[2 * n], given[2 * n + 1]
            grads_of_taps(
                h_ref,
                g_ref,
                taps_ref,
                flat,
                lambda r: out.at[r, n],
                cols,
                depth,
            )

    return section_call(
        body,
        [((4, count, 4, depth, LANES), BF)],
        line,
        enc_in,
        name,
        scratch=[
            pltpu.VMEM((pixels, TAPS * LANES), BF),
            pltpu.VMEM((TAPS * channels, LANES), BF),
        ],
        paired=enumerate(dec_in),
    )[0]


def dec_task_grads(line, dec_xs, q_cells, mask, att, cots, enc_grads, depth, cols):
    tasks_n, size, _ = q_cells[0].shape
    pixels, channels = 4 * size, att.shape[1]

    def body(ids_ref, *refs, parts):
        x_in, q_in, mask_ref, att_ref, cot_in = refs[:4], refs[4:8], refs[8], refs[9], refs[10:14]
        u_ref, out, taps_ref, flat, x_ref, s_ref, pairs_ref, g_ref, field_ref = refs[14:]
        for j in range(4):
            x_ref[:, span(ids_ref[0] ^ j, LANES)] = x_in[j][...]

        def task(t):
            for j in range(4):
                g_ref[j * size : (j + 1) * size, :] = cot_in[j][t]

            def one_image(i):
                image = ids_ref[0] ^ i
                rows = span(image, size)
                x_low = x_ref[rows, :]
                x = x_low.astype(F32)
                own = mask_ref[rows, :]
                for j in range(4):
                    kept = q_in[j][t, span(image, size // 4), :].astype(F32)
                    cells = spread_pairs(kept, pairs_ref, cols)
                    s_ref[:, span(ids_ref[0] ^ j, LANES)] = cells.astype(BF) * own
                mixture = (x + s_ref[...].astype(F32)).astype(BF)
                _, _, gate = attend(x_low, mixture, att_ref[t], att_ref[tasks_n + t])
                field_ref[span(i, size), :] = (gate * x).astype(BF)

            all_of(4, one_image)
            u_ref[t] = field_ref[...]
            parts.send(0, t)
            grads_of_taps(field_ref, g_ref, taps_ref, flat, lambda r: out.at[r, t], cols, depth)

        each(tasks_n, task)

    return section_call(
        body,
        [((tasks_n, pixels, channels), BF), ((4, tasks_n, 4, depth, LANES), BF)],
        line,
        list(dec_xs) + list(q_cells) + [mask, att] + list(cots),
        "dec_task_grads",
        scratch=[
            pltpu.VMEM((pixels, TAPS * LANES), BF),
            pltpu.VMEM((TAPS * channels, LANES), BF),
            pltpu.VMEM((pixels, channels), BF),
            pltpu.VMEM((size, channels), BF),
            pltpu.VMEM((size // 2, LANES), F32),
            pltpu.VMEM((pixels, LANES), BF),
            pltpu.VMEM((pixels, channels), BF),
        ],
        only=1,
        other={1: enc_grads},
        split_out=(0,),
    )


def enc_tasks_reverse(line, labels, grad_pieces, fields, weights, mask, depth, cols):
    tasks_n, given_size, _ = grad_pieces[0].shape
    channels = weights.shape[1]
    size = 4 * given_size
    pixels = 4 * size

    def body(ids_ref, label_ref, *refs, parts):
        given, u_in, w_ref, mask_ref, outs = refs[:4], refs[4:8], refs[8], refs[9], refs[10:14]
        grads, pairs_ref, taps_ref, flat, whole, g_ref, back_ref = refs[14:]
        for j in range(4):
            outs[j][1] = jnp.zeros((size, channels), BF)
        def task(t):
            parts.need(8, t)
            for j in range(4):
                rows = slice(j * size, (j + 1) * size)
                cells = spread_pairs(given[j][t].astype(F32), pairs_ref, cols)
                g_ref[rows, :] = cells.astype(BF) * mask_ref[span(ids_ref[0] ^ j, size), :]
                parts.need(4 + j, t)
                whole[rows, :] = u_in[j][t]

            def spread(i):
                part = span(i, size)
                taps_ref[part, :] = spread_taps(g_ref[part, :].astype(F32), cols)
                device = ids_ref[0] ^ i

                @pl.when(label_at(label_ref, ids_ref, device, t) == 1)
                def _():
                    back_ref[i] = dot_nt(taps_ref[part, :], w_ref[t]).astype(BF)

            all_of(4, spread)
            for j in range(4):
                device = ids_ref[0] ^ j

                @pl.when(label_at(label_ref, ids_ref, device, t) == 1)
                def _(j=j, device=device):
                    outs[j][slot_of(label_ref, ids_ref, device, t)] = back_ref[j]

            grads_of_taps(whole, None, taps_ref, flat, lambda r: grads.at[r, t], cols, depth)

        each(tasks_n, task)

    return section_call(
        body,
        [((2, size, channels), BF)] * 4 + [((4, tasks_n, 4, depth, LANES), BF)],
        line,
        list(grad_pieces) + list(fields) + [weights, mask],
        "enc_tasks_back",
        scratch=[
            pltpu.VMEM((size // 2, LANES), F32),
            pltpu.VMEM((pixels, TAPS * LANES), BF),
            pltpu.VMEM((TAPS * channels, LANES), BF),
            pltpu.VMEM((pixels, channels), BF),
            pltpu.VMEM((pixels, LANES), BF),
            pltpu.VMEM((4, size, channels), BF),
        ],
        only=0,
        split_in=range(4, 9),
        smem=[labels],
    )


def dec_task_layer(line, fields, weights, enc_feats, cols, name):
    tasks_n, channels, _ = weights.shape
    size = fields.shape[1] // 4

    def body(ids_ref, u_ref, w_ref, *rest, parts):
        outs, all_ref = rest[:4], rest[4]

        def task(t):
            parts.need(1, t)
            parts.need(0, t)

            def convolve(i):
                value = dot(u_ref[t, span(i, size), :], w_ref[t])
                all_ref[i] = fold_taps(value, cols).astype(BF)

            all_of(4, convolve)
            for j in range(4):
                outs[j][t] = all_ref[j]

        each(tasks_n, task)

    return section_call(
        body,
        [((tasks_n, size, LANES), BF)] * 4,
        line,
        [fields, weights],
        name,
        scratch=[pltpu.VMEM((4, size, LANES), BF)],
        only=1,
        other=enumerate(enc_feats),
        split_in=(0, 1),
    )


def heads_reverse(line, labels, x_pieces, carried, mask, du_pieces, att, cols, name, only, other=None):
    size = x_pieces[0].shape[0] // 4
    channels = att.shape[1]
    tasks_n = att.shape[0] // 2
    carry = carried is not None

    def body(ids_ref, label_ref, *refs):
        x_in, rest = refs[:4], refs[4:]
        if carry:
            q_in, mask_ref, rest = rest[:4], rest[4], rest[5:]
        du_in, att_ref, rest = rest[:4], rest[4], rest[5:]
        outs, (x_ref, s_ref, ds_ref, da_ref, pairs_ref) = rest[:-5], rest[-5:]
        dx_ref, g_ref, grads = outs[0], outs[1], outs[2:6]
        for j in range(4):
            x_ref[:, span(ids_ref[0] ^ j, LANES)] = x_in[j][span(ids_ref[0], size), :]

        def task(t):
            x_low = x_ref[...]
            x = x_low.astype(F32)
            slot = slot_of(label_ref, ids_ref, ids_ref[0], t)
            if carry:
                own = mask_ref[span(ids_ref[0], size), :]
                for j in range(4):
                    kept = q_in[j][t, span(ids_ref[0], size // 4), :].astype(F32)
                    cells = spread_pairs(kept, pairs_ref, cols)
                    s_ref[:, span(ids_ref[0] ^ j, LANES)] = cells.astype(BF) * own
                mixture = (x + s_ref[...].astype(F32)).astype(BF)
            else:
                mixture = x_low
            inner, active, gate = attend(x, mixture, att_ref[t], att_ref[tasks_n + t])
            du = (
                (du_in[0][slot].astype(F32) + du_in[1][slot].astype(F32))
                + (du_in[2][slot].astype(F32) + du_in[3][slot].astype(F32))
            )
            gated = du * gate
            do = (gated * x * (1.0 - gate)).astype(BF)
            sig = jax.nn.sigmoid(inner)
            dk = (dot(do, att_ref[tasks_n + t]) * (sig * (1.0 + inner * (1.0 - sig)))).astype(BF)
            ds = dot_nt(dk, att_ref[t])
            dx_ref[t] = gated + ds
            if carry:
                ds_ref[...] = ds
                for j in range(4):
                    kept = ds_ref[:, span(ids_ref[0] ^ j, LANES)] * own.astype(F32)
                    outs[6 + j][t] = pool_pairs(kept, pairs_ref, cols).astype(BF)
            for row, value in ((t, dot_tn(mixture, dk)), (tasks_n + t, dot_tn(do, active))):
                da_ref[...] = value
                for j in range(4):
                    grads[j][row] = da_ref[span(ids_ref[0] ^ j, LANES), :].astype(BF)

        def no_task(t):
            dx_ref[t] = jnp.zeros((size, channels), F32)
            for j in range(4):
                if carry:
                    outs[6 + j][t] = jnp.zeros((size // 4, LANES), BF)
                grads[j][t] = jnp.zeros((LANES, LANES), BF)
                grads[j][tasks_n + t] = jnp.zeros((LANES, LANES), BF)

        def either(t):
            label = label_at(label_ref, ids_ref, ids_ref[0], t)
            pl.when(label == 1)(functools.partial(task, t))
            pl.when(label != 1)(functools.partial(no_task, t))

        each(tasks_n, either)
        row = 0
        g_ref[...] = jnp.zeros_like(g_ref)
        for a in range(tasks_n):
            for b in range(a, tasks_n):
                line_sum = jnp.sum(dx_ref[a] * dx_ref[b], axis=0, keepdims=True)
                folded = line_sum[:, :LANES]
                for part in range(1, channels // LANES):
                    folded = folded + line_sum[:, part * LANES : (part + 1) * LANES]
                g_ref[row : row + 1, :] = folded
                row += 1

    outs = [((tasks_n, size, channels), F32), ((8, LANES), F32)]
    outs += [((2 * tasks_n, LANES, LANES), BF)] * 4
    if carry:
        outs += [((tasks_n, size // 4, LANES), BF)] * 4
    return section_call(
        body,
        outs,
        line,
        list(x_pieces) + (list(carried) + [mask] if carry else []) + list(du_pieces) + [att],
        name,
        scratch=[
            pltpu.VMEM((size, channels), BF),
            pltpu.VMEM((size, channels), BF),
            pltpu.VMEM((size, channels), F32),
            pltpu.VMEM((channels, LANES), F32),
            pltpu.VMEM((size // 2, LANES), F32),
        ],
        only=only,
        other=other,
        smem=[labels],
    )


def nash_values(lines, tasks_n):
    def full(row):
        return jnp.broadcast_to(jnp.sum(lines[row : row + 1, :], axis=1, keepdims=True), (8, LANES))

    gram = [[None] * tasks_n for _ in range(tasks_n)]
    row = 0
    for a in range(tasks_n):
        for b in range(a, tasks_n):
            gram[a][b] = gram[b][a] = full(row)
            row += 1
    trace_mean = (gram[0][0] + gram[1][1] + gram[2][2]) / 3.0 + 1e-06
    norm = [[gram[a][b] / trace_mean for b in range(3)] for a in range(3)]
    alpha = [lax.rsqrt(norm[a][a] + 1e-06) for a in range(3)]
    for _ in range(NASH_ITERS):
        right = [
            norm[a][0] * alpha[0] + norm[a][1] * alpha[1] + norm[a][2] * alpha[2] - 1.0 / alpha[a]
            for a in range(3)
        ]
        matrix = [
            [norm[a][b] + 1.0 / (alpha[a] * alpha[a]) if a == b else norm[a][b] for b in range(3)]
            for a in range(3)
        ]
        cof = [[None] * 3 for _ in range(3)]
        for a in range(3):
            for b in range(3):
                a1, a2, b1, b2 = (a + 1) % 3, (a + 2) % 3, (b + 1) % 3, (b + 2) % 3
                cof[a][b] = matrix[a1][b1] * matrix[a2][b2] - matrix[a1][b2] * matrix[a2][b1]
        determinant = (
            matrix[0][0] * cof[0][0] + matrix[0][1] * cof[0][1] + matrix[0][2] * cof[0][2]
        )
        update = [
            (cof[0][b] * right[0] + cof[1][b] * right[1] + cof[2][b] * right[2]) / determinant
            for b in range(3)
        ]
        alpha = [alpha[a] * jnp.exp(-0.5 * jnp.tanh(update[a] / alpha[a])) for a in range(3)]
    return alpha


def weigh(line, dx, w_or_lines, solve, name):
    tasks_n, size, channels = dx.shape

    def body(ids_ref, *refs):
        given, dx_ref, outs, total = refs[: len(w_or_lines)], refs[len(w_or_lines)], refs[-6:-1], refs[-1]
        if solve:
            lines = (given[0][0] + given[0][1]) + (given[0][2] + given[0][3])
            alpha = nash_values(lines, tasks_n)
            outs[0][...] = jnp.concatenate(
                [alpha[t][:1] for t in range(3)] + [jnp.zeros((5, LANES), F32)], axis=0
            )
        else:
            outs[0][...] = given[0][...]
        acc = None
        for t in range(tasks_n):
            scale = jnp.tile(outs[0][t : t + 1, :], (1, channels // LANES))
            term = dx_ref[t] * scale
            acc = term if acc is None else acc + term
        total[...] = acc
        for j in range(4):
            outs[1 + j][...] = total[:, span(ids_ref[0] ^ j, LANES)].astype(BF)

    return kernel_call(
        body,
        [((8, LANES), F32)] + [((size, LANES), BF)] * 4,
        line,
        list(w_or_lines) + [dx],
        name,
        scratch=[pltpu.VMEM((size, channels), F32)],
    )


def trunk_reverse(
    line, pieces, by_image, cells, mask, normed, inverse, norms, layer, weight, cols, parts, other, name, only
):
    pixels = normed.shape[0]
    size = pixels // 4
    channels = weight.shape[1]
    takes, gives = cells is not None, "cells" in parts
    shapes = {"slices": (pixels, LANES), "images": (size, channels), "cells": (size, LANES)}

    def body(ids_ref, *refs):
        given, rest = refs[:4], refs[4:]
        if takes:
            cells_in, rest = rest[:4], rest[4:]
        if takes or gives:
            mask_ref, rest = rest[0], rest[1:]
        (n_ref, inv_ref, norm_ref, w_ref), rest = rest[:4], rest[4:]
        if other is not None:
            other_in, rest = rest[:4], rest[4:]
        outs, (acc_ref, back_ref, pairs_ref) = rest[:-3], rest[-3:]
        gain = norm_ref[layer : layer + 1, :]

        @pl.when(ids_ref[2] == only)
        def _():
            if by_image:
                for j in range(4):
                    acc_ref[span(ids_ref[0] ^ j, size), :] = given[j][...].astype(F32)
            else:
                acc_ref[...] = (given[0][...].astype(F32) + given[1][...].astype(F32)) + (
                    given[2][...].astype(F32) + given[3][...].astype(F32)
                )
            grad = acc_ref[...]
            if takes:
                start = (cells_in[0][...].astype(F32) + cells_in[1][...].astype(F32)) + (
                    cells_in[2][...].astype(F32) + cells_in[3][...].astype(F32)
                )
                start = start.astype(BF).astype(F32)
                grad = grad + spread_pairs(start, pairs_ref, cols) * mask_ref[...].astype(F32)
            normed_value = n_ref[...]
            preact = gain * normed_value + norm_ref[2 + layer : 3 + layer, :]
            sig = jax.nn.sigmoid(preact)
            dp = grad * (sig * (1.0 + preact * (1.0 - sig)))
            bias_total = jnp.sum(dp, axis=0, keepdims=True)
            gain_total = jnp.sum(dp * normed_value, axis=0, keepdims=True)
            outs[1][...] = jnp.concatenate(
                [gain_total, bias_total, jnp.zeros((6, LANES), F32)], axis=0
            )
            scale = inv_ref[0:1, :] * gain
            dv = scale * (dp - bias_total / pixels - normed_value * (gain_total / pixels))
            outs[0][...] = dv.astype(BF)
            acc_ref[...] = dv.astype(BF).astype(F32)

            def convolve(i):
                part = span(i, size)
                back_ref[part, :] = dot_nt(spread_taps(acc_ref[part, :], cols), w_ref[0])

            all_of(4, convolve)
            for at, kind in enumerate(parts):
                for j in range(4):
                    peer = ids_ref[0] ^ j
                    out = outs[2 + 4 * at + j]
                    if kind == "images":
                        out[...] = back_ref[span(peer, size), :].astype(BF)
                    elif kind == "slices":
                        out[...] = back_ref[:, span(peer, LANES)].astype(BF)
                    else:
                        kept = back_ref[:, span(peer, LANES)] * mask_ref[...].astype(F32)
                        out[...] = pool_pairs(kept, pairs_ref, cols).astype(BF)

        if other is not None:

            @pl.when(ids_ref[2] != only)
            def _():
                for j in range(4):
                    outs[2 + 4 * parts.index("images") + j][...] = other_in[j][...]

    outs = [((pixels, LANES), BF), ((8, LANES), F32)]
    for kind in parts:
        outs += [(shapes[kind], BF)] * 4
    extra = list(cells) if takes else []
    if takes or gives:
        extra.append(mask)
    return kernel_call(
        body,
        outs,
        line,
        list(pieces) + extra + [normed, inverse, norms, weight] + list(other or []),
        name,
        scratch=[
            pltpu.VMEM((pixels, LANES), F32),
            pltpu.VMEM((pixels, channels), F32),
            pltpu.VMEM((pixels // 2, LANES), F32),
        ],
    )


def plane_device(
    x_in,
    pool_index,
    task_mask,
    task_cot,
    trunk_conv,
    norm_gain,
    norm_bias,
    att_down,
    attention_up_weights,
    task_conv,
):
    micro_count, _, rows_n, cols, channels = x_in.shape
    tasks_n = task_cot.shape[0]
    strip = rows_n * cols
    size = strip * micro_count
    depth = trunk_conv.shape[2]
    part = att_down.shape[2]
    section = lax.axis_index("pipe")
    decoder = section == 1
    row_at = lax.axis_index("rows")
    line = Line(jnp.stack([lax.axis_index("dp"), row_at, section]).astype(jnp.int32))
    ENC, DEC, BOTH = (0,), (1,), (0, 1)

    norm_own = jnp.concatenate([norm_gain[0], norm_bias[0]], axis=0)
    own_lanes = jnp.arange(LANES) // part == row_at
    norm_own = jnp.where(own_lanes[None], jnp.tile(norm_own, (1, LANES // part)), 0).astype(BF)
    norm_own = jnp.pad(norm_own, ((0, 12), (0, 0)))
    att_own = jnp.concatenate(
        [att_down[0], jnp.swapaxes(attention_up_weights[0], 1, 2)], axis=0
    ).reshape(2 * tasks_n * part, LANES)

    trunk_cut = trade(cut_weights(line, [(trunk_conv[0], [0, 1])], "cut_trunk"), "dp", BOTH)

    labels = lax.all_gather(task_mask, "dp").reshape(-1)

    picked = pool_index[:, 0, :, None, :, None]
    place = jnp.arange(2)[:, None, None] * 2 + jnp.arange(2)[None, None, :]
    cells = (picked == place[None, None]).astype(BF)
    cells = jnp.broadcast_to(cells.reshape(micro_count, strip, 1), (micro_count, strip, LANES))
    strips = x_in.reshape(micro_count, strip, channels)

    def cut_input(ids_ref, x_ref, m_ref, *outs):
        for j in range(4):
            outs[j][:, :channels] = x_ref[ids_ref[1] ^ j]
            outs[j][:, channels:] = m_ref[ids_ref[1] ^ j]

    strips = kernel_call(
        cut_input, [((strip, channels + LANES), BF)] * 4, line, [strips, cells], "cut_input"
    )
    strips = trade(strips, "rows", BOTH)

    trunk_block = stack_weights(line, trunk_cut, [[0, 1]], [[norm_own, att_own]], "stack_trunk")[0]
    trunk_all = lax.all_gather(trunk_block, "rows")

    def place_input(ids_ref, a, b, c, e, o_ref):
        for j, piece in enumerate((a, b, c, e)):
            o_ref[span(ids_ref[1] ^ j, strip), :] = piece[...]

    x_image = kernel_call(
        place_input, [((size, channels + LANES), BF)], line, strips, "place_input"
    )[0]
    x_images = trade([x_image] * 4, "dp", ENC)
    task_cut = trade(
        cut_weights(line, [(task_conv[0], range(tasks_n))], "cut_tasks"), "dp", BOTH
    )
    anchor(line, x_images, "input_there")
    task_block = stack_weights(line, task_cut, [list(range(tasks_n))], [[]], "stack_tasks")[0]
    task_all = lax.all_gather(task_block, "rows")

    half = channels // 2

    def cut_cot(ids_ref, mask_ref, c_ref, *outs):
        for j in range(4):
            micro = ids_ref[1] ^ j
            for t in range(tasks_n):
                labelled = mask_ref[micro * tasks_n + t].astype(F32)
                value = c_ref[t, micro, :, span(ids_ref[2], half)].astype(F32)
                outs[j][t] = (value * labelled).astype(BF)

    cot_strips = kernel_call(
        cut_cot,
        [((tasks_n, strip, half), BF)] * 4,
        line,
        [task_cot.reshape(tasks_n, micro_count, strip, channels)],
        "cut_cotangents",
        smem=[task_mask.reshape(-1)],
    )
    cot_strips = trade(cot_strips, "rows", BOTH)

    def place_cot(ids_ref, _, a, b, c, e, o_ref):
        for j, piece in enumerate((a, b, c, e)):
            for t in range(tasks_n):
                o_ref[t, span(ids_ref[1] ^ j, strip), :] = piece[t]

    cot_half = kernel_call(
        place_cot, [((tasks_n, size, half), BF)], line, cot_strips, "place_cotangents", smem=[labels]
    )[0]
    cot_other = swap_sections([cot_half])[0]

    def slice_cot(ids_ref, own_ref, other_ref, *rest):
        outs, image = rest[:4], rest[4]
        image[:, :, :half] = other_ref[...]
        image[:, :, half:] = own_ref[...]
        for j in range(4):
            outs[j][...] = image[:, :, span(ids_ref[0] ^ j, LANES)]

    cots = kernel_call(
        slice_cot,
        [((tasks_n, size, LANES), BF)] * 4,
        line,
        [cot_half, cot_other],
        "slice_cotangents",
        scratch=[pltpu.VMEM((tasks_n, size, channels), BF)],
    )
    cots = trade(cots, "dp", BOTH)
    first_w, second_w, norms, att_rows = place_weights(
        line, trunk_all, 2, depth, "place_trunk", norm_own.shape[0], att_own.shape[0]
    )
    enc_h0, enc_n1, enc_i1, enc_h, mask = trunk_layer(
        line, x_images, first_w, norms, 0, cols, eps, "images", False, None, "enc_layer1", 0
    )
    enc_hs = trade([enc_h] * 4, "dp", ENC)
    dec_mask = swap_sections([mask])[0]
    att = place_attention(line, trade([att_rows] * 4, "dp", BOTH), 2 * tasks_n, part)
    enc_h1, enc_n2, enc_i2, enc_x, z = trunk_layer(
        line, enc_hs, second_w, norms, 1, cols, eps, "slices", True, mask, "enc_layer2", 0
    )
    z_pieces = swap_sections([z] * 4)
    enc_xs = trade([enc_x] * 4, "dp", ENC)

    dec_h0, dec_n1, dec_i1, dec_h = trunk_layer(
        line, z_pieces, first_w, norms, 0, cols, eps, "cells", False, dec_mask, "dec_layer1", 1
    )
    dec_hs = trade([dec_h] * 4, "dp", DEC)

    dec_h1, dec_n2, dec_i2, dec_x = trunk_layer(
        line, dec_hs, second_w, norms, 1, cols, eps, "slices", True, None, "dec_layer2", 1
    )
    dec_xs = trade([dec_x] * 4, "dp", BOTH)

    gathered = task_all.reshape(4, tasks_n, 4 * depth, LANES)
    enc_us, enc_feats, kept, du, task_w = section_tasks(
        line, labels, enc_xs, att, gathered, depth, mask, cots, cols
    )
    anchor(line, dec_xs, "decoder_there")
    dec_du = trade(du, "dp", DEC)
    q_cells = swap_sections([kept] * 4)

    dec_dx, lines, *rest = heads_reverse(
        line, labels, dec_xs, q_cells, dec_mask, dec_du, att, cols, "dec_heads", 1
    )
    dec_att, ds = rest[:4], rest[4:]
    ds = swap_sections(ds)
    lines = jnp.sum(lax.all_gather(lines, "dp"), axis=0)
    terms = lax.all_gather(lines, "rows")
    dec_w, *dh = weigh(line, dec_dx, [terms], True, "bargain")
    dh = trade(dh, "dp", BOTH)
    enc_w = swap_sections([dec_w])[0]
    nash_w = jnp.where(decoder, dec_w, enc_w)

    anchor(line, dh, "bargain_there")
    *du, enc_dw = enc_tasks_reverse(
        line, labels, ds, enc_us, task_w, mask, depth, cols
    )
    enc_du = trade(du, "dp", ENC)
    dec_dv2, dec_s2, *dh = trunk_reverse(
        line, dh, True, None, None, dec_n2, dec_i2, norms, 1, second_w, cols, ["slices"], None, "dec_back2", 1
    )
    dh = trade(dh, "dp", DEC)
    dec_u, task_dw = dec_task_grads(
        line, dec_xs, q_cells, dec_mask, att, cots, enc_dw, depth, cols
    )
    task_dw = lax.psum_scatter(task_dw, "rows", scatter_dimension=0, tiled=True)
    dec_dv1, dec_s1, *rest = trunk_reverse(
        line, dh, False, None, dec_mask, dec_n1, dec_i1, norms, 0, first_w, cols, ["cells", "images"], None, "dec_back1", 1
    )
    dec_start, dec_dz = swap_sections(rest[:4]), rest[4:]
    enc_dx, _, *att_parts = heads_reverse(
        line, labels, enc_xs, None, None, enc_du, att, cols, "enc_heads_back", 0, {k + 2: a for k, a in enumerate(dec_att)}
    )
    _, *dh = weigh(line, enc_dx, [enc_w], False, "enc_weigh")
    dh = trade(dh, "dp", BOTH)
    att_parts = trade(att_parts, "dp", BOTH)

    feats = dec_task_layer(line, dec_u, task_w, enc_feats, cols, "dec_tasks")
    feats = trade(feats, "dp", BOTH)
    enc_dv2, enc_s2, *dh = trunk_reverse(
        line, dh, True, dec_start, mask, enc_n2, enc_i2, norms, 1, second_w, cols, ["slices"], None, "enc_back2", 0
    )
    dh = trade(dh, "dp", ENC)

    enc_dv1, enc_s1, *dz = trunk_reverse(
        line, dh, False, None, None, enc_n1, enc_i1, norms, 0, first_w, cols, ["images"], dec_dz, "enc_back1", 0
    )
    dz = trade(dz, "dp", BOTH)
    trunk_dw = trunk_grads(
        line,
        [(enc_h0, enc_dv1), (enc_h1, enc_dv2)],
        [(dec_h0, dec_dv1), (dec_h1, dec_dv2)],
        depth,
        cols,
        "trunk_grads",
    )
    trunk_dw = lax.psum_scatter(trunk_dw, "rows", scatter_dimension=0, tiled=True)


    def cut_shares(sums, name):
        count = sums.shape[1]

        def cut(ids_ref, g_ref, *outs):
            for j in range(4):
                for n in range(count):
                    outs[j][n] = g_ref[0, n, ids_ref[0] ^ j]

        return kernel_call(cut, [((count, depth, LANES), BF)] * 4, line, [sums], name)

    def join(layers, scale, name):
        counts = [pieces[0].shape[0] for pieces in layers]

        def body(ids_ref, *refs):
            o_ref, at = refs[-1], 0
            for m, count in enumerate(counts):
                for n in range(count):
                    for j in range(4):
                        value = refs[4 * m + j][n].astype(F32)
                        if scale is not None:
                            value = value * refs[4 * len(counts)][n : n + 1, :]
                        o_ref[at, :, span(ids_ref[0] ^ j, LANES)] = value
                    at += 1

        return kernel_call(
            body,
            [((sum(counts), depth, channels), F32)],
            line,
            [piece for pieces in layers for piece in pieces] + ([] if scale is None else [scale]),
            name,
        )[0]

    def cut_att(ids_ref, a, b, c, e, *rest):
        outs, total = rest[:4], rest[4]
        total[...] = (a[...].astype(F32) + b[...].astype(F32)) + (
            c[...].astype(F32) + e[...].astype(F32)
        )
        for j in range(4):
            outs[j][...] = total[:, span(ids_ref[1] ^ j, part), :].astype(BF)

    att_parts = kernel_call(
        cut_att,
        [((2 * tasks_n, part, LANES), BF)] * 4,
        line,
        att_parts,
        "cut_attention",
        scratch=[pltpu.VMEM((2 * tasks_n, LANES, LANES), F32)],
    )
    att_parts = trade(att_parts, "rows", BOTH)

    def cut_feats(ids_ref, a, b, c, e, *rest):
        outs, image = rest[:4], rest[4]
        for j, piece in enumerate((a, b, c, e)):
            image[:, :, span(ids_ref[0] ^ j, LANES)] = piece[...]
        for j in range(4):
            outs[j][...] = image[:, span(ids_ref[1] ^ j, strip), :]

    feats = kernel_call(
        cut_feats,
        [((tasks_n, strip, channels), BF)] * 4,
        line,
        feats,
        "cut_features",
        scratch=[pltpu.VMEM((tasks_n, size, channels), BF)],
    )
    feats = trade(feats, "rows", BOTH)

    sums = jnp.where(
        decoder, jnp.concatenate([dec_s1, dec_s2]), jnp.concatenate([enc_s1, enc_s2])
    )
    sums = trade([sums] * 4, "rows", BOTH)
    sums = (sums[0] + sums[1]) + (sums[2] + sums[3])
    sums = lax.dynamic_slice_in_dim(sums, row_at * part, part, axis=1)
    gain_out = jnp.stack([sums[0], sums[8]])
    bias_out = jnp.stack([sums[1], sums[9]])

    def cut_start(ids_ref, a, b, c, e, *rest):
        outs, image = rest[:4], rest[4]
        image[...] = (a[...].astype(F32) + b[...].astype(F32)) + (
            c[...].astype(F32) + e[...].astype(F32)
        )
        for j in range(4):
            outs[j][...] = image[span(ids_ref[1] ^ j, strip), :].astype(BF)

    starts = kernel_call(
        cut_start,
        [((strip, channels), BF)] * 4,
        line,
        dz,
        "cut_start",
        scratch=[pltpu.VMEM((size, channels), F32)],
    )
    starts = trade(starts, "rows", BOTH)

    task_parts = trade(cut_shares(task_dw, "share_tasks"), "dp", BOTH)

    def join_att(ids_ref, a, b, c, e, w_ref, o_ref):
        total = (a[...].astype(F32) + b[...].astype(F32)) + (
            c[...].astype(F32) + e[...].astype(F32)
        )
        for t in range(2 * tasks_n):
            at = t % tasks_n
            o_ref[t] = total[t] * w_ref[at : at + 1, :]

    att_out = kernel_call(
        join_att,
        [((2 * tasks_n, part, LANES), F32)],
        line,
        att_parts + [nash_w],
        "join_attention",
    )[0]

    task_out = join([task_parts], nash_w, "join_tasks")

    def place_feats(ids_ref, a, b, c, e, o_ref):
        for j, piece in enumerate((a, b, c, e)):
            for t in range(tasks_n):
                o_ref[t, ids_ref[1] ^ j] = piece[t]

    feats_out = kernel_call(
        place_feats, [((tasks_n, micro_count, strip, channels), BF)], line, feats, "place_features"
    )[0]

    def place_start(ids_ref, a, b, c, e, o_ref):
        for j, piece in enumerate((a, b, c, e)):
            o_ref[ids_ref[1] ^ j] = piece[...].astype(F32)

    start_out = kernel_call(
        place_start, [((micro_count, strip, channels), F32)], line, starts, "place_start"
    )[0]
    trunk_parts = trade(cut_shares(trunk_dw, "share_trunk"), "dp", BOTH)
    trunk_out = join([trunk_parts], None, "join_trunk")

    return (
        feats_out.reshape(1, tasks_n, micro_count, 1, rows_n, cols, channels),
        start_out.reshape(1, micro_count, 1, rows_n, cols, channels),
        trunk_out[None],
        gain_out[None],
        bias_out[None],
        att_out[:tasks_n][None],
        jnp.swapaxes(att_out[tasks_n:], 1, 2)[None],
        task_out[None],
        nash_w[:3, 0],
    )


def by_planes(x_in, task_cot):
    peers, planes = lax.axis_size("dp"), lax.axis_size("rows")
    micro, samples, _, _, channels = x_in.shape
    return (
        peers == 4
        and planes == 4
        and micro == planes
        and samples == 1
        and channels == peers * LANES
        and task_cot.shape[0] == 3
    )


def section_device(*arrays):
    if by_planes(arrays[0], arrays[3]):
        return plane_device(*arrays)
    return on_device(*arrays)


def solution(mesh):
    in_specs = (
        P(None, "dp", "rows", None, None),
        P(None, "dp", "rows", None),
        P(None, "dp", None),
        P(None, None, "dp", "rows", None, None),
        P("pipe", None, ("dp", "rows"), None),
        P("pipe", None, ("dp", "rows")),
        P("pipe", None, ("dp", "rows")),
        P("pipe", None, ("dp", "rows"), None),
        P("pipe", None, None, ("dp", "rows")),
        P("pipe", None, ("dp", "rows"), None),
    )
    out_specs = (
        P("pipe", None, None, "dp", "rows", None, None),
        P("pipe", None, "dp", "rows", None, None),
        P("pipe", None, ("dp", "rows"), None),
        P("pipe", None, ("dp", "rows")),
        P("pipe", None, ("dp", "rows")),
        P("pipe", None, ("dp", "rows"), None),
        P("pipe", None, None, ("dp", "rows")),
        P("pipe", None, ("dp", "rows"), None),
        P(),
    )
    return jax.shard_map(
        section_device, mesh=mesh, in_specs=in_specs, out_specs=out_specs, check_vma=False
    )
```

```python
import functools

import jax
import jax.numpy as jnp
from jax import lax
from jax.experimental import pallas as pl
from jax.experimental.pallas import tpu as pltpu
from jax.sharding import PartitionSpec as P

NASH_ITERS = 3


eps = 1e-05


def extended_2(array, sides, width):
    for axis, dim in sides:
        peers, length = (lax.axis_size(axis), array.shape[dim])
        up = [(i, (i + 1) % peers) for i in range(peers - 1)]
        down = [(j, i) for i, j in up]
        last = lax.slice_in_dim(array, length - width, length, axis=dim)
        first = lax.slice_in_dim(array, 0, width, axis=dim)
        before = lax.ppermute(last, axis, up)
        after = lax.ppermute(first, axis, down)
        array = jnp.concatenate([before, array, after], axis=dim)
    return array


def from_behind(array, axis, by):
    peers = lax.axis_size(axis)
    pairs = [(i, i + by) for i in range(peers) if 0 <= i + by < peers]
    return lax.ppermute(array, axis, pairs)


def silu_slope(preact):
    sigmoid_val = jax.nn.sigmoid(preact)
    return sigmoid_val * (1.0 + preact * (1.0 - sigmoid_val))


def choose_side(condition, when_true, when_false):

    def either(true_leaf, false_leaf):
        return jnp.where(condition, true_leaf, false_leaf)

    return jax.tree.map(either, when_true, when_false)


def pool_cells(field, positions):
    leading = field.shape[:-4]
    samples, rows_n, cols_n, channels = field.shape[-4:]
    blocks = field.astype(jnp.float32).reshape(
        leading + (samples, rows_n // 2, 2, cols_n // 2, 2, channels)
    )
    blocks = jnp.moveaxis(blocks, -4, -3).reshape(
        leading + (samples, rows_n // 2, cols_n // 2, 4, channels)
    )
    return jnp.sum(blocks * positions[..., None], axis=-2)


def unpool_cells(small, positions):
    leading = small.shape[:-4]
    samples, rows_h, cols_h, channels = small.shape[-4:]
    blocks = small.astype(jnp.float32)[..., None, :] * positions[..., None]
    blocks = blocks.reshape(leading + (samples, rows_h, cols_h, 2, 2, channels))
    blocks = jnp.moveaxis(blocks, -3, -4)
    return blocks.reshape(leading + (samples, 2 * rows_h, 2 * cols_h, channels))


def gather_taps(padded, rows_n, cols_n):
    stencil = [
        padded[:, :, offset // 3 : offset // 3 + rows_n, offset % 3 : offset % 3 + cols_n, :]
        for offset in range(9)
    ]
    return jnp.concatenate(stencil, axis=-1)


def conv_forward(field, weight):
    extended = extended_2(field, (("rows", 2),), 1)
    padded = jnp.pad(extended, ((0, 0), (0, 0), (0, 0), (1, 1), (0, 0)))
    stencil = gather_taps(padded, field.shape[2], field.shape[3])
    conv_out = jnp.einsum("ksrwq,kqd->ksrwd", stencil, weight, preferred_element_type=jnp.float32)
    return (conv_out, padded)


def conv_backward(padded, grad_out, weight, wanted):
    rows_n, cols_n = (grad_out.shape[2], grad_out.shape[3])
    extended = extended_2(grad_out, (("rows", 2),), 1)
    beside_all = jnp.pad(extended, ((0, 0), (0, 0), (0, 0), (1, 1), (0, 0)))
    flipped = jnp.stack(
        [
            beside_all[
                :,
                :,
                2 - offset // 3 : 2 - offset // 3 + rows_n,
                2 - offset % 3 : 2 - offset % 3 + cols_n,
                :,
            ]
            for offset in range(9)
        ],
        axis=-2,
    )
    kernel = weight.reshape(weight.shape[0], 9, weight.shape[2], weight.shape[2])
    grad_in = jnp.einsum("ksrwtd,ktcd->ksrwc", flipped, kernel, preferred_element_type=jnp.float32)
    weight_grad = None
    if wanted:
        weight_grad = jnp.einsum(
            "ksrwq,ksrwd->kqd",
            gather_taps(padded, rows_n, cols_n),
            grad_out,
            preferred_element_type=jnp.float32,
        )
    return (grad_in, weight_grad)


def norm_moments(conv_out, pixel_count):
    center = lax.psum(jnp.sum(conv_out, axis=(0, 1, 2, 3)), ("dp", "rows")) / pixel_count
    spread = (
        lax.psum(jnp.sum(jnp.square(conv_out - center), axis=(0, 1, 2, 3)), ("dp", "rows"))
        / pixel_count
    )
    return (center, lax.rsqrt(spread + eps))


def section_forward(section_input, carried, positions, params, stats, pixel_count):
    trunk_maps, gain_rows, bias_rows, down_maps, upward_maps, task_maps = params
    hidden = section_input[None]
    layers = []
    moments = []
    for section_layer in range(2):
        conv_out, padded = conv_forward(hidden, trunk_maps[section_layer][None])
        if stats is None:
            center, inverse_std = norm_moments(conv_out, pixel_count)
        else:
            center, inverse_std = stats[section_layer]
        normed = (conv_out - center) * inverse_std
        preact = gain_rows[section_layer] * normed + bias_rows[section_layer]
        layers.append((padded, normed, preact))
        moments.append((center, inverse_std))
        hidden = jax.nn.silu(preact).astype(jnp.bfloat16)
    mixture = (hidden.astype(jnp.float32) + carried.astype(jnp.float32)).astype(jnp.bfloat16)
    inner_act = jnp.einsum(
        "tsrwc,tca->tsrwa", mixture, down_maps, preferred_element_type=jnp.float32
    )
    active_mask_flag = jax.nn.silu(inner_act).astype(jnp.bfloat16)
    class_logits = jnp.einsum(
        "zfhpv,zvm->zfhpm", active_mask_flag, upward_maps, preferred_element_type=jnp.float32
    )
    gating = jax.nn.sigmoid(class_logits)
    product = (gating * hidden.astype(jnp.float32)).astype(jnp.bfloat16)
    features, padded_task = conv_forward(product, task_maps)
    return {
        "layers": layers,
        "moments": moments,
        "shared": hidden,
        "mixture": mixture,
        "inner_act": inner_act,
        "active": active_mask_flag,
        "gating": gating,
        "padded_task": padded_task,
        "features": features,
        "section_input": section_input,
        "carried": carried,
        "positions": positions,
    }


def heads_backward(saved_record, grad_feats, params, wanted):
    down_maps, upward_maps, task_maps = (params[3], params[4], params[5])
    task_back, task_slope = conv_backward(
        saved_record["padded_task"], grad_feats, task_maps, wanted
    )
    shared = saved_record["shared"].astype(jnp.float32)
    gating = saved_record["gating"]
    logits_gradient = (task_back * shared * gating * (1.0 - gating)).astype(jnp.bfloat16)
    grad_active = jnp.einsum(
        "qubef,qxf->qubex", logits_gradient, upward_maps, preferred_element_type=jnp.float32
    )
    grad_inner = (grad_active * silu_slope(saved_record["inner_act"])).astype(jnp.bfloat16)
    grad_mixture = jnp.einsum(
        "tsrwa,tca->tsrwc", grad_inner, down_maps, preferred_element_type=jnp.float32
    )
    through = task_back * gating + grad_mixture
    slopes = None
    if wanted:
        slope_up = jnp.einsum(
            "munfg,munfq->mgq",
            saved_record["active"],
            logits_gradient,
            preferred_element_type=jnp.float32,
        )
        slope_down = jnp.einsum(
            "tsrwc,tsrwa->tca",
            saved_record["mixture"],
            grad_inner,
            preferred_element_type=jnp.float32,
        )
        slopes = (slope_down, slope_up, task_slope)
    return (through, grad_mixture, slopes)


def trunk_backward(saved_record, grad_shared, params, pixel_count):
    trunk_maps, gain_rows = (params[0], params[1])
    grad_hidden = grad_shared
    conv_grads = [None, None]
    gain_grads = [None, None]
    bias_grads = [None, None]
    for section_layer in (1, 0):
        padded, normed, preact = saved_record["layers"][section_layer]
        inverse_std = saved_record["moments"][section_layer][1]
        grad_pre = grad_hidden * silu_slope(preact)
        bias_part = jnp.sum(grad_pre, axis=(0, 1, 2, 3))
        gain_part = jnp.sum(grad_pre * normed, axis=(0, 1, 2, 3))
        bias_total, gain_total = lax.psum((bias_part, gain_part), ("dp", "rows"))
        grad_conv = (
            inverse_std
            * gain_rows[section_layer]
            * (grad_pre - bias_total / pixel_count - normed * gain_total / pixel_count)
        )
        grad_hidden, weight_grad = conv_backward(
            padded, grad_conv.astype(jnp.bfloat16), trunk_maps[section_layer][None], True
        )
        conv_grads[section_layer] = weight_grad[0]
        gain_grads[section_layer] = gain_part
        bias_grads[section_layer] = bias_part
    return (grad_hidden, jnp.stack(conv_grads), jnp.stack(gain_grads), jnp.stack(bias_grads))


def solve_small(matrix, right_side):
    cofactor = [
        [
            matrix[1, 1] * matrix[2, 2] - matrix[1, 2] * matrix[2, 1],
            matrix[1, 2] * matrix[2, 0] - matrix[1, 0] * matrix[2, 2],
            matrix[1, 0] * matrix[2, 1] - matrix[1, 1] * matrix[2, 0],
        ],
        [
            matrix[0, 2] * matrix[2, 1] - matrix[0, 1] * matrix[2, 2],
            matrix[0, 0] * matrix[2, 2] - matrix[0, 2] * matrix[2, 0],
            matrix[0, 1] * matrix[2, 0] - matrix[0, 0] * matrix[2, 1],
        ],
        [
            matrix[0, 1] * matrix[1, 2] - matrix[0, 2] * matrix[1, 1],
            matrix[0, 2] * matrix[1, 0] - matrix[0, 0] * matrix[1, 2],
            matrix[0, 0] * matrix[1, 1] - matrix[0, 1] * matrix[1, 0],
        ],
    ]
    determinant = (
        matrix[0, 0] * cofactor[0][0]
        + matrix[0, 1] * cofactor[0][1]
        + matrix[0, 2] * cofactor[0][2]
    )
    answer = [
        (
            cofactor[0][col_index] * right_side[0]
            + cofactor[1][col_index] * right_side[1]
            + cofactor[2][col_index] * right_side[2]
        )
        / determinant
        for col_index in range(3)
    ]
    return jnp.stack(answer)


def nash_solve(gram_sum):
    trace_mean = (gram_sum[0, 0] + gram_sum[1, 1] + gram_sum[2, 2]) / 3.0 + 1e-06
    normalized = gram_sum / trace_mean
    diagonal = jnp.stack([normalized[0, 0], normalized[1, 1], normalized[2, 2]])
    nash_alpha = lax.rsqrt(diagonal + 1e-06)
    for sweep_index in range(NASH_ITERS):
        residual = jnp.sum(normalized * nash_alpha[None, :], axis=1) - 1.0 / nash_alpha
        curvature = normalized + jnp.diag(1.0 / (nash_alpha * nash_alpha))
        update = solve_small(curvature, residual)
        nash_alpha = nash_alpha * jnp.exp(-0.5 * jnp.tanh(update / nash_alpha))
    return nash_alpha


def on_device(
    x_in,
    pool_index,
    task_mask,
    task_cot,
    trunk_conv,
    norm_gain,
    norm_bias,
    att_down,
    attention_up_weights,
    task_conv,
):
    micro_count = x_in.shape[0]
    tasks_n = task_cot.shape[0]
    decoder_side = lax.axis_index("pipe") == 1
    pixel_count = (
        x_in.shape[1] * x_in.shape[2] * x_in.shape[3] * lax.axis_size("dp") * lax.axis_size("rows")
    )
    pieces = (
        lax.all_gather(trunk_conv, ("dp", "rows"), axis=2, tiled=True),
        lax.all_gather(norm_gain, ("dp", "rows"), axis=2, tiled=True),
        lax.all_gather(norm_bias, ("dp", "rows"), axis=2, tiled=True),
        lax.all_gather(att_down, ("dp", "rows"), axis=2, tiled=True),
        lax.all_gather(attention_up_weights, ("dp", "rows"), axis=3, tiled=True),
        lax.all_gather(task_conv, ("dp", "rows"), axis=2, tiled=True),
    )
    params = (
        pieces[0][0],
        pieces[1][0].astype(jnp.float32),
        pieces[2][0].astype(jnp.float32),
        pieces[3][0],
        pieces[4][0],
        pieces[5][0],
    )
    onehot = (pool_index[..., None] == jnp.arange(4, dtype=jnp.int32)).astype(jnp.float32)
    mask_weights = jnp.transpose(task_mask, (0, 2, 1)).astype(jnp.float32)
    no_carry = jnp.zeros((tasks_n,) + x_in.shape[1:], jnp.bfloat16)
    incoming = jnp.zeros(
        (tasks_n + 1, x_in.shape[1], x_in.shape[2] // 2, x_in.shape[3] // 2, x_in.shape[4]),
        jnp.bfloat16,
    )
    records = []
    for period in range(micro_count + 1):
        enc_index = min(period, micro_count - 1)
        dec_index = max(period - 1, 0)
        positions = jnp.where(decoder_side, onehot[dec_index], onehot[enc_index])
        section_input = jnp.where(
            decoder_side, unpool_cells(incoming[0], positions).astype(jnp.bfloat16), x_in[enc_index]
        )
        carried = jnp.where(
            decoder_side, unpool_cells(incoming[1:], positions).astype(jnp.bfloat16), no_carry
        )
        saved_record = section_forward(section_input, carried, positions, params, None, pixel_count)
        records.append(saved_record)
        if period < micro_count:
            outgoing = jnp.concatenate(
                [
                    pool_cells(saved_record["shared"], positions),
                    pool_cells(saved_record["features"].astype(jnp.bfloat16), positions),
                ],
                axis=0,
            )
            incoming = from_behind(outgoing.astype(jnp.bfloat16), "pipe", 1)
    kept_records = []
    gram_sum = jnp.zeros((tasks_n, tasks_n), jnp.float32)
    for micro_index in range(micro_count):
        source_input = choose_side(decoder_side, records[micro_index + 1], records[micro_index])
        chosen = section_forward(
            source_input["section_input"],
            source_input["carried"],
            source_input["positions"],
            params,
            source_input["moments"],
            pixel_count,
        )
        kept_records.append(chosen)
        plain_cot = task_cot[:, micro_index] * mask_weights[micro_index][:, :, None, None, None]
        through, unused_mixture, unused_slopes = heads_backward(
            chosen, plain_cot.astype(jnp.bfloat16), params, False
        )
        flattened = through.reshape(tasks_n, -1)
        partial_gram = jnp.dot(flattened, flattened.T, precision=lax.Precision.HIGHEST)
        gram_sum = gram_sum + jnp.where(decoder_side, partial_gram, 0.0)
    gram_sum = lax.psum(gram_sum, ("pipe", "dp", "rows"))
    nash_alpha = nash_solve(gram_sum)
    returning = jnp.zeros_like(incoming)
    start_grads = []
    trunk_sum, gain_sum, bias_sum = (0.0, 0.0, 0.0)
    down_sum, up_sum, task_sum = (0.0, 0.0, 0.0)
    for period in range(micro_count + 1):
        dec_index = max(micro_count - 1 - period, 0)
        enc_index = min(micro_count - period, micro_count - 1)
        active_flag = 1.0 if period < micro_count else 0.0
        chosen = choose_side(decoder_side, kept_records[dec_index], kept_records[enc_index])
        positions = chosen["positions"]
        weighted = (
            nash_alpha[:, None, None, None, None]
            * mask_weights[dec_index][:, :, None, None, None]
            * task_cot[:, dec_index].astype(jnp.float32)
            * active_flag
        )
        grad_feats = jnp.where(
            decoder_side, weighted, unpool_cells(returning[1:], positions)
        ).astype(jnp.bfloat16)
        through, grad_mixture, slopes = heads_backward(chosen, grad_feats, params, True)
        down_sum = down_sum + slopes[0]
        up_sum = up_sum + slopes[1]
        task_sum = task_sum + slopes[2]
        pooled_back = jnp.where(decoder_side, 0.0, unpool_cells(returning[0:1], positions))
        grad_shared = jnp.sum(through, axis=0, keepdims=True) + pooled_back
        grad_start, conv_grads, gain_grads, bias_grads = trunk_backward(
            chosen, grad_shared, params, pixel_count
        )
        start_grads.append(grad_start[0])
        trunk_sum = trunk_sum + conv_grads
        gain_sum = gain_sum + gain_grads
        bias_sum = bias_sum + bias_grads
        if period < micro_count:
            outgoing = jnp.concatenate(
                [pool_cells(grad_start, positions), pool_cells(grad_mixture, positions)], axis=0
            )
            returning = from_behind(outgoing.astype(jnp.bfloat16), "pipe", -1)
    features_out = jnp.stack(
        [
            jnp.where(
                decoder_side, records[micro_index + 1]["features"], records[micro_index]["features"]
            )
            for micro_index in range(micro_count)
        ],
        axis=1,
    ).astype(jnp.bfloat16)
    grads_out = jnp.stack(
        [
            jnp.where(
                decoder_side,
                start_grads[micro_count - 1 - micro_index],
                start_grads[micro_count - micro_index],
            )
            for micro_index in range(micro_count)
        ],
        axis=0,
    )
    shares = (
        lax.psum_scatter(trunk_sum[None], ("dp", "rows"), scatter_dimension=2, tiled=True),
        lax.psum_scatter(gain_sum[None], ("dp", "rows"), scatter_dimension=2, tiled=True),
        lax.psum_scatter(bias_sum[None], ("dp", "rows"), scatter_dimension=2, tiled=True),
        lax.psum_scatter(down_sum[None], ("dp", "rows"), scatter_dimension=2, tiled=True),
        lax.psum_scatter(up_sum[None], ("dp", "rows"), scatter_dimension=3, tiled=True),
        lax.psum_scatter(task_sum[None], ("dp", "rows"), scatter_dimension=2, tiled=True),
    )
    return (
        features_out[None],
        grads_out[None],
        shares[0],
        shares[1],
        shares[2],
        shares[3],
        shares[4],
        shares[5],
        nash_alpha,
    )


BF = jnp.bfloat16
F32 = jnp.float32
LANES = 128
TAPS = 9
VMEM_BYTES = 56 * 1024 * 1024


class Line:
    def __init__(self, ids):
        self.ids = ids
        self.last = None


def on_section(body, only):
    if only is None:
        return body

    def gated(ids_ref, *refs):
        @pl.when(ids_ref[2] == only)
        def _():
            body(ids_ref, *refs)

    return gated


def unread(body, count, first):
    def whole(*refs):
        body(*refs[:first], *refs[first + count :])

    return whole


LIGHT = pl.CostEstimate(flops=6_000_000_000, bytes_accessed=1, transcendentals=0)


def kernel_call(body, outs, line, vmem, name, scratch=(), only=None, smem=(), after=()):
    extra = list(after) + ([] if line.last is None else [line.last])
    first = 1 + len(smem) + len(vmem)
    results = pl.pallas_call(
        unread(on_section(body, only), len(extra), first),
        out_shape=[jax.ShapeDtypeStruct(shape, dtype) for shape, dtype in outs],
        in_specs=[pl.BlockSpec(memory_space=pltpu.SMEM)] * (1 + len(smem))
        + [pl.BlockSpec(memory_space=pltpu.VMEM)] * len(vmem)
        + [pl.BlockSpec(memory_space=pl.ANY)] * len(extra),
        out_specs=[pl.BlockSpec(memory_space=pltpu.VMEM)] * len(outs),
        scratch_shapes=list(scratch),
        compiler_params=pltpu.CompilerParams(vmem_limit_bytes=VMEM_BYTES),
        cost_estimate=LIGHT,
        name=name,
    )(line.ids, *smem, *vmem, *extra)
    line.last = results[-1]
    return results


def stepped_call(body, outs, line, vmem, name, scratch=(), only=None, fixed=()):
    extra = [] if line.last is None else [line.last]
    steps = outs[0][0][0]

    def block(shape):
        rest = len(shape) - 1
        return pl.BlockSpec(
            (1,) + tuple(shape[1:]),
            lambda t, ids: (t if only is None else jnp.where(ids[2] == only, t, 0),) + (0,) * rest,
        )

    def same(shape):
        return pl.BlockSpec(shape, lambda t, ids: (0,) * len(shape))

    results = pl.pallas_call(
        unread(on_section(body, only), len(extra), 1 + len(vmem)),
        grid_spec=pltpu.PrefetchScalarGridSpec(
            num_scalar_prefetch=1,
            grid=(steps,),
            in_specs=[same(a.shape) if k in fixed else block(a.shape) for k, a in enumerate(vmem)]
            + [pl.BlockSpec(memory_space=pl.ANY)] * len(extra),
            out_specs=[block(shape) for shape, _ in outs],
            scratch_shapes=list(scratch),
        ),
        out_shape=[jax.ShapeDtypeStruct(shape, dtype) for shape, dtype in outs],
        compiler_params=pltpu.CompilerParams(vmem_limit_bytes=VMEM_BYTES),
        cost_estimate=LIGHT,
        name=name,
    )(line.ids, *vmem, *extra)
    line.last = results[-1]
    return results


class Parts:
    def __init__(self, given, held, given_sems, results, kept, result_sems):
        self.given = [(a, b, given_sems, k) for k, (a, b) in enumerate(zip(given, held))]
        self.results = [(b, a, result_sems, k) for k, (a, b) in enumerate(zip(results, kept))]

    @staticmethod
    def copy(pair, p):
        source, target, sems, k = pair
        if p is None:
            return pltpu.make_async_copy(source, target, sems.at[k, 0])
        return pltpu.make_async_copy(source.at[p], target.at[p], sems.at[k, p])

    def need(self, k, p=None):
        self.copy(self.given[k], p).wait()

    def send(self, k, p=None):
        self.copy(self.results[k], p).start()


def section_call(
    body, outs, line, vmem, name, scratch=(), only=None, other=None, paired=(), split_in=(), split_out=(), smem=()
):
    other, paired = dict(other or {}), dict(paired)
    n_in, n_out = len(vmem), len(outs)
    passed, swapped = list(other.values()), list(paired.values())
    extra = [] if line.last is None else [line.last]

    def whole(*refs):
        scalars, refs = refs[: 1 + len(smem)], refs[1 + len(smem) :]
        ids_ref = scalars[0]
        given, refs = refs[:n_in], refs[n_in:]
        passed_refs, refs = refs[: len(passed)], refs[len(passed) :]
        swapped_refs, refs = refs[: len(swapped)], refs[len(swapped) + len(extra) :]
        results, refs = refs[:n_out], refs[n_out:]
        held, refs = refs[:n_in], refs[n_in:]
        kept, refs = refs[:n_out], refs[n_out:]
        given_sems, result_sems, refs = refs[0], refs[1], refs[2:]

        def run(sources):
            parts = Parts(sources, held, given_sems, results, kept, result_sems)
            for k in range(n_in):
                if k not in split_in:
                    parts.copy(parts.given[k], None).start()
            for p in range(3):
                for k in split_in:
                    parts.copy(parts.given[k], p).start()
            for k in range(n_in):
                if k not in split_in:
                    parts.need(k)
            if split_in or split_out:
                body(*scalars, *held, *kept, *refs, parts=parts)
            else:
                body(*scalars, *held, *kept, *refs)
            for k in range(n_out):
                if k not in split_out:
                    parts.send(k)
            for k in range(n_out):
                if k not in split_out:
                    parts.copy(parts.results[k], None).wait()
            for p in range(3):
                for k in split_out:
                    parts.copy(parts.results[k], p).wait()

        def hand_out():
            for source, target in ((passed_refs, kept), (kept, results)):
                copies = []
                for at, k in enumerate(other):
                    first = source[at] if source is passed_refs else source[k]
                    copies.append(pltpu.make_async_copy(first, target[k], result_sems.at[k, 0]))
                for copy in copies:
                    copy.start()
                for copy in copies:
                    copy.wait()

        if only is not None:
            pl.when(ids_ref[2] == only)(lambda: run(given))
            if passed:
                pl.when(ids_ref[2] != only)(hand_out)
        elif paired:
            mixed = list(given)
            for k, ref in zip(paired, swapped_refs):
                mixed[k] = ref
            pl.when(ids_ref[2] == 0)(lambda: run(given))
            pl.when(ids_ref[2] == 1)(lambda: run(mixed))
        else:
            run(given)

    results = pl.pallas_call(
        whole,
        out_shape=[jax.ShapeDtypeStruct(shape, dtype) for shape, dtype in outs],
        in_specs=[pl.BlockSpec(memory_space=pltpu.SMEM)] * (1 + len(smem))
        + [pl.BlockSpec(memory_space=pl.ANY)] * (n_in + len(passed) + len(swapped) + len(extra)),
        out_specs=[pl.BlockSpec(memory_space=pl.ANY)] * n_out,
        scratch_shapes=[pltpu.VMEM(a.shape, a.dtype) for a in vmem]
        + [pltpu.VMEM(shape, dtype) for shape, dtype in outs]
        + [pltpu.SemaphoreType.DMA((n_in, 3)), pltpu.SemaphoreType.DMA((n_out, 3))]
        + list(scratch),
        compiler_params=pltpu.CompilerParams(vmem_limit_bytes=VMEM_BYTES),
        cost_estimate=LIGHT,
        name=name,
    )(line.ids, *smem, *vmem, *passed, *swapped, *extra)
    line.last = results[-1]
    return results


def anchor(line, arrays, name):
    def body(*refs):
        refs[-1][...] = jnp.zeros((8, LANES), F32)

    line.last = pl.pallas_call(
        body,
        out_shape=jax.ShapeDtypeStruct((8, LANES), F32),
        in_specs=[pl.BlockSpec(memory_space=pl.ANY)] * (len(arrays) + 1),
        out_specs=pl.BlockSpec(memory_space=pltpu.VMEM),
        cost_estimate=LIGHT,
        name=name,
    )(*arrays, line.last)


def trade(pieces, axis, sections):
    count = lax.axis_size(axis)
    taken = [pieces[0]]
    for j in range(1, count):
        pairs = [(p * count + i, p * count + (i ^ j)) for p in sections for i in range(count)]
        taken.append(lax.ppermute(pieces[j], ("pipe", axis), pairs))
    return taken


def swap_sections(pieces):
    count = lax.axis_size("dp")
    return [
        lax.ppermute(
            pieces[j],
            ("pipe", "dp"),
            [(p * count + i, (1 - p) * count + (i ^ j)) for p in range(2) for i in range(count)],
        )
        for j in range(len(pieces))
    ]


def all_of(count, step):
    for i in range(count):
        step(i)


def each(count, step):
    def run(i, carry):
        step(i)
        return carry

    lax.fori_loop(0, count, run, 0)


def span(index, size):
    return pl.ds(pl.multiple_of(index * size, size), size)


def dot(a, b):
    return jnp.dot(a, b, preferred_element_type=F32)


def dot_nt(a, b):
    return lax.dot_general(a, b, (((1,), (1,)), ((), ())), preferred_element_type=F32)


def dot_tn(a, b):
    return lax.dot_general(a, b, (((0,), (0,)), ((), ())), preferred_element_type=F32)


def column_of(shape, cols):
    return lax.broadcasted_iota(jnp.int32, shape, 0) % cols


def fold_taps(taps, cols):
    size = taps.shape[0]
    blank = jnp.zeros((cols, LANES), F32)
    sums = []
    for b in range(3):
        first = taps[:, b * LANES : (b + 1) * LANES]
        second = taps[:, (3 + b) * LANES : (4 + b) * LANES]
        third = taps[:, (6 + b) * LANES : (7 + b) * LANES]
        sums.append(
            second
            + jnp.concatenate([blank, first[: size - cols]], axis=0)
            + jnp.concatenate([third[cols:], blank], axis=0)
        )
    column = column_of((size, LANES), cols)
    left = jnp.where(column == 0, 0.0, pltpu.roll(sums[0], 1, 0))
    right = jnp.where(column == cols - 1, 0.0, pltpu.roll(sums[2], size - 1, 0))
    return sums[1] + left + right


def spread_taps(grad, cols):
    size = grad.shape[0]
    column = column_of((size, LANES), cols)
    moved = [
        jnp.where(column == cols - 1, 0.0, pltpu.roll(grad, size - 1, 0)).astype(BF),
        grad.astype(BF),
        jnp.where(column == 0, 0.0, pltpu.roll(grad, 1, 0)).astype(BF),
    ]
    blank = jnp.zeros((cols, LANES), BF)
    above = [jnp.concatenate([m[cols:], blank], axis=0) for m in moved]
    below = [jnp.concatenate([blank, m[: size - cols]], axis=0) for m in moved]
    return jnp.concatenate(above + moved + below, axis=1)


def cut_weights(line, arrays, name):
    depth = arrays[0][0].shape[1]
    count = sum(len(layers) for _, layers in arrays)

    def body(ids_ref, *refs):
        given, outs = refs[: len(arrays)], refs[len(arrays) :]
        for j in range(4):
            cut = span(ids_ref[0] ^ j, LANES)
            row = 0
            for ref, (_, layers) in zip(given, arrays):
                for n in layers:
                    outs[j][row * depth : (row + 1) * depth, :] = ref[n, :, cut]
                    row += 1

    return kernel_call(
        body, [((count * depth, LANES), BF)] * 4, line, [a for a, _ in arrays], name
    )


def stack_weights(line, pieces, groups, extra, name):
    depth = pieces[0].shape[0] // sum(len(group) for group in groups)
    more = [a for arrays in extra for a in arrays]

    def body(ids_ref, *refs):
        given, more_in, outs = refs[:4], list(refs[4 : 4 + len(more)]), refs[4 + len(more) :]
        for k, group in enumerate(groups):
            for at, n in enumerate(group):
                for j in range(4):
                    rows = span(4 * at + (ids_ref[0] ^ j), depth)
                    outs[k][rows, :] = given[j][n * depth : (n + 1) * depth, :]
            at = 4 * len(group) * depth
            for array in extra[k]:
                outs[k][at : at + array.shape[0], :] = more_in.pop(0)[...]
                at += array.shape[0]

    sizes = [
        4 * len(group) * depth + sum(a.shape[0] for a in extra[k])
        for k, group in enumerate(groups)
    ]
    return kernel_call(
        body, [((n, LANES), BF) for n in sizes], line, list(pieces) + more, name
    )


def place_weights(line, gathered, count, depth, name, norm_rows=0, tail_rows=0):
    whole = 16 * depth
    channels = whole // TAPS
    end = 4 * count * depth
    apart = norm_rows > 0

    def body(ids_ref, g_ref, *rest):
        flat = rest[-1]
        for n in range(count):
            for r in range(4):
                for p in range(4):
                    rows = slice((4 * n + p) * depth, (4 * n + p + 1) * depth)
                    flat[(p * 4 + r) * depth : (p * 4 + r + 1) * depth, :] = g_ref[r, rows, :]
            for tap in range(TAPS):
                lanes = slice(tap * LANES, (tap + 1) * LANES)
                value = flat[tap * channels : (tap + 1) * channels, :]
                if apart:
                    rest[n][0, :, lanes] = value
                else:
                    rest[0][n, :, lanes] = value
        if apart:
            own = [g_ref[r, end : end + norm_rows, :].astype(F32) for r in range(4)]
            rest[count][...] = (own[0] + own[1]) + (own[2] + own[3])
            rest[count + 1][...] = g_ref[:, end + norm_rows : end + norm_rows + tail_rows, :]

    if apart:
        outs = [((1, channels, TAPS * LANES), BF)] * count
        outs += [((norm_rows, LANES), F32), ((4, tail_rows, LANES), BF)]
    else:
        outs = [((count, channels, TAPS * LANES), BF)]
    return kernel_call(
        body, outs, line, [gathered], name, scratch=[pltpu.VMEM((whole, LANES), BF)]
    )


def place_attention(line, pieces, maps, part):
    def body(ids_ref, *refs):
        given, out = refs[:4], refs[4]
        for j in range(4):
            for r in range(4):
                chunk = (ids_ref[0] ^ j) * 4 + r
                for t in range(maps):
                    out[t, span(chunk, part), :] = given[j][r, t * part : (t + 1) * part, :]

    return kernel_call(
        body, [((maps, 16 * part, LANES), BF)], line, list(pieces), "place_attention"
    )[0]


def trunk_layer(
    line, pieces, weight, norms, layer, cols, eps_value, form, last, masked, name, only=None
):
    channels = weight.shape[1]
    size = {"images": 1, "slices": 0.25, "cells": 1}[form]
    size = int(pieces[0].shape[0] * size)
    pixels = 4 * size
    whole_images = form == "images"

    def body(ids_ref, *refs):
        given, (w_ref, norm_ref) = refs[:4], refs[4:6]
        at = 6
        if masked is not None and not whole_images:
            mask_ref = refs[6]
            at = 7
        outs, v_ref, pairs_ref = refs[at:-2], refs[-2], refs[-1]
        field = outs[0]
        for j in range(4):
            peer = ids_ref[0] ^ j
            if whole_images:
                field[span(peer, size), :] = given[j][:, :channels]
                outs[4][span(peer, size), :] = given[j][:, channels:]
            elif form == "cells":
                cells = spread_pairs(given[j][...].astype(F32), pairs_ref, cols)
                field[:, span(peer, LANES)] = cells.astype(BF) * mask_ref[...]
            else:
                field[:, span(peer, LANES)] = given[j][...]

        def convolve(i):
            part = span(i, size)
            v_ref[part, :] = fold_taps(dot(field[part, :], w_ref[0]), cols)

        all_of(4, convolve)
        conv_out = v_ref[...]
        center = jnp.sum(conv_out, axis=0, keepdims=True) / pixels
        moved = conv_out - center
        spread = jnp.sum(moved * moved, axis=0, keepdims=True) / pixels
        inverse = lax.rsqrt(spread + eps_value)
        normed = moved * inverse
        outs[1][...] = normed
        outs[2][...] = jnp.broadcast_to(inverse, (8, LANES))
        preact = norm_ref[layer : layer + 1, :] * normed + norm_ref[2 + layer : 3 + layer, :]
        hidden = (preact * jax.nn.sigmoid(preact)).astype(BF)
        outs[3][...] = hidden
        if last and masked is not None:
            kept = hidden.astype(F32) * mask_ref[...].astype(F32)
            outs[4][...] = pool_pairs(kept, pairs_ref, cols).astype(BF)

    outs = [((pixels, channels), BF), ((pixels, LANES), F32), ((8, LANES), F32)]
    outs.append(((pixels, LANES), BF))
    if last and masked is not None:
        outs.append(((size, LANES), BF))
    elif whole_images:
        outs.append(((pixels, LANES), BF))
    extra = [masked] if masked is not None and not whole_images else []
    return kernel_call(
        body,
        outs,
        line,
        list(pieces) + [weight, norms] + extra,
        name,
        scratch=[pltpu.VMEM((pixels, LANES), F32), pltpu.VMEM((pixels // 2, LANES), F32)],
        only=only,
    )


def pool_pairs(value, pairs_ref, cols):
    size = value.shape[0]
    halves = value.reshape(size // (2 * cols), 2, cols, LANES)
    pairs_ref[: size // 2, :] = (halves[:, 0] + halves[:, 1]).reshape(size // 2, LANES)
    return pairs_ref[pl.ds(0, size // 4, stride=2), :] + pairs_ref[pl.ds(1, size // 4, stride=2), :]


def spread_pairs(small, pairs_ref, cols):
    size = 4 * small.shape[0]
    pairs_ref[pl.ds(0, size // 4, stride=2), :] = small
    pairs_ref[pl.ds(1, size // 4, stride=2), :] = small
    rows = pairs_ref[: size // 2, :].reshape(size // (2 * cols), 1, cols, LANES)
    return jnp.broadcast_to(rows, (size // (2 * cols), 2, cols, LANES)).reshape(size, LANES)


def attend(x, mixture, down, up_t):
    inner = dot(mixture, down)
    active = (inner * jax.nn.sigmoid(inner)).astype(BF)
    gate = jax.nn.sigmoid(dot_nt(active, up_t))
    return inner, active, gate


def label_at(label_ref, ids_ref, device, t):
    return label_ref[(device * 4 + ids_ref[1]) * 3 + t]


def slot_of(label_ref, ids_ref, device, t):
    first = jnp.where(t > 0, label_at(label_ref, ids_ref, device, 0), 0)
    return first + jnp.where(t > 1, label_at(label_ref, ids_ref, device, 1), 0)


def section_tasks(line, labels, x_slices, att, gathered, depth, mask, cots, cols):
    pixels = x_slices[0].shape[0]
    size = pixels // 4
    tasks_n, channels = gathered.shape[1], att.shape[1]
    down, up_t = att[:tasks_n], att[tasks_n:]

    def body(ids_ref, label_ref, *refs):
        x_in, down_ref, up_ref, g_ref, mask_ref, cot_in = refs[:4], *refs[4:8], refs[8:12]
        fields, feats, cells, du, w_ref = refs[12:16], refs[16:20], refs[20], refs[21:25], refs[25]
        x_ref, pairs_ref, flat, u_ref, f_ref, c_ref = refs[26:]
        t = pl.program_id(0)
        for r in range(4):
            for p in range(4):
                flat[(p * 4 + r) * depth : (p * 4 + r + 1) * depth, :] = g_ref[
                    r, 0, p * depth : (p + 1) * depth, :
                ]
        for tap in range(TAPS):
            w_ref[0, :, tap * LANES : (tap + 1) * LANES] = flat[
                tap * channels : (tap + 1) * channels, :
            ]

        @pl.when(ids_ref[2] == 0)
        def _():
            @pl.when(t == 0)
            def _():
                for j in range(4):
                    x_ref[:, span(ids_ref[0] ^ j, LANES)] = x_in[j][...]

            def one_image(i):
                rows = span(ids_ref[0] ^ i, size)
                x = x_ref[rows, :]
                _, _, gate = attend(x, x, down_ref[0], up_ref[0])
                u = (gate * x.astype(F32)).astype(BF)
                u_ref[i] = u
                value = fold_taps(dot(u, w_ref[0]), cols)
                f_ref[i] = value.astype(BF)
                kept = value * mask_ref[rows, :].astype(F32)
                cells[0, span(ids_ref[0] ^ i, size // 4), :] = pool_pairs(
                    kept, pairs_ref, cols
                ).astype(BF)

            all_of(4, one_image)
            for j in range(4):
                fields[j][0] = u_ref[j]
                feats[j][0] = f_ref[j]

        @pl.when(ids_ref[2] == 1)
        def _():
            for j in range(4):
                c_ref[j] = cot_in[j][0]

            def one_image(i):
                @pl.when(label_at(label_ref, ids_ref, ids_ref[0] ^ i, t) == 1)
                def _():
                    u_ref[i] = dot_nt(spread_taps(c_ref[i].astype(F32), cols), w_ref[0]).astype(BF)

            all_of(4, one_image)
            for j in range(4):
                device = ids_ref[0] ^ j

                @pl.when(t == 0)
                def _(j=j):
                    du[j][...] = jnp.zeros_like(du[j])

                @pl.when(label_at(label_ref, ids_ref, device, t) == 1)
                def _(j=j, device=device):
                    du[j][slot_of(label_ref, ids_ref, device, t)] = u_ref[j]

    def step(shape, only=None):
        return pl.BlockSpec(
            (1,) + shape[1:],
            lambda t, ids, _: (t if only is None else jnp.where(ids[2] == only, t, 0),)
            + (0,) * (len(shape) - 1),
        )

    def same(shape):
        return pl.BlockSpec(shape, lambda t, ids, _: (0,) * len(shape))

    outs = [(tasks_n, size, channels)] * 4 + [(tasks_n, size, LANES)] * 5 + [(2, size, channels)] * 4
    outs.append((tasks_n, channels, TAPS * LANES))
    args = list(x_slices) + [down, up_t, gathered, mask] + list(cots)
    results = pl.pallas_call(
        unread(body, 1, 2 + len(args)),
        grid_spec=pltpu.PrefetchScalarGridSpec(
            num_scalar_prefetch=2,
            grid=(tasks_n,),
            in_specs=[same(a.shape) for a in x_slices]
            + [step(down.shape, 0), step(up_t.shape, 0)]
            + [pl.BlockSpec((4, 1, 4 * depth, LANES), lambda t, ids, _: (0, t, 0, 0)), same(mask.shape)]
            + [step(a.shape, 1) for a in cots]
            + [pl.BlockSpec(memory_space=pl.ANY)],
            out_specs=[step(shape, 0) for shape in outs[:9]]
            + [same(shape) for shape in outs[9:13]]
            + [step(outs[13])],
            scratch_shapes=[
                pltpu.VMEM((pixels, channels), BF),
                pltpu.VMEM((size // 2, LANES), F32),
                pltpu.VMEM((TAPS * channels, LANES), BF),
                pltpu.VMEM((4, size, channels), BF),
                pltpu.VMEM((4, size, LANES), BF),
                pltpu.VMEM((4, size, LANES), BF),
            ],
        ),
        out_shape=[jax.ShapeDtypeStruct(shape, BF) for shape in outs],
        compiler_params=pltpu.CompilerParams(vmem_limit_bytes=VMEM_BYTES),
        cost_estimate=LIGHT,
        name="section_tasks",
    )(line.ids, labels, *args, line.last)
    line.last = results[-1]
    return results[:4], results[4:8], results[8], results[9:13], results[13]


def grads_of_taps(field, grad_ref, taps_ref, flat, out_at, cols, depth):
    size = taps_ref.shape[0] // 4
    channels = field.shape[1]

    def spread(i):
        part = span(i, size)
        taps_ref[part, :] = spread_taps(grad_ref[part, :].astype(F32), cols)

    if grad_ref is not None:
        all_of(4, spread)

    def row_of_taps(row):
        whole = dot_tn(field[...], taps_ref[:, span(row, 3 * LANES)])
        for b in range(3):
            flat[span(3 * row + b, channels), :] = whole[:, b * LANES : (b + 1) * LANES].astype(BF)

    all_of(3, row_of_taps)

    def keep(r):
        out = out_at(r)
        for p in range(4):
            out[p] = flat[span(p * 4 + r, depth), :]

    all_of(4, keep)


def trunk_grads(line, enc_pairs, dec_pairs, depth, cols, name):
    count = len(enc_pairs)
    pixels, channels = enc_pairs[0][0].shape
    enc_in = [a for pair in enc_pairs for a in pair]
    dec_in = [a for pair in dec_pairs for a in pair]

    def body(ids_ref, *refs):
        given, out, taps_ref, flat = refs[: 2 * count], *refs[2 * count :]
        for n in range(count):
            h_ref, g_ref = given[2 * n], given[2 * n + 1]
            grads_of_taps(
                h_ref,
                g_ref,
                taps_ref,
                flat,
                lambda r: out.at[r, n],
                cols,
                depth,
            )

    return section_call(
        body,
        [((4, count, 4, depth, LANES), BF)],
        line,
        enc_in,
        name,
        scratch=[
            pltpu.VMEM((pixels, TAPS * LANES), BF),
            pltpu.VMEM((TAPS * channels, LANES), BF),
        ],
        paired=enumerate(dec_in),
    )[0]


def dec_task_grads(line, dec_xs, q_cells, mask, att, cots, enc_grads, depth, cols):
    tasks_n, size, _ = q_cells[0].shape
    pixels, channels = 4 * size, att.shape[1]

    def body(ids_ref, *refs, parts):
        x_in, q_in, mask_ref, att_ref, cot_in = refs[:4], refs[4:8], refs[8], refs[9], refs[10:14]
        u_ref, out, taps_ref, flat, x_ref, s_ref, pairs_ref, g_ref, field_ref = refs[14:]
        for j in range(4):
            x_ref[:, span(ids_ref[0] ^ j, LANES)] = x_in[j][...]

        def task(t):
            for j in range(4):
                g_ref[j * size : (j + 1) * size, :] = cot_in[j][t]

            def one_image(i):
                image = ids_ref[0] ^ i
                rows = span(image, size)
                x_low = x_ref[rows, :]
                x = x_low.astype(F32)
                own = mask_ref[rows, :]
                for j in range(4):
                    kept = q_in[j][t, span(image, size // 4), :].astype(F32)
                    cells = spread_pairs(kept, pairs_ref, cols)
                    s_ref[:, span(ids_ref[0] ^ j, LANES)] = cells.astype(BF) * own
                mixture = (x + s_ref[...].astype(F32)).astype(BF)
                _, _, gate = attend(x_low, mixture, att_ref[t], att_ref[tasks_n + t])
                field_ref[span(i, size), :] = (gate * x).astype(BF)

            all_of(4, one_image)
            u_ref[t] = field_ref[...]
            parts.send(0, t)
            grads_of_taps(field_ref, g_ref, taps_ref, flat, lambda r: out.at[r, t], cols, depth)

        each(tasks_n, task)

    return section_call(
        body,
        [((tasks_n, pixels, channels), BF), ((4, tasks_n, 4, depth, LANES), BF)],
        line,
        list(dec_xs) + list(q_cells) + [mask, att] + list(cots),
        "dec_task_grads",
        scratch=[
            pltpu.VMEM((pixels, TAPS * LANES), BF),
            pltpu.VMEM((TAPS * channels, LANES), BF),
            pltpu.VMEM((pixels, channels), BF),
            pltpu.VMEM((size, channels), BF),
            pltpu.VMEM((size // 2, LANES), F32),
            pltpu.VMEM((pixels, LANES), BF),
            pltpu.VMEM((pixels, channels), BF),
        ],
        only=1,
        other={1: enc_grads},
        split_out=(0,),
    )


def enc_tasks_reverse(line, labels, grad_pieces, fields, weights, mask, depth, cols):
    tasks_n, given_size, _ = grad_pieces[0].shape
    channels = weights.shape[1]
    size = 4 * given_size
    pixels = 4 * size

    def body(ids_ref, label_ref, *refs, parts):
        given, u_in, w_ref, mask_ref, outs = refs[:4], refs[4:8], refs[8], refs[9], refs[10:14]
        grads, pairs_ref, taps_ref, flat, whole, g_ref, back_ref = refs[14:]
        for j in range(4):
            outs[j][1] = jnp.zeros((size, channels), BF)
        def task(t):
            parts.need(8, t)
            for j in range(4):
                rows = slice(j * size, (j + 1) * size)
                cells = spread_pairs(given[j][t].astype(F32), pairs_ref, cols)
                g_ref[rows, :] = cells.astype(BF) * mask_ref[span(ids_ref[0] ^ j, size), :]
                parts.need(4 + j, t)
                whole[rows, :] = u_in[j][t]

            def spread(i):
                part = span(i, size)
                taps_ref[part, :] = spread_taps(g_ref[part, :].astype(F32), cols)
                device = ids_ref[0] ^ i

                @pl.when(label_at(label_ref, ids_ref, device, t) == 1)
                def _():
                    back_ref[i] = dot_nt(taps_ref[part, :], w_ref[t]).astype(BF)

            all_of(4, spread)
            for j in range(4):
                device = ids_ref[0] ^ j

                @pl.when(label_at(label_ref, ids_ref, device, t) == 1)
                def _(j=j, device=device):
                    outs[j][slot_of(label_ref, ids_ref, device, t)] = back_ref[j]

            grads_of_taps(whole, None, taps_ref, flat, lambda r: grads.at[r, t], cols, depth)

        each(tasks_n, task)

    return section_call(
        body,
        [((2, size, channels), BF)] * 4 + [((4, tasks_n, 4, depth, LANES), BF)],
        line,
        list(grad_pieces) + list(fields) + [weights, mask],
        "enc_tasks_back",
        scratch=[
            pltpu.VMEM((size // 2, LANES), F32),
            pltpu.VMEM((pixels, TAPS * LANES), BF),
            pltpu.VMEM((TAPS * channels, LANES), BF),
            pltpu.VMEM((pixels, channels), BF),
            pltpu.VMEM((pixels, LANES), BF),
            pltpu.VMEM((4, size, channels), BF),
        ],
        only=0,
        split_in=range(4, 9),
        smem=[labels],
    )


def dec_task_layer(line, fields, weights, enc_feats, cols, name):
    tasks_n, channels, _ = weights.shape
    size = fields.shape[1] // 4

    def body(ids_ref, u_ref, w_ref, *rest, parts):
        outs, all_ref = rest[:4], rest[4]

        def task(t):
            parts.need(1, t)
            parts.need(0, t)

            def convolve(i):
                value = dot(u_ref[t, span(i, size), :], w_ref[t])
                all_ref[i] = fold_taps(value, cols).astype(BF)

            all_of(4, convolve)
            for j in range(4):
                outs[j][t] = all_ref[j]

        each(tasks_n, task)

    return section_call(
        body,
        [((tasks_n, size, LANES), BF)] * 4,
        line,
        [fields, weights],
        name,
        scratch=[pltpu.VMEM((4, size, LANES), BF)],
        only=1,
        other=enumerate(enc_feats),
        split_in=(0, 1),
    )


def heads_reverse(line, labels, x_pieces, carried, mask, du_pieces, att, cols, name, only, other=None):
    size = x_pieces[0].shape[0] // 4
    channels = att.shape[1]
    tasks_n = att.shape[0] // 2
    carry = carried is not None

    def body(ids_ref, label_ref, *refs):
        x_in, rest = refs[:4], refs[4:]
        if carry:
            q_in, mask_ref, rest = rest[:4], rest[4], rest[5:]
        du_in, att_ref, rest = rest[:4], rest[4], rest[5:]
        outs, (x_ref, s_ref, ds_ref, da_ref, pairs_ref) = rest[:-5], rest[-5:]
        dx_ref, g_ref, grads = outs[0], outs[1], outs[2:6]
        for j in range(4):
            x_ref[:, span(ids_ref[0] ^ j, LANES)] = x_in[j][span(ids_ref[0], size), :]

        def task(t):
            x_low = x_ref[...]
            x = x_low.astype(F32)
            slot = slot_of(label_ref, ids_ref, ids_ref[0], t)
            if carry:
                own = mask_ref[span(ids_ref[0], size), :]
                for j in range(4):
                    kept = q_in[j][t, span(ids_ref[0], size // 4), :].astype(F32)
                    cells = spread_pairs(kept, pairs_ref, cols)
                    s_ref[:, span(ids_ref[0] ^ j, LANES)] = cells.astype(BF) * own
                mixture = (x + s_ref[...].astype(F32)).astype(BF)
            else:
                mixture = x_low
            inner, active, gate = attend(x, mixture, att_ref[t], att_ref[tasks_n + t])
            du = (
                (du_in[0][slot].astype(F32) + du_in[1][slot].astype(F32))
                + (du_in[2][slot].astype(F32) + du_in[3][slot].astype(F32))
            )
            gated = du * gate
            do = (gated * x * (1.0 - gate)).astype(BF)
            sig = jax.nn.sigmoid(inner)
            dk = (dot(do, att_ref[tasks_n + t]) * (sig * (1.0 + inner * (1.0 - sig)))).astype(BF)
            ds = dot_nt(dk, att_ref[t])
            dx_ref[t] = gated + ds
            if carry:
                ds_ref[...] = ds
                for j in range(4):
                    kept = ds_ref[:, span(ids_ref[0] ^ j, LANES)] * own.astype(F32)
                    outs[6 + j][t] = pool_pairs(kept, pairs_ref, cols).astype(BF)
            for row, value in ((t, dot_tn(mixture, dk)), (tasks_n + t, dot_tn(do, active))):
                da_ref[...] = value
                for j in range(4):
                    grads[j][row] = da_ref[span(ids_ref[0] ^ j, LANES), :].astype(BF)

        def no_task(t):
            dx_ref[t] = jnp.zeros((size, channels), F32)
            for j in range(4):
                if carry:
                    outs[6 + j][t] = jnp.zeros((size // 4, LANES), BF)
                grads[j][t] = jnp.zeros((LANES, LANES), BF)
                grads[j][tasks_n + t] = jnp.zeros((LANES, LANES), BF)

        def either(t):
            label = label_at(label_ref, ids_ref, ids_ref[0], t)
            pl.when(label == 1)(functools.partial(task, t))
            pl.when(label != 1)(functools.partial(no_task, t))

        each(tasks_n, either)
        row = 0
        g_ref[...] = jnp.zeros_like(g_ref)
        for a in range(tasks_n):
            for b in range(a, tasks_n):
                line_sum = jnp.sum(dx_ref[a] * dx_ref[b], axis=0, keepdims=True)
                folded = line_sum[:, :LANES]
                for part in range(1, channels // LANES):
                    folded = folded + line_sum[:, part * LANES : (part + 1) * LANES]
                g_ref[row : row + 1, :] = folded
                row += 1

    outs = [((tasks_n, size, channels), F32), ((8, LANES), F32)]
    outs += [((2 * tasks_n, LANES, LANES), BF)] * 4
    if carry:
        outs += [((tasks_n, size // 4, LANES), BF)] * 4
    return section_call(
        body,
        outs,
        line,
        list(x_pieces) + (list(carried) + [mask] if carry else []) + list(du_pieces) + [att],
        name,
        scratch=[
            pltpu.VMEM((size, channels), BF),
            pltpu.VMEM((size, channels), BF),
            pltpu.VMEM((size, channels), F32),
            pltpu.VMEM((channels, LANES), F32),
            pltpu.VMEM((size // 2, LANES), F32),
        ],
        only=only,
        other=other,
        smem=[labels],
    )


def nash_values(lines, tasks_n):
    def full(row):
        return jnp.broadcast_to(jnp.sum(lines[row : row + 1, :], axis=1, keepdims=True), (8, LANES))

    gram = [[None] * tasks_n for _ in range(tasks_n)]
    row = 0
    for a in range(tasks_n):
        for b in range(a, tasks_n):
            gram[a][b] = gram[b][a] = full(row)
            row += 1
    trace_mean = (gram[0][0] + gram[1][1] + gram[2][2]) / 3.0 + 1e-06
    norm = [[gram[a][b] / trace_mean for b in range(3)] for a in range(3)]
    alpha = [lax.rsqrt(norm[a][a] + 1e-06) for a in range(3)]
    for _ in range(NASH_ITERS):
        right = [
            norm[a][0] * alpha[0] + norm[a][1] * alpha[1] + norm[a][2] * alpha[2] - 1.0 / alpha[a]
            for a in range(3)
        ]
        matrix = [
            [norm[a][b] + 1.0 / (alpha[a] * alpha[a]) if a == b else norm[a][b] for b in range(3)]
            for a in range(3)
        ]
        cof = [[None] * 3 for _ in range(3)]
        for a in range(3):
            for b in range(3):
                a1, a2, b1, b2 = (a + 1) % 3, (a + 2) % 3, (b + 1) % 3, (b + 2) % 3
                cof[a][b] = matrix[a1][b1] * matrix[a2][b2] - matrix[a1][b2] * matrix[a2][b1]
        determinant = (
            matrix[0][0] * cof[0][0] + matrix[0][1] * cof[0][1] + matrix[0][2] * cof[0][2]
        )
        update = [
            (cof[0][b] * right[0] + cof[1][b] * right[1] + cof[2][b] * right[2]) / determinant
            for b in range(3)
        ]
        alpha = [alpha[a] * jnp.exp(-0.5 * jnp.tanh(update[a] / alpha[a])) for a in range(3)]
    return alpha


def weigh(line, dx, w_or_lines, solve, name):
    tasks_n, size, channels = dx.shape

    def body(ids_ref, *refs):
        given, dx_ref, outs, total = refs[: len(w_or_lines)], refs[len(w_or_lines)], refs[-6:-1], refs[-1]
        if solve:
            lines = (given[0][0] + given[0][1]) + (given[0][2] + given[0][3])
            alpha = nash_values(lines, tasks_n)
            outs[0][...] = jnp.concatenate(
                [alpha[t][:1] for t in range(3)] + [jnp.zeros((5, LANES), F32)], axis=0
            )
        else:
            outs[0][...] = given[0][...]
        acc = None
        for t in range(tasks_n):
            scale = jnp.tile(outs[0][t : t + 1, :], (1, channels // LANES))
            term = dx_ref[t] * scale
            acc = term if acc is None else acc + term
        total[...] = acc
        for j in range(4):
            outs[1 + j][...] = total[:, span(ids_ref[0] ^ j, LANES)].astype(BF)

    return kernel_call(
        body,
        [((8, LANES), F32)] + [((size, LANES), BF)] * 4,
        line,
        list(w_or_lines) + [dx],
        name,
        scratch=[pltpu.VMEM((size, channels), F32)],
    )


def trunk_reverse(
    line, pieces, by_image, cells, mask, normed, inverse, norms, layer, weight, cols, parts, other, name, only
):
    pixels = normed.shape[0]
    size = pixels // 4
    channels = weight.shape[1]
    takes, gives = cells is not None, "cells" in parts
    shapes = {"slices": (pixels, LANES), "images": (size, channels), "cells": (size, LANES)}

    def body(ids_ref, *refs):
        given, rest = refs[:4], refs[4:]
        if takes:
            cells_in, rest = rest[:4], rest[4:]
        if takes or gives:
            mask_ref, rest = rest[0], rest[1:]
        (n_ref, inv_ref, norm_ref, w_ref), rest = rest[:4], rest[4:]
        if other is not None:
            other_in, rest = rest[:4], rest[4:]
        outs, (acc_ref, back_ref, pairs_ref) = rest[:-3], rest[-3:]
        gain = norm_ref[layer : layer + 1, :]

        @pl.when(ids_ref[2] == only)
        def _():
            if by_image:
                for j in range(4):
                    acc_ref[span(ids_ref[0] ^ j, size), :] = given[j][...].astype(F32)
            else:
                acc_ref[...] = (given[0][...].astype(F32) + given[1][...].astype(F32)) + (
                    given[2][...].astype(F32) + given[3][...].astype(F32)
                )
            grad = acc_ref[...]
            if takes:
                start = (cells_in[0][...].astype(F32) + cells_in[1][...].astype(F32)) + (
                    cells_in[2][...].astype(F32) + cells_in[3][...].astype(F32)
                )
                start = start.astype(BF).astype(F32)
                grad = grad + spread_pairs(start, pairs_ref, cols) * mask_ref[...].astype(F32)
            normed_value = n_ref[...]
            preact = gain * normed_value + norm_ref[2 + layer : 3 + layer, :]
            sig = jax.nn.sigmoid(preact)
            dp = grad * (sig * (1.0 + preact * (1.0 - sig)))
            bias_total = jnp.sum(dp, axis=0, keepdims=True)
            gain_total = jnp.sum(dp * normed_value, axis=0, keepdims=True)
            outs[1][...] = jnp.concatenate(
                [gain_total, bias_total, jnp.zeros((6, LANES), F32)], axis=0
            )
            scale = inv_ref[0:1, :] * gain
            dv = scale * (dp - bias_total / pixels - normed_value * (gain_total / pixels))
            outs[0][...] = dv.astype(BF)
            acc_ref[...] = dv.astype(BF).astype(F32)

            def convolve(i):
                part = span(i, size)
                back_ref[part, :] = dot_nt(spread_taps(acc_ref[part, :], cols), w_ref[0])

            all_of(4, convolve)
            for at, kind in enumerate(parts):
                for j in range(4):
                    peer = ids_ref[0] ^ j
                    out = outs[2 + 4 * at + j]
                    if kind == "images":
                        out[...] = back_ref[span(peer, size), :].astype(BF)
                    elif kind == "slices":
                        out[...] = back_ref[:, span(peer, LANES)].astype(BF)
                    else:
                        kept = back_ref[:, span(peer, LANES)] * mask_ref[...].astype(F32)
                        out[...] = pool_pairs(kept, pairs_ref, cols).astype(BF)

        if other is not None:

            @pl.when(ids_ref[2] != only)
            def _():
                for j in range(4):
                    outs[2 + 4 * parts.index("images") + j][...] = other_in[j][...]

    outs = [((pixels, LANES), BF), ((8, LANES), F32)]
    for kind in parts:
        outs += [(shapes[kind], BF)] * 4
    extra = list(cells) if takes else []
    if takes or gives:
        extra.append(mask)
    return kernel_call(
        body,
        outs,
        line,
        list(pieces) + extra + [normed, inverse, norms, weight] + list(other or []),
        name,
        scratch=[
            pltpu.VMEM((pixels, LANES), F32),
            pltpu.VMEM((pixels, channels), F32),
            pltpu.VMEM((pixels // 2, LANES), F32),
        ],
    )


def plane_device(
    x_in,
    pool_index,
    task_mask,
    task_cot,
    trunk_conv,
    norm_gain,
    norm_bias,
    att_down,
    attention_up_weights,
    task_conv,
):
    micro_count, _, rows_n, cols, channels = x_in.shape
    tasks_n = task_cot.shape[0]
    strip = rows_n * cols
    size = strip * micro_count
    depth = trunk_conv.shape[2]
    part = att_down.shape[2]
    section = lax.axis_index("pipe")
    decoder = section == 1
    row_at = lax.axis_index("rows")
    line = Line(jnp.stack([lax.axis_index("dp"), row_at, section]).astype(jnp.int32))
    ENC, DEC, BOTH = (0,), (1,), (0, 1)

    norm_own = jnp.concatenate([norm_gain[0], norm_bias[0]], axis=0)
    own_lanes = jnp.arange(LANES) // part == row_at
    norm_own = jnp.where(own_lanes[None], jnp.tile(norm_own, (1, LANES // part)), 0).astype(BF)
    norm_own = jnp.pad(norm_own, ((0, 12), (0, 0)))
    att_own = jnp.concatenate(
        [att_down[0], jnp.swapaxes(attention_up_weights[0], 1, 2)], axis=0
    ).reshape(2 * tasks_n * part, LANES)

    trunk_cut = trade(cut_weights(line, [(trunk_conv[0], [0, 1])], "cut_trunk"), "dp", BOTH)

    labels = lax.all_gather(task_mask, "dp").reshape(-1)

    picked = pool_index[:, 0, :, None, :, None]
    place = jnp.arange(2)[:, None, None] * 2 + jnp.arange(2)[None, None, :]
    cells = (picked == place[None, None]).astype(BF)
    cells = jnp.broadcast_to(cells.reshape(micro_count, strip, 1), (micro_count, strip, LANES))
    strips = x_in.reshape(micro_count, strip, channels)

    def cut_input(ids_ref, x_ref, m_ref, *outs):
        for j in range(4):
            outs[j][:, :channels] = x_ref[ids_ref[1] ^ j]
            outs[j][:, channels:] = m_ref[ids_ref[1] ^ j]

    strips = kernel_call(
        cut_input, [((strip, channels + LANES), BF)] * 4, line, [strips, cells], "cut_input"
    )
    strips = trade(strips, "rows", BOTH)

    trunk_block = stack_weights(line, trunk_cut, [[0, 1]], [[norm_own, att_own]], "stack_trunk")[0]
    trunk_all = lax.all_gather(trunk_block, "rows")

    def place_input(ids_ref, a, b, c, e, o_ref):
        for j, piece in enumerate((a, b, c, e)):
            o_ref[span(ids_ref[1] ^ j, strip), :] = piece[...]

    x_image = kernel_call(
        place_input, [((size, channels + LANES), BF)], line, strips, "place_input"
    )[0]
    x_images = trade([x_image] * 4, "dp", ENC)
    task_cut = trade(
        cut_weights(line, [(task_conv[0], range(tasks_n))], "cut_tasks"), "dp", BOTH
    )
    anchor(line, x_images, "input_there")
    task_block = stack_weights(line, task_cut, [list(range(tasks_n))], [[]], "stack_tasks")[0]
    task_all = lax.all_gather(task_block, "rows")

    half = channels // 2

    def cut_cot(ids_ref, mask_ref, c_ref, *outs):
        for j in range(4):
            micro = ids_ref[1] ^ j
            for t in range(tasks_n):
                labelled = mask_ref[micro * tasks_n + t].astype(F32)
                value = c_ref[t, micro, :, span(ids_ref[2], half)].astype(F32)
                outs[j][t] = (value * labelled).astype(BF)

    cot_strips = kernel_call(
        cut_cot,
        [((tasks_n, strip, half), BF)] * 4,
        line,
        [task_cot.reshape(tasks_n, micro_count, strip, channels)],
        "cut_cotangents",
        smem=[task_mask.reshape(-1)],
    )
    cot_strips = trade(cot_strips, "rows", BOTH)

    def place_cot(ids_ref, _, a, b, c, e, o_ref):
        for j, piece in enumerate((a, b, c, e)):
            for t in range(tasks_n):
                o_ref[t, span(ids_ref[1] ^ j, strip), :] = piece[t]

    cot_half = kernel_call(
        place_cot, [((tasks_n, size, half), BF)], line, cot_strips, "place_cotangents", smem=[labels]
    )[0]
    cot_other = swap_sections([cot_half])[0]

    def slice_cot(ids_ref, own_ref, other_ref, *rest):
        outs, image = rest[:4], rest[4]
        image[:, :, :half] = other_ref[...]
        image[:, :, half:] = own_ref[...]
        for j in range(4):
            outs[j][...] = image[:, :, span(ids_ref[0] ^ j, LANES)]

    cots = kernel_call(
        slice_cot,
        [((tasks_n, size, LANES), BF)] * 4,
        line,
        [cot_half, cot_other],
        "slice_cotangents",
        scratch=[pltpu.VMEM((tasks_n, size, channels), BF)],
    )
    cots = trade(cots, "dp", DEC)
    first_w, second_w, norms, att_rows = place_weights(
        line, trunk_all, 2, depth, "place_trunk", norm_own.shape[0], att_own.shape[0]
    )
    enc_h0, enc_n1, enc_i1, enc_h, mask = trunk_layer(
        line, x_images, first_w, norms, 0, cols, eps, "images", False, None, "enc_layer1", 0
    )
    enc_hs = trade([enc_h] * 4, "dp", BOTH)
    dec_mask = swap_sections([mask])[0]
    att = place_attention(line, trade([att_rows] * 4, "dp", BOTH), 2 * tasks_n, part)
    anchor(line, cots, "cotangents_there")
    enc_h1, enc_n2, enc_i2, enc_x, z = trunk_layer(
        line, enc_hs, second_w, norms, 1, cols, eps, "slices", True, mask, "enc_layer2", 0
    )
    z_pieces = swap_sections([z] * 4)
    enc_xs = trade([enc_x] * 4, "dp", ENC)

    dec_h0, dec_n1, dec_i1, dec_h = trunk_layer(
        line, z_pieces, first_w, norms, 0, cols, eps, "cells", False, dec_mask, "dec_layer1", 1
    )
    dec_hs = trade([dec_h] * 4, "dp", DEC)

    dec_h1, dec_n2, dec_i2, dec_x = trunk_layer(
        line, dec_hs, second_w, norms, 1, cols, eps, "slices", True, None, "dec_layer2", 1
    )
    dec_xs = trade([dec_x] * 4, "dp", BOTH)

    gathered = task_all.reshape(4, tasks_n, 4 * depth, LANES)
    enc_us, enc_feats, kept, du, task_w = section_tasks(
        line, labels, enc_xs, att, gathered, depth, mask, cots, cols
    )
    anchor(line, dec_xs, "decoder_there")
    dec_du = trade(du, "dp", DEC)
    q_cells = swap_sections([kept] * 4)

    dec_dx, lines, *rest = heads_reverse(
        line, labels, dec_xs, q_cells, dec_mask, dec_du, att, cols, "dec_heads", 1
    )
    dec_att, ds = rest[:4], rest[4:]
    ds = swap_sections(ds)
    lines = jnp.sum(lax.all_gather(lines, "dp"), axis=0)
    terms = lax.all_gather(lines, "rows")
    dec_w, *dh = weigh(line, dec_dx, [terms], True, "bargain")
    dh = trade(dh, "dp", BOTH)
    enc_w = swap_sections([dec_w])[0]
    nash_w = jnp.where(decoder, dec_w, enc_w)

    anchor(line, dh, "bargain_there")
    *du, enc_dw = enc_tasks_reverse(
        line, labels, ds, enc_us, task_w, mask, depth, cols
    )
    enc_du = trade(du, "dp", ENC)
    dec_dv2, dec_s2, *dh = trunk_reverse(
        line, dh, True, None, None, dec_n2, dec_i2, norms, 1, second_w, cols, ["slices"], None, "dec_back2", 1
    )
    dh = trade(dh, "dp", DEC)
    dec_u, task_dw = dec_task_grads(
        line, dec_xs, q_cells, dec_mask, att, cots, enc_dw, depth, cols
    )
    task_dw = lax.psum_scatter(task_dw, "rows", scatter_dimension=0, tiled=True)
    dec_dv1, dec_s1, *rest = trunk_reverse(
        line, dh, False, None, dec_mask, dec_n1, dec_i1, norms, 0, first_w, cols, ["cells", "images"], None, "dec_back1", 1
    )
    dec_start, dec_dz = swap_sections(rest[:4]), rest[4:]
    enc_dx, _, *att_parts = heads_reverse(
        line, labels, enc_xs, None, None, enc_du, att, cols, "enc_heads_back", 0, {k + 2: a for k, a in enumerate(dec_att)}
    )
    _, *dh = weigh(line, enc_dx, [enc_w], False, "enc_weigh")
    dh = trade(dh, "dp", BOTH)
    att_parts = trade(att_parts, "dp", BOTH)

    feats = dec_task_layer(line, dec_u, task_w, enc_feats, cols, "dec_tasks")
    feats = trade(feats, "dp", BOTH)
    enc_dv2, enc_s2, *dh = trunk_reverse(
        line, dh, True, dec_start, mask, enc_n2, enc_i2, norms, 1, second_w, cols, ["slices"], None, "enc_back2", 0
    )
    dh = trade(dh, "dp", ENC)

    enc_dv1, enc_s1, *dz = trunk_reverse(
        line, dh, False, None, None, enc_n1, enc_i1, norms, 0, first_w, cols, ["images"], dec_dz, "enc_back1", 0
    )
    dz = trade(dz, "dp", BOTH)
    trunk_dw = trunk_grads(
        line,
        [(enc_h0, enc_dv1), (enc_h1, enc_dv2)],
        [(dec_h0, dec_dv1), (dec_h1, dec_dv2)],
        depth,
        cols,
        "trunk_grads",
    )
    trunk_dw = lax.psum_scatter(trunk_dw, "rows", scatter_dimension=0, tiled=True)


    def cut_shares(sums, name):
        count = sums.shape[1]

        def cut(ids_ref, g_ref, *outs):
            for j in range(4):
                for n in range(count):
                    outs[j][n] = g_ref[0, n, ids_ref[0] ^ j]

        return kernel_call(cut, [((count, depth, LANES), BF)] * 4, line, [sums], name)

    def join(layers, scale, name):
        counts = [pieces[0].shape[0] for pieces in layers]

        def body(ids_ref, *refs):
            o_ref, at = refs[-1], 0
            for m, count in enumerate(counts):
                for n in range(count):
                    for j in range(4):
                        value = refs[4 * m + j][n].astype(F32)
                        if scale is not None:
                            value = value * refs[4 * len(counts)][n : n + 1, :]
                        o_ref[at, :, span(ids_ref[0] ^ j, LANES)] = value
                    at += 1

        return kernel_call(
            body,
            [((sum(counts), depth, channels), F32)],
            line,
            [piece for pieces in layers for piece in pieces] + ([] if scale is None else [scale]),
            name,
        )[0]

    def cut_att(ids_ref, a, b, c, e, *rest):
        outs, total = rest[:4], rest[4]
        total[...] = (a[...].astype(F32) + b[...].astype(F32)) + (
            c[...].astype(F32) + e[...].astype(F32)
        )
        for j in range(4):
            outs[j][...] = total[:, span(ids_ref[1] ^ j, part), :].astype(BF)

    att_parts = kernel_call(
        cut_att,
        [((2 * tasks_n, part, LANES), BF)] * 4,
        line,
        att_parts,
        "cut_attention",
        scratch=[pltpu.VMEM((2 * tasks_n, LANES, LANES), F32)],
    )
    att_parts = trade(att_parts, "rows", BOTH)

    def cut_feats(ids_ref, a, b, c, e, *rest):
        outs, image = rest[:4], rest[4]
        for j, piece in enumerate((a, b, c, e)):
            image[:, :, span(ids_ref[0] ^ j, LANES)] = piece[...]
        for j in range(4):
            outs[j][...] = image[:, span(ids_ref[1] ^ j, strip), :]

    feats = kernel_call(
        cut_feats,
        [((tasks_n, strip, channels), BF)] * 4,
        line,
        feats,
        "cut_features",
        scratch=[pltpu.VMEM((tasks_n, size, channels), BF)],
    )
    feats = trade(feats, "rows", BOTH)

    sums = jnp.where(
        decoder, jnp.concatenate([dec_s1, dec_s2]), jnp.concatenate([enc_s1, enc_s2])
    )
    sums = trade([sums] * 4, "rows", BOTH)
    sums = (sums[0] + sums[1]) + (sums[2] + sums[3])
    sums = lax.dynamic_slice_in_dim(sums, row_at * part, part, axis=1)
    gain_out = jnp.stack([sums[0], sums[8]])
    bias_out = jnp.stack([sums[1], sums[9]])

    def cut_start(ids_ref, a, b, c, e, *rest):
        outs, image = rest[:4], rest[4]
        image[...] = (a[...].astype(F32) + b[...].astype(F32)) + (
            c[...].astype(F32) + e[...].astype(F32)
        )
        for j in range(4):
            outs[j][...] = image[span(ids_ref[1] ^ j, strip), :].astype(BF)

    starts = kernel_call(
        cut_start,
        [((strip, channels), BF)] * 4,
        line,
        dz,
        "cut_start",
        scratch=[pltpu.VMEM((size, channels), F32)],
    )
    starts = trade(starts, "rows", BOTH)

    task_parts = trade(cut_shares(task_dw, "share_tasks"), "dp", BOTH)

    def join_att(ids_ref, a, b, c, e, w_ref, o_ref):
        total = (a[...].astype(F32) + b[...].astype(F32)) + (
            c[...].astype(F32) + e[...].astype(F32)
        )
        for t in range(2 * tasks_n):
            at = t % tasks_n
            o_ref[t] = total[t] * w_ref[at : at + 1, :]

    att_out = kernel_call(
        join_att,
        [((2 * tasks_n, part, LANES), F32)],
        line,
        att_parts + [nash_w],
        "join_attention",
    )[0]

    task_out = join([task_parts], nash_w, "join_tasks")
    trunk_parts = trade(cut_shares(trunk_dw, "share_trunk"), "dp", BOTH)

    def place_feats(ids_ref, a, b, c, e, o_ref):
        for j, piece in enumerate((a, b, c, e)):
            for t in range(tasks_n):
                o_ref[t, ids_ref[1] ^ j] = piece[t]

    feats_out = kernel_call(
        place_feats, [((tasks_n, micro_count, strip, channels), BF)], line, feats, "place_features"
    )[0]

    def place_start(ids_ref, a, b, c, e, o_ref):
        for j, piece in enumerate((a, b, c, e)):
            o_ref[ids_ref[1] ^ j] = piece[...].astype(F32)

    start_out = kernel_call(
        place_start, [((micro_count, strip, channels), F32)], line, starts, "place_start"
    )[0]
    trunk_out = join([trunk_parts], None, "join_trunk")

    return (
        feats_out.reshape(1, tasks_n, micro_count, 1, rows_n, cols, channels),
        start_out.reshape(1, micro_count, 1, rows_n, cols, channels),
        trunk_out[None],
        gain_out[None],
        bias_out[None],
        att_out[:tasks_n][None],
        jnp.swapaxes(att_out[tasks_n:], 1, 2)[None],
        task_out[None],
        nash_w[:3, 0],
    )


def by_planes(x_in, task_cot):
    peers, planes = lax.axis_size("dp"), lax.axis_size("rows")
    micro, samples, _, _, channels = x_in.shape
    return (
        peers == 4
        and planes == 4
        and micro == planes
        and samples == 1
        and channels == peers * LANES
        and task_cot.shape[0] == 3
    )


def section_device(*arrays):
    if by_planes(arrays[0], arrays[3]):
        return plane_device(*arrays)
    return on_device(*arrays)


def solution(mesh):
    in_specs = (
        P(None, "dp", "rows", None, None),
        P(None, "dp", "rows", None),
        P(None, "dp", None),
        P(None, None, "dp", "rows", None, None),
        P("pipe", None, ("dp", "rows"), None),
        P("pipe", None, ("dp", "rows")),
        P("pipe", None, ("dp", "rows")),
        P("pipe", None, ("dp", "rows"), None),
        P("pipe", None, None, ("dp", "rows")),
        P("pipe", None, ("dp", "rows"), None),
    )
    out_specs = (
        P("pipe", None, None, "dp", "rows", None, None),
        P("pipe", None, "dp", "rows", None, None),
        P("pipe", None, ("dp", "rows"), None),
        P("pipe", None, ("dp", "rows")),
        P("pipe", None, ("dp", "rows")),
        P("pipe", None, ("dp", "rows"), None),
        P("pipe", None, None, ("dp", "rows")),
        P("pipe", None, ("dp", "rows"), None),
        P(),
    )
    return jax.shard_map(
        section_device, mesh=mesh, in_specs=in_specs, out_specs=out_specs, check_vma=False
    )
```

```python
import functools

import jax
import jax.numpy as jnp
from jax import lax
from jax.experimental import pallas as pl
from jax.experimental.pallas import tpu as pltpu
from jax.sharding import PartitionSpec as P

NASH_ITERS = 3


eps = 1e-05


def extended_2(array, sides, width):
    for axis, dim in sides:
        peers, length = (lax.axis_size(axis), array.shape[dim])
        up = [(i, (i + 1) % peers) for i in range(peers - 1)]
        down = [(j, i) for i, j in up]
        last = lax.slice_in_dim(array, length - width, length, axis=dim)
        first = lax.slice_in_dim(array, 0, width, axis=dim)
        before = lax.ppermute(last, axis, up)
        after = lax.ppermute(first, axis, down)
        array = jnp.concatenate([before, array, after], axis=dim)
    return array


def from_behind(array, axis, by):
    peers = lax.axis_size(axis)
    pairs = [(i, i + by) for i in range(peers) if 0 <= i + by < peers]
    return lax.ppermute(array, axis, pairs)


def silu_slope(preact):
    sigmoid_val = jax.nn.sigmoid(preact)
    return sigmoid_val * (1.0 + preact * (1.0 - sigmoid_val))


def choose_side(condition, when_true, when_false):

    def either(true_leaf, false_leaf):
        return jnp.where(condition, true_leaf, false_leaf)

    return jax.tree.map(either, when_true, when_false)


def pool_cells(field, positions):
    leading = field.shape[:-4]
    samples, rows_n, cols_n, channels = field.shape[-4:]
    blocks = field.astype(jnp.float32).reshape(
        leading + (samples, rows_n // 2, 2, cols_n // 2, 2, channels)
    )
    blocks = jnp.moveaxis(blocks, -4, -3).reshape(
        leading + (samples, rows_n // 2, cols_n // 2, 4, channels)
    )
    return jnp.sum(blocks * positions[..., None], axis=-2)


def unpool_cells(small, positions):
    leading = small.shape[:-4]
    samples, rows_h, cols_h, channels = small.shape[-4:]
    blocks = small.astype(jnp.float32)[..., None, :] * positions[..., None]
    blocks = blocks.reshape(leading + (samples, rows_h, cols_h, 2, 2, channels))
    blocks = jnp.moveaxis(blocks, -3, -4)
    return blocks.reshape(leading + (samples, 2 * rows_h, 2 * cols_h, channels))


def gather_taps(padded, rows_n, cols_n):
    stencil = [
        padded[:, :, offset // 3 : offset // 3 + rows_n, offset % 3 : offset % 3 + cols_n, :]
        for offset in range(9)
    ]
    return jnp.concatenate(stencil, axis=-1)


def conv_forward(field, weight):
    extended = extended_2(field, (("rows", 2),), 1)
    padded = jnp.pad(extended, ((0, 0), (0, 0), (0, 0), (1, 1), (0, 0)))
    stencil = gather_taps(padded, field.shape[2], field.shape[3])
    conv_out = jnp.einsum("ksrwq,kqd->ksrwd", stencil, weight, preferred_element_type=jnp.float32)
    return (conv_out, padded)


def conv_backward(padded, grad_out, weight, wanted):
    rows_n, cols_n = (grad_out.shape[2], grad_out.shape[3])
    extended = extended_2(grad_out, (("rows", 2),), 1)
    beside_all = jnp.pad(extended, ((0, 0), (0, 0), (0, 0), (1, 1), (0, 0)))
    flipped = jnp.stack(
        [
            beside_all[
                :,
                :,
                2 - offset // 3 : 2 - offset // 3 + rows_n,
                2 - offset % 3 : 2 - offset % 3 + cols_n,
                :,
            ]
            for offset in range(9)
        ],
        axis=-2,
    )
    kernel = weight.reshape(weight.shape[0], 9, weight.shape[2], weight.shape[2])
    grad_in = jnp.einsum("ksrwtd,ktcd->ksrwc", flipped, kernel, preferred_element_type=jnp.float32)
    weight_grad = None
    if wanted:
        weight_grad = jnp.einsum(
            "ksrwq,ksrwd->kqd",
            gather_taps(padded, rows_n, cols_n),
            grad_out,
            preferred_element_type=jnp.float32,
        )
    return (grad_in, weight_grad)


def norm_moments(conv_out, pixel_count):
    center = lax.psum(jnp.sum(conv_out, axis=(0, 1, 2, 3)), ("dp", "rows")) / pixel_count
    spread = (
        lax.psum(jnp.sum(jnp.square(conv_out - center), axis=(0, 1, 2, 3)), ("dp", "rows"))
        / pixel_count
    )
    return (center, lax.rsqrt(spread + eps))


def section_forward(section_input, carried, positions, params, stats, pixel_count):
    trunk_maps, gain_rows, bias_rows, down_maps, upward_maps, task_maps = params
    hidden = section_input[None]
    layers = []
    moments = []
    for section_layer in range(2):
        conv_out, padded = conv_forward(hidden, trunk_maps[section_layer][None])
        if stats is None:
            center, inverse_std = norm_moments(conv_out, pixel_count)
        else:
            center, inverse_std = stats[section_layer]
        normed = (conv_out - center) * inverse_std
        preact = gain_rows[section_layer] * normed + bias_rows[section_layer]
        layers.append((padded, normed, preact))
        moments.append((center, inverse_std))
        hidden = jax.nn.silu(preact).astype(jnp.bfloat16)
    mixture = (hidden.astype(jnp.float32) + carried.astype(jnp.float32)).astype(jnp.bfloat16)
    inner_act = jnp.einsum(
        "tsrwc,tca->tsrwa", mixture, down_maps, preferred_element_type=jnp.float32
    )
    active_mask_flag = jax.nn.silu(inner_act).astype(jnp.bfloat16)
    class_logits = jnp.einsum(
        "zfhpv,zvm->zfhpm", active_mask_flag, upward_maps, preferred_element_type=jnp.float32
    )
    gating = jax.nn.sigmoid(class_logits)
    product = (gating * hidden.astype(jnp.float32)).astype(jnp.bfloat16)
    features, padded_task = conv_forward(product, task_maps)
    return {
        "layers": layers,
        "moments": moments,
        "shared": hidden,
        "mixture": mixture,
        "inner_act": inner_act,
        "active": active_mask_flag,
        "gating": gating,
        "padded_task": padded_task,
        "features": features,
        "section_input": section_input,
        "carried": carried,
        "positions": positions,
    }


def heads_backward(saved_record, grad_feats, params, wanted):
    down_maps, upward_maps, task_maps = (params[3], params[4], params[5])
    task_back, task_slope = conv_backward(
        saved_record["padded_task"], grad_feats, task_maps, wanted
    )
    shared = saved_record["shared"].astype(jnp.float32)
    gating = saved_record["gating"]
    logits_gradient = (task_back * shared * gating * (1.0 - gating)).astype(jnp.bfloat16)
    grad_active = jnp.einsum(
        "qubef,qxf->qubex", logits_gradient, upward_maps, preferred_element_type=jnp.float32
    )
    grad_inner = (grad_active * silu_slope(saved_record["inner_act"])).astype(jnp.bfloat16)
    grad_mixture = jnp.einsum(
        "tsrwa,tca->tsrwc", grad_inner, down_maps, preferred_element_type=jnp.float32
    )
    through = task_back * gating + grad_mixture
    slopes = None
    if wanted:
        slope_up = jnp.einsum(
            "munfg,munfq->mgq",
            saved_record["active"],
            logits_gradient,
            preferred_element_type=jnp.float32,
        )
        slope_down = jnp.einsum(
            "tsrwc,tsrwa->tca",
            saved_record["mixture"],
            grad_inner,
            preferred_element_type=jnp.float32,
        )
        slopes = (slope_down, slope_up, task_slope)
    return (through, grad_mixture, slopes)


def trunk_backward(saved_record, grad_shared, params, pixel_count):
    trunk_maps, gain_rows = (params[0], params[1])
    grad_hidden = grad_shared
    conv_grads = [None, None]
    gain_grads = [None, None]
    bias_grads = [None, None]
    for section_layer in (1, 0):
        padded, normed, preact = saved_record["layers"][section_layer]
        inverse_std = saved_record["moments"][section_layer][1]
        grad_pre = grad_hidden * silu_slope(preact)
        bias_part = jnp.sum(grad_pre, axis=(0, 1, 2, 3))
        gain_part = jnp.sum(grad_pre * normed, axis=(0, 1, 2, 3))
        bias_total, gain_total = lax.psum((bias_part, gain_part), ("dp", "rows"))
        grad_conv = (
            inverse_std
            * gain_rows[section_layer]
            * (grad_pre - bias_total / pixel_count - normed * gain_total / pixel_count)
        )
        grad_hidden, weight_grad = conv_backward(
            padded, grad_conv.astype(jnp.bfloat16), trunk_maps[section_layer][None], True
        )
        conv_grads[section_layer] = weight_grad[0]
        gain_grads[section_layer] = gain_part
        bias_grads[section_layer] = bias_part
    return (grad_hidden, jnp.stack(conv_grads), jnp.stack(gain_grads), jnp.stack(bias_grads))


def solve_small(matrix, right_side):
    cofactor = [
        [
            matrix[1, 1] * matrix[2, 2] - matrix[1, 2] * matrix[2, 1],
            matrix[1, 2] * matrix[2, 0] - matrix[1, 0] * matrix[2, 2],
            matrix[1, 0] * matrix[2, 1] - matrix[1, 1] * matrix[2, 0],
        ],
        [
            matrix[0, 2] * matrix[2, 1] - matrix[0, 1] * matrix[2, 2],
            matrix[0, 0] * matrix[2, 2] - matrix[0, 2] * matrix[2, 0],
            matrix[0, 1] * matrix[2, 0] - matrix[0, 0] * matrix[2, 1],
        ],
        [
            matrix[0, 1] * matrix[1, 2] - matrix[0, 2] * matrix[1, 1],
            matrix[0, 2] * matrix[1, 0] - matrix[0, 0] * matrix[1, 2],
            matrix[0, 0] * matrix[1, 1] - matrix[0, 1] * matrix[1, 0],
        ],
    ]
    determinant = (
        matrix[0, 0] * cofactor[0][0]
        + matrix[0, 1] * cofactor[0][1]
        + matrix[0, 2] * cofactor[0][2]
    )
    answer = [
        (
            cofactor[0][col_index] * right_side[0]
            + cofactor[1][col_index] * right_side[1]
            + cofactor[2][col_index] * right_side[2]
        )
        / determinant
        for col_index in range(3)
    ]
    return jnp.stack(answer)


def nash_solve(gram_sum):
    trace_mean = (gram_sum[0, 0] + gram_sum[1, 1] + gram_sum[2, 2]) / 3.0 + 1e-06
    normalized = gram_sum / trace_mean
    diagonal = jnp.stack([normalized[0, 0], normalized[1, 1], normalized[2, 2]])
    nash_alpha = lax.rsqrt(diagonal + 1e-06)
    for sweep_index in range(NASH_ITERS):
        residual = jnp.sum(normalized * nash_alpha[None, :], axis=1) - 1.0 / nash_alpha
        curvature = normalized + jnp.diag(1.0 / (nash_alpha * nash_alpha))
        update = solve_small(curvature, residual)
        nash_alpha = nash_alpha * jnp.exp(-0.5 * jnp.tanh(update / nash_alpha))
    return nash_alpha


def on_device(
    x_in,
    pool_index,
    task_mask,
    task_cot,
    trunk_conv,
    norm_gain,
    norm_bias,
    att_down,
    attention_up_weights,
    task_conv,
):
    micro_count = x_in.shape[0]
    tasks_n = task_cot.shape[0]
    decoder_side = lax.axis_index("pipe") == 1
    pixel_count = (
        x_in.shape[1] * x_in.shape[2] * x_in.shape[3] * lax.axis_size("dp") * lax.axis_size("rows")
    )
    pieces = (
        lax.all_gather(trunk_conv, ("dp", "rows"), axis=2, tiled=True),
        lax.all_gather(norm_gain, ("dp", "rows"), axis=2, tiled=True),
        lax.all_gather(norm_bias, ("dp", "rows"), axis=2, tiled=True),
        lax.all_gather(att_down, ("dp", "rows"), axis=2, tiled=True),
        lax.all_gather(attention_up_weights, ("dp", "rows"), axis=3, tiled=True),
        lax.all_gather(task_conv, ("dp", "rows"), axis=2, tiled=True),
    )
    params = (
        pieces[0][0],
        pieces[1][0].astype(jnp.float32),
        pieces[2][0].astype(jnp.float32),
        pieces[3][0],
        pieces[4][0],
        pieces[5][0],
    )
    onehot = (pool_index[..., None] == jnp.arange(4, dtype=jnp.int32)).astype(jnp.float32)
    mask_weights = jnp.transpose(task_mask, (0, 2, 1)).astype(jnp.float32)
    no_carry = jnp.zeros((tasks_n,) + x_in.shape[1:], jnp.bfloat16)
    incoming = jnp.zeros(
        (tasks_n + 1, x_in.shape[1], x_in.shape[2] // 2, x_in.shape[3] // 2, x_in.shape[4]),
        jnp.bfloat16,
    )
    records = []
    for period in range(micro_count + 1):
        enc_index = min(period, micro_count - 1)
        dec_index = max(period - 1, 0)
        positions = jnp.where(decoder_side, onehot[dec_index], onehot[enc_index])
        section_input = jnp.where(
            decoder_side, unpool_cells(incoming[0], positions).astype(jnp.bfloat16), x_in[enc_index]
        )
        carried = jnp.where(
            decoder_side, unpool_cells(incoming[1:], positions).astype(jnp.bfloat16), no_carry
        )
        saved_record = section_forward(section_input, carried, positions, params, None, pixel_count)
        records.append(saved_record)
        if period < micro_count:
            outgoing = jnp.concatenate(
                [
                    pool_cells(saved_record["shared"], positions),
                    pool_cells(saved_record["features"].astype(jnp.bfloat16), positions),
                ],
                axis=0,
            )
            incoming = from_behind(outgoing.astype(jnp.bfloat16), "pipe", 1)
    kept_records = []
    gram_sum = jnp.zeros((tasks_n, tasks_n), jnp.float32)
    for micro_index in range(micro_count):
        source_input = choose_side(decoder_side, records[micro_index + 1], records[micro_index])
        chosen = section_forward(
            source_input["section_input"],
            source_input["carried"],
            source_input["positions"],
            params,
            source_input["moments"],
            pixel_count,
        )
        kept_records.append(chosen)
        plain_cot = task_cot[:, micro_index] * mask_weights[micro_index][:, :, None, None, None]
        through, unused_mixture, unused_slopes = heads_backward(
            chosen, plain_cot.astype(jnp.bfloat16), params, False
        )
        flattened = through.reshape(tasks_n, -1)
        partial_gram = jnp.dot(flattened, flattened.T, precision=lax.Precision.HIGHEST)
        gram_sum = gram_sum + jnp.where(decoder_side, partial_gram, 0.0)
    gram_sum = lax.psum(gram_sum, ("pipe", "dp", "rows"))
    nash_alpha = nash_solve(gram_sum)
    returning = jnp.zeros_like(incoming)
    start_grads = []
    trunk_sum, gain_sum, bias_sum = (0.0, 0.0, 0.0)
    down_sum, up_sum, task_sum = (0.0, 0.0, 0.0)
    for period in range(micro_count + 1):
        dec_index = max(micro_count - 1 - period, 0)
        enc_index = min(micro_count - period, micro_count - 1)
        active_flag = 1.0 if period < micro_count else 0.0
        chosen = choose_side(decoder_side, kept_records[dec_index], kept_records[enc_index])
        positions = chosen["positions"]
        weighted = (
            nash_alpha[:, None, None, None, None]
            * mask_weights[dec_index][:, :, None, None, None]
            * task_cot[:, dec_index].astype(jnp.float32)
            * active_flag
        )
        grad_feats = jnp.where(
            decoder_side, weighted, unpool_cells(returning[1:], positions)
        ).astype(jnp.bfloat16)
        through, grad_mixture, slopes = heads_backward(chosen, grad_feats, params, True)
        down_sum = down_sum + slopes[0]
        up_sum = up_sum + slopes[1]
        task_sum = task_sum + slopes[2]
        pooled_back = jnp.where(decoder_side, 0.0, unpool_cells(returning[0:1], positions))
        grad_shared = jnp.sum(through, axis=0, keepdims=True) + pooled_back
        grad_start, conv_grads, gain_grads, bias_grads = trunk_backward(
            chosen, grad_shared, params, pixel_count
        )
        start_grads.append(grad_start[0])
        trunk_sum = trunk_sum + conv_grads
        gain_sum = gain_sum + gain_grads
        bias_sum = bias_sum + bias_grads
        if period < micro_count:
            outgoing = jnp.concatenate(
                [pool_cells(grad_start, positions), pool_cells(grad_mixture, positions)], axis=0
            )
            returning = from_behind(outgoing.astype(jnp.bfloat16), "pipe", -1)
    features_out = jnp.stack(
        [
            jnp.where(
                decoder_side, records[micro_index + 1]["features"], records[micro_index]["features"]
            )
            for micro_index in range(micro_count)
        ],
        axis=1,
    ).astype(jnp.bfloat16)
    grads_out = jnp.stack(
        [
            jnp.where(
                decoder_side,
                start_grads[micro_count - 1 - micro_index],
                start_grads[micro_count - micro_index],
            )
            for micro_index in range(micro_count)
        ],
        axis=0,
    )
    shares = (
        lax.psum_scatter(trunk_sum[None], ("dp", "rows"), scatter_dimension=2, tiled=True),
        lax.psum_scatter(gain_sum[None], ("dp", "rows"), scatter_dimension=2, tiled=True),
        lax.psum_scatter(bias_sum[None], ("dp", "rows"), scatter_dimension=2, tiled=True),
        lax.psum_scatter(down_sum[None], ("dp", "rows"), scatter_dimension=2, tiled=True),
        lax.psum_scatter(up_sum[None], ("dp", "rows"), scatter_dimension=3, tiled=True),
        lax.psum_scatter(task_sum[None], ("dp", "rows"), scatter_dimension=2, tiled=True),
    )
    return (
        features_out[None],
        grads_out[None],
        shares[0],
        shares[1],
        shares[2],
        shares[3],
        shares[4],
        shares[5],
        nash_alpha,
    )


BF = jnp.bfloat16
F32 = jnp.float32
LANES = 128
TAPS = 9
VMEM_BYTES = 56 * 1024 * 1024


class Line:
    def __init__(self, ids):
        self.ids = ids
        self.last = None


def on_section(body, only):
    if only is None:
        return body

    def gated(ids_ref, *refs):
        @pl.when(ids_ref[2] == only)
        def _():
            body(ids_ref, *refs)

    return gated


def unread(body, count, first):
    def whole(*refs):
        body(*refs[:first], *refs[first + count :])

    return whole


LIGHT = pl.CostEstimate(flops=6_000_000_000, bytes_accessed=1, transcendentals=0)


def kernel_call(body, outs, line, vmem, name, scratch=(), only=None, smem=(), after=()):
    extra = list(after) + ([] if line.last is None else [line.last])
    first = 1 + len(smem) + len(vmem)
    results = pl.pallas_call(
        unread(on_section(body, only), len(extra), first),
        out_shape=[jax.ShapeDtypeStruct(shape, dtype) for shape, dtype in outs],
        in_specs=[pl.BlockSpec(memory_space=pltpu.SMEM)] * (1 + len(smem))
        + [pl.BlockSpec(memory_space=pltpu.VMEM)] * len(vmem)
        + [pl.BlockSpec(memory_space=pl.ANY)] * len(extra),
        out_specs=[pl.BlockSpec(memory_space=pltpu.VMEM)] * len(outs),
        scratch_shapes=list(scratch),
        compiler_params=pltpu.CompilerParams(vmem_limit_bytes=VMEM_BYTES),
        cost_estimate=LIGHT,
        name=name,
    )(line.ids, *smem, *vmem, *extra)
    line.last = results[-1]
    return results


def stepped_call(body, outs, line, vmem, name, scratch=(), only=None, fixed=()):
    extra = [] if line.last is None else [line.last]
    steps = outs[0][0][0]

    def block(shape):
        rest = len(shape) - 1
        return pl.BlockSpec(
            (1,) + tuple(shape[1:]),
            lambda t, ids: (t if only is None else jnp.where(ids[2] == only, t, 0),) + (0,) * rest,
        )

    def same(shape):
        return pl.BlockSpec(shape, lambda t, ids: (0,) * len(shape))

    results = pl.pallas_call(
        unread(on_section(body, only), len(extra), 1 + len(vmem)),
        grid_spec=pltpu.PrefetchScalarGridSpec(
            num_scalar_prefetch=1,
            grid=(steps,),
            in_specs=[same(a.shape) if k in fixed else block(a.shape) for k, a in enumerate(vmem)]
            + [pl.BlockSpec(memory_space=pl.ANY)] * len(extra),
            out_specs=[block(shape) for shape, _ in outs],
            scratch_shapes=list(scratch),
        ),
        out_shape=[jax.ShapeDtypeStruct(shape, dtype) for shape, dtype in outs],
        compiler_params=pltpu.CompilerParams(vmem_limit_bytes=VMEM_BYTES),
        cost_estimate=LIGHT,
        name=name,
    )(line.ids, *vmem, *extra)
    line.last = results[-1]
    return results


class Parts:
    def __init__(self, given, held, given_sems, results, kept, result_sems):
        self.given = [(a, b, given_sems, k) for k, (a, b) in enumerate(zip(given, held))]
        self.results = [(b, a, result_sems, k) for k, (a, b) in enumerate(zip(results, kept))]

    @staticmethod
    def copy(pair, p):
        source, target, sems, k = pair
        if p is None:
            return pltpu.make_async_copy(source, target, sems.at[k, 0])
        return pltpu.make_async_copy(source.at[p], target.at[p], sems.at[k, p])

    def need(self, k, p=None):
        self.copy(self.given[k], p).wait()

    def send(self, k, p=None):
        self.copy(self.results[k], p).start()


def section_call(
    body, outs, line, vmem, name, scratch=(), only=None, other=None, paired=(), split_in=(), split_out=(), smem=()
):
    other, paired = dict(other or {}), dict(paired)
    n_in, n_out = len(vmem), len(outs)
    passed, swapped = list(other.values()), list(paired.values())
    extra = [] if line.last is None else [line.last]

    def whole(*refs):
        scalars, refs = refs[: 1 + len(smem)], refs[1 + len(smem) :]
        ids_ref = scalars[0]
        given, refs = refs[:n_in], refs[n_in:]
        passed_refs, refs = refs[: len(passed)], refs[len(passed) :]
        swapped_refs, refs = refs[: len(swapped)], refs[len(swapped) + len(extra) :]
        results, refs = refs[:n_out], refs[n_out:]
        held, refs = refs[:n_in], refs[n_in:]
        kept, refs = refs[:n_out], refs[n_out:]
        given_sems, result_sems, refs = refs[0], refs[1], refs[2:]

        def run(sources):
            parts = Parts(sources, held, given_sems, results, kept, result_sems)
            for k in range(n_in):
                if k not in split_in:
                    parts.copy(parts.given[k], None).start()
            for p in range(3):
                for k in split_in:
                    parts.copy(parts.given[k], p).start()
            for k in range(n_in):
                if k not in split_in:
                    parts.need(k)
            if split_in or split_out:
                body(*scalars, *held, *kept, *refs, parts=parts)
            else:
                body(*scalars, *held, *kept, *refs)
            for k in range(n_out):
                if k not in split_out:
                    parts.send(k)
            for k in range(n_out):
                if k not in split_out:
                    parts.copy(parts.results[k], None).wait()
            for p in range(3):
                for k in split_out:
                    parts.copy(parts.results[k], p).wait()

        def hand_out():
            for source, target in ((passed_refs, kept), (kept, results)):
                copies = []
                for at, k in enumerate(other):
                    first = source[at] if source is passed_refs else source[k]
                    copies.append(pltpu.make_async_copy(first, target[k], result_sems.at[k, 0]))
                for copy in copies:
                    copy.start()
                for copy in copies:
                    copy.wait()

        if only is not None:
            pl.when(ids_ref[2] == only)(lambda: run(given))
            if passed:
                pl.when(ids_ref[2] != only)(hand_out)
        elif paired:
            mixed = list(given)
            for k, ref in zip(paired, swapped_refs):
                mixed[k] = ref
            pl.when(ids_ref[2] == 0)(lambda: run(given))
            pl.when(ids_ref[2] == 1)(lambda: run(mixed))
        else:
            run(given)

    results = pl.pallas_call(
        whole,
        out_shape=[jax.ShapeDtypeStruct(shape, dtype) for shape, dtype in outs],
        in_specs=[pl.BlockSpec(memory_space=pltpu.SMEM)] * (1 + len(smem))
        + [pl.BlockSpec(memory_space=pl.ANY)] * (n_in + len(passed) + len(swapped) + len(extra)),
        out_specs=[pl.BlockSpec(memory_space=pl.ANY)] * n_out,
        scratch_shapes=[pltpu.VMEM(a.shape, a.dtype) for a in vmem]
        + [pltpu.VMEM(shape, dtype) for shape, dtype in outs]
        + [pltpu.SemaphoreType.DMA((n_in, 3)), pltpu.SemaphoreType.DMA((n_out, 3))]
        + list(scratch),
        compiler_params=pltpu.CompilerParams(vmem_limit_bytes=VMEM_BYTES),
        cost_estimate=LIGHT,
        name=name,
    )(line.ids, *smem, *vmem, *passed, *swapped, *extra)
    line.last = results[-1]
    return results


def anchor(line, arrays, name):
    def body(*refs):
        refs[-1][...] = jnp.zeros((8, LANES), F32)

    line.last = pl.pallas_call(
        body,
        out_shape=jax.ShapeDtypeStruct((8, LANES), F32),
        in_specs=[pl.BlockSpec(memory_space=pl.ANY)] * (len(arrays) + 1),
        out_specs=pl.BlockSpec(memory_space=pltpu.VMEM),
        cost_estimate=LIGHT,
        name=name,
    )(*arrays, line.last)


def trade(pieces, axis, sections):
    count = lax.axis_size(axis)
    taken = [pieces[0]]
    for j in range(1, count):
        pairs = [(p * count + i, p * count + (i ^ j)) for p in sections for i in range(count)]
        taken.append(lax.ppermute(pieces[j], ("pipe", axis), pairs))
    return taken


def swap_sections(pieces):
    count = lax.axis_size("dp")
    return [
        lax.ppermute(
            pieces[j],
            ("pipe", "dp"),
            [(p * count + i, (1 - p) * count + (i ^ j)) for p in range(2) for i in range(count)],
        )
        for j in range(len(pieces))
    ]


def all_of(count, step):
    for i in range(count):
        step(i)


def each(count, step):
    def run(i, carry):
        step(i)
        return carry

    lax.fori_loop(0, count, run, 0)


def span(index, size):
    return pl.ds(pl.multiple_of(index * size, size), size)


def dot(a, b):
    return jnp.dot(a, b, preferred_element_type=F32)


def dot_nt(a, b):
    return lax.dot_general(a, b, (((1,), (1,)), ((), ())), preferred_element_type=F32)


def dot_tn(a, b):
    return lax.dot_general(a, b, (((0,), (0,)), ((), ())), preferred_element_type=F32)


def column_of(shape, cols):
    return lax.broadcasted_iota(jnp.int32, shape, 0) % cols


def fold_taps(taps, cols):
    size = taps.shape[0]
    blank = jnp.zeros((cols, LANES), F32)
    sums = []
    for b in range(3):
        first = taps[:, b * LANES : (b + 1) * LANES]
        second = taps[:, (3 + b) * LANES : (4 + b) * LANES]
        third = taps[:, (6 + b) * LANES : (7 + b) * LANES]
        sums.append(
            second
            + jnp.concatenate([blank, first[: size - cols]], axis=0)
            + jnp.concatenate([third[cols:], blank], axis=0)
        )
    column = column_of((size, LANES), cols)
    left = jnp.where(column == 0, 0.0, pltpu.roll(sums[0], 1, 0))
    right = jnp.where(column == cols - 1, 0.0, pltpu.roll(sums[2], size - 1, 0))
    return sums[1] + left + right


def spread_taps(grad, cols):
    size = grad.shape[0]
    column = column_of((size, LANES), cols)
    moved = [
        jnp.where(column == cols - 1, 0.0, pltpu.roll(grad, size - 1, 0)).astype(BF),
        grad.astype(BF),
        jnp.where(column == 0, 0.0, pltpu.roll(grad, 1, 0)).astype(BF),
    ]
    blank = jnp.zeros((cols, LANES), BF)
    above = [jnp.concatenate([m[cols:], blank], axis=0) for m in moved]
    below = [jnp.concatenate([blank, m[: size - cols]], axis=0) for m in moved]
    return jnp.concatenate(above + moved + below, axis=1)


def cut_weights(line, arrays, name):
    depth = arrays[0][0].shape[1]
    count = sum(len(layers) for _, layers in arrays)

    def body(ids_ref, *refs):
        given, outs = refs[: len(arrays)], refs[len(arrays) :]
        for j in range(4):
            cut = span(ids_ref[0] ^ j, LANES)
            row = 0
            for ref, (_, layers) in zip(given, arrays):
                for n in layers:
                    outs[j][row * depth : (row + 1) * depth, :] = ref[n, :, cut]
                    row += 1

    return kernel_call(
        body, [((count * depth, LANES), BF)] * 4, line, [a for a, _ in arrays], name
    )


def stack_weights(line, pieces, groups, extra, name):
    depth = pieces[0].shape[0] // sum(len(group) for group in groups)
    more = [a for arrays in extra for a in arrays]

    def body(ids_ref, *refs):
        given, more_in, outs = refs[:4], list(refs[4 : 4 + len(more)]), refs[4 + len(more) :]
        for k, group in enumerate(groups):
            for at, n in enumerate(group):
                for j in range(4):
                    rows = span(4 * at + (ids_ref[0] ^ j), depth)
                    outs[k][rows, :] = given[j][n * depth : (n + 1) * depth, :]
            at = 4 * len(group) * depth
            for array in extra[k]:
                outs[k][at : at + array.shape[0], :] = more_in.pop(0)[...]
                at += array.shape[0]

    sizes = [
        4 * len(group) * depth + sum(a.shape[0] for a in extra[k])
        for k, group in enumerate(groups)
    ]
    return kernel_call(
        body, [((n, LANES), BF) for n in sizes], line, list(pieces) + more, name
    )


def place_weights(line, gathered, count, depth, name, norm_rows=0, tail_rows=0):
    whole = 16 * depth
    channels = whole // TAPS
    end = 4 * count * depth
    apart = norm_rows > 0

    def body(ids_ref, g_ref, *rest):
        flat = rest[-1]
        for n in range(count):
            for r in range(4):
                for p in range(4):
                    rows = slice((4 * n + p) * depth, (4 * n + p + 1) * depth)
                    flat[(p * 4 + r) * depth : (p * 4 + r + 1) * depth, :] = g_ref[r, rows, :]
            for tap in range(TAPS):
                lanes = slice(tap * LANES, (tap + 1) * LANES)
                value = flat[tap * channels : (tap + 1) * channels, :]
                if apart:
                    rest[n][0, :, lanes] = value
                else:
                    rest[0][n, :, lanes] = value
        if apart:
            own = [g_ref[r, end : end + norm_rows, :].astype(F32) for r in range(4)]
            rest[count][...] = (own[0] + own[1]) + (own[2] + own[3])
            rest[count + 1][...] = g_ref[:, end + norm_rows : end + norm_rows + tail_rows, :]

    if apart:
        outs = [((1, channels, TAPS * LANES), BF)] * count
        outs += [((norm_rows, LANES), F32), ((4, tail_rows, LANES), BF)]
    else:
        outs = [((count, channels, TAPS * LANES), BF)]
    return kernel_call(
        body, outs, line, [gathered], name, scratch=[pltpu.VMEM((whole, LANES), BF)]
    )


def place_attention(line, pieces, maps, part):
    def body(ids_ref, *refs):
        given, out = refs[:4], refs[4]
        for j in range(4):
            for r in range(4):
                chunk = (ids_ref[0] ^ j) * 4 + r
                for t in range(maps):
                    out[t, span(chunk, part), :] = given[j][r, t * part : (t + 1) * part, :]

    return kernel_call(
        body, [((maps, 16 * part, LANES), BF)], line, list(pieces), "place_attention"
    )[0]


def trunk_layer(
    line, pieces, weight, norms, layer, cols, eps_value, form, last, masked, name, only=None
):
    channels = weight.shape[1]
    size = {"images": 1, "slices": 0.25, "cells": 1}[form]
    size = int(pieces[0].shape[0] * size)
    pixels = 4 * size
    whole_images = form == "images"

    def body(ids_ref, *refs):
        given, (w_ref, norm_ref) = refs[:4], refs[4:6]
        at = 6
        if masked is not None and not whole_images:
            mask_ref = refs[6]
            at = 7
        outs, v_ref, pairs_ref = refs[at:-2], refs[-2], refs[-1]
        field = outs[0]
        for j in range(4):
            peer = ids_ref[0] ^ j
            if whole_images:
                field[span(peer, size), :] = given[j][:, :channels]
                outs[4][span(peer, size), :] = given[j][:, channels:]
            elif form == "cells":
                cells = spread_pairs(given[j][...].astype(F32), pairs_ref, cols)
                field[:, span(peer, LANES)] = cells.astype(BF) * mask_ref[...]
            else:
                field[:, span(peer, LANES)] = given[j][...]

        def convolve(i):
            part = span(i, size)
            v_ref[part, :] = fold_taps(dot(field[part, :], w_ref[0]), cols)

        all_of(4, convolve)
        conv_out = v_ref[...]
        center = jnp.sum(conv_out, axis=0, keepdims=True) / pixels
        moved = conv_out - center
        spread = jnp.sum(moved * moved, axis=0, keepdims=True) / pixels
        inverse = lax.rsqrt(spread + eps_value)
        normed = moved * inverse
        outs[1][...] = normed
        outs[2][...] = jnp.broadcast_to(inverse, (8, LANES))
        preact = norm_ref[layer : layer + 1, :] * normed + norm_ref[2 + layer : 3 + layer, :]
        hidden = (preact * jax.nn.sigmoid(preact)).astype(BF)
        outs[3][...] = hidden
        if last and masked is not None:
            kept = hidden.astype(F32) * mask_ref[...].astype(F32)
            outs[4][...] = pool_pairs(kept, pairs_ref, cols).astype(BF)

    outs = [((pixels, channels), BF), ((pixels, LANES), F32), ((8, LANES), F32)]
    outs.append(((pixels, LANES), BF))
    if last and masked is not None:
        outs.append(((size, LANES), BF))
    elif whole_images:
        outs.append(((pixels, LANES), BF))
    extra = [masked] if masked is not None and not whole_images else []
    return kernel_call(
        body,
        outs,
        line,
        list(pieces) + [weight, norms] + extra,
        name,
        scratch=[pltpu.VMEM((pixels, LANES), F32), pltpu.VMEM((pixels // 2, LANES), F32)],
        only=only,
    )


def pool_pairs(value, pairs_ref, cols):
    size = value.shape[0]
    halves = value.reshape(size // (2 * cols), 2, cols, LANES)
    pairs_ref[: size // 2, :] = (halves[:, 0] + halves[:, 1]).reshape(size // 2, LANES)
    return pairs_ref[pl.ds(0, size // 4, stride=2), :] + pairs_ref[pl.ds(1, size // 4, stride=2), :]


def spread_pairs(small, pairs_ref, cols):
    size = 4 * small.shape[0]
    pairs_ref[pl.ds(0, size // 4, stride=2), :] = small
    pairs_ref[pl.ds(1, size // 4, stride=2), :] = small
    rows = pairs_ref[: size // 2, :].reshape(size // (2 * cols), 1, cols, LANES)
    return jnp.broadcast_to(rows, (size // (2 * cols), 2, cols, LANES)).reshape(size, LANES)


def attend(x, mixture, down, up_t):
    inner = dot(mixture, down)
    active = (inner * jax.nn.sigmoid(inner)).astype(BF)
    gate = jax.nn.sigmoid(dot_nt(active, up_t))
    return inner, active, gate


def label_at(label_ref, ids_ref, device, t):
    return label_ref[(device * 4 + ids_ref[1]) * 3 + t]


def slot_of(label_ref, ids_ref, device, t):
    first = jnp.where(t > 0, label_at(label_ref, ids_ref, device, 0), 0)
    return first + jnp.where(t > 1, label_at(label_ref, ids_ref, device, 1), 0)


def section_tasks(line, labels, x_slices, att, gathered, depth, mask, cots, cols):
    pixels = x_slices[0].shape[0]
    size = pixels // 4
    tasks_n, channels = gathered.shape[1], att.shape[1]
    down, up_t = att[:tasks_n], att[tasks_n:]

    def body(ids_ref, label_ref, *refs):
        x_in, down_ref, up_ref, g_ref, mask_ref, cot_in = refs[:4], *refs[4:8], refs[8:12]
        fields, feats, cells, du, w_ref = refs[12:16], refs[16:20], refs[20], refs[21:25], refs[25]
        x_ref, pairs_ref, flat, u_ref, f_ref, c_ref = refs[26:]
        t = pl.program_id(0)
        for r in range(4):
            for p in range(4):
                flat[(p * 4 + r) * depth : (p * 4 + r + 1) * depth, :] = g_ref[
                    r, 0, p * depth : (p + 1) * depth, :
                ]
        for tap in range(TAPS):
            w_ref[0, :, tap * LANES : (tap + 1) * LANES] = flat[
                tap * channels : (tap + 1) * channels, :
            ]

        @pl.when(ids_ref[2] == 0)
        def _():
            @pl.when(t == 0)
            def _():
                for j in range(4):
                    x_ref[:, span(ids_ref[0] ^ j, LANES)] = x_in[j][...]

            def one_image(i):
                rows = span(ids_ref[0] ^ i, size)
                x = x_ref[rows, :]
                _, _, gate = attend(x, x, down_ref[0], up_ref[0])
                u = (gate * x.astype(F32)).astype(BF)
                u_ref[i] = u
                value = fold_taps(dot(u, w_ref[0]), cols)
                f_ref[i] = value.astype(BF)
                kept = value * mask_ref[rows, :].astype(F32)
                cells[0, span(ids_ref[0] ^ i, size // 4), :] = pool_pairs(
                    kept, pairs_ref, cols
                ).astype(BF)

            all_of(4, one_image)
            for j in range(4):
                fields[j][0] = u_ref[j]
                feats[j][0] = f_ref[j]

        @pl.when(ids_ref[2] == 1)
        def _():
            for j in range(4):
                c_ref[j] = cot_in[j][0]

            def one_image(i):
                @pl.when(label_at(label_ref, ids_ref, ids_ref[0] ^ i, t) == 1)
                def _():
                    u_ref[i] = dot_nt(spread_taps(c_ref[i].astype(F32), cols), w_ref[0]).astype(BF)

            all_of(4, one_image)
            for j in range(4):
                device = ids_ref[0] ^ j

                @pl.when(t == 0)
                def _(j=j):
                    du[j][...] = jnp.zeros_like(du[j])

                @pl.when(label_at(label_ref, ids_ref, device, t) == 1)
                def _(j=j, device=device):
                    du[j][slot_of(label_ref, ids_ref, device, t)] = u_ref[j]

    def step(shape, only=None):
        return pl.BlockSpec(
            (1,) + shape[1:],
            lambda t, ids, _: (t if only is None else jnp.where(ids[2] == only, t, 0),)
            + (0,) * (len(shape) - 1),
        )

    def same(shape):
        return pl.BlockSpec(shape, lambda t, ids, _: (0,) * len(shape))

    outs = [(tasks_n, size, channels)] * 4 + [(tasks_n, size, LANES)] * 5 + [(2, size, channels)] * 4
    outs.append((tasks_n, channels, TAPS * LANES))
    args = list(x_slices) + [down, up_t, gathered, mask] + list(cots)
    results = pl.pallas_call(
        unread(body, 1, 2 + len(args)),
        grid_spec=pltpu.PrefetchScalarGridSpec(
            num_scalar_prefetch=2,
            grid=(tasks_n,),
            in_specs=[same(a.shape) for a in x_slices]
            + [step(down.shape, 0), step(up_t.shape, 0)]
            + [pl.BlockSpec((4, 1, 4 * depth, LANES), lambda t, ids, _: (0, t, 0, 0)), same(mask.shape)]
            + [step(a.shape, 1) for a in cots]
            + [pl.BlockSpec(memory_space=pl.ANY)],
            out_specs=[step(shape, 0) for shape in outs[:9]]
            + [same(shape) for shape in outs[9:13]]
            + [step(outs[13])],
            scratch_shapes=[
                pltpu.VMEM((pixels, channels), BF),
                pltpu.VMEM((size // 2, LANES), F32),
                pltpu.VMEM((TAPS * channels, LANES), BF),
                pltpu.VMEM((4, size, channels), BF),
                pltpu.VMEM((4, size, LANES), BF),
                pltpu.VMEM((4, size, LANES), BF),
            ],
        ),
        out_shape=[jax.ShapeDtypeStruct(shape, BF) for shape in outs],
        compiler_params=pltpu.CompilerParams(vmem_limit_bytes=VMEM_BYTES),
        cost_estimate=LIGHT,
        name="section_tasks",
    )(line.ids, labels, *args, line.last)
    line.last = results[-1]
    return results[:4], results[4:8], results[8], results[9:13], results[13]


def grads_of_taps(field, grad_ref, taps_ref, flat, out_at, cols, depth):
    size = taps_ref.shape[0] // 4
    channels = field.shape[1]

    def spread(i):
        part = span(i, size)
        taps_ref[part, :] = spread_taps(grad_ref[part, :].astype(F32), cols)

    if grad_ref is not None:
        all_of(4, spread)

    def row_of_taps(row):
        whole = dot_tn(field[...], taps_ref[:, span(row, 3 * LANES)])
        for b in range(3):
            flat[span(3 * row + b, channels), :] = whole[:, b * LANES : (b + 1) * LANES].astype(BF)

    all_of(3, row_of_taps)

    def keep(r):
        out = out_at(r)
        for p in range(4):
            out[p] = flat[span(p * 4 + r, depth), :]

    all_of(4, keep)


def trunk_grads(line, enc_pairs, dec_pairs, depth, cols, name):
    count = len(enc_pairs)
    pixels, channels = enc_pairs[0][0].shape
    enc_in = [a for pair in enc_pairs for a in pair]
    dec_in = [a for pair in dec_pairs for a in pair]

    def body(ids_ref, *refs):
        given, out, taps_ref, flat = refs[: 2 * count], *refs[2 * count :]
        for n in range(count):
            h_ref, g_ref = given[2 * n], given[2 * n + 1]
            grads_of_taps(
                h_ref,
                g_ref,
                taps_ref,
                flat,
                lambda r: out.at[r, n],
                cols,
                depth,
            )

    return section_call(
        body,
        [((4, count, 4, depth, LANES), BF)],
        line,
        enc_in,
        name,
        scratch=[
            pltpu.VMEM((pixels, TAPS * LANES), BF),
            pltpu.VMEM((TAPS * channels, LANES), BF),
        ],
        paired=enumerate(dec_in),
    )[0]


def dec_task_grads(line, dec_xs, q_cells, mask, att, cots, enc_grads, depth, cols):
    tasks_n, size, _ = q_cells[0].shape
    pixels, channels = 4 * size, att.shape[1]

    def body(ids_ref, *refs, parts):
        x_in, q_in, mask_ref, att_ref, cot_in = refs[:4], refs[4:8], refs[8], refs[9], refs[10:14]
        u_ref, out, taps_ref, flat, x_ref, s_ref, pairs_ref, g_ref, field_ref = refs[14:]
        for j in range(4):
            x_ref[:, span(ids_ref[0] ^ j, LANES)] = x_in[j][...]

        def task(t):
            for j in range(4):
                g_ref[j * size : (j + 1) * size, :] = cot_in[j][t]

            def one_image(i):
                image = ids_ref[0] ^ i
                rows = span(image, size)
                x_low = x_ref[rows, :]
                x = x_low.astype(F32)
                own = mask_ref[rows, :]
                for j in range(4):
                    kept = q_in[j][t, span(image, size // 4), :].astype(F32)
                    cells = spread_pairs(kept, pairs_ref, cols)
                    s_ref[:, span(ids_ref[0] ^ j, LANES)] = cells.astype(BF) * own
                mixture = (x + s_ref[...].astype(F32)).astype(BF)
                _, _, gate = attend(x_low, mixture, att_ref[t], att_ref[tasks_n + t])
                field_ref[span(i, size), :] = (gate * x).astype(BF)

            all_of(4, one_image)
            u_ref[t] = field_ref[...]
            parts.send(0, t)
            grads_of_taps(field_ref, g_ref, taps_ref, flat, lambda r: out.at[r, t], cols, depth)

        each(tasks_n, task)

    return section_call(
        body,
        [((tasks_n, pixels, channels), BF), ((4, tasks_n, 4, depth, LANES), BF)],
        line,
        list(dec_xs) + list(q_cells) + [mask, att] + list(cots),
        "dec_task_grads",
        scratch=[
            pltpu.VMEM((pixels, TAPS * LANES), BF),
            pltpu.VMEM((TAPS * channels, LANES), BF),
            pltpu.VMEM((pixels, channels), BF),
            pltpu.VMEM((size, channels), BF),
            pltpu.VMEM((size // 2, LANES), F32),
            pltpu.VMEM((pixels, LANES), BF),
            pltpu.VMEM((pixels, channels), BF),
        ],
        only=1,
        other={1: enc_grads},
        split_out=(0,),
    )


def enc_tasks_reverse(line, labels, grad_pieces, fields, weights, mask, depth, cols):
    tasks_n, given_size, _ = grad_pieces[0].shape
    channels = weights.shape[1]
    size = 4 * given_size
    pixels = 4 * size

    def body(ids_ref, label_ref, *refs, parts):
        given, u_in, w_ref, mask_ref, outs = refs[:4], refs[4:8], refs[8], refs[9], refs[10:14]
        grads, pairs_ref, taps_ref, flat, whole, g_ref, back_ref = refs[14:]
        for j in range(4):
            outs[j][1] = jnp.zeros((size, channels), BF)
        def task(t):
            parts.need(8, t)
            for j in range(4):
                rows = slice(j * size, (j + 1) * size)
                cells = spread_pairs(given[j][t].astype(F32), pairs_ref, cols)
                g_ref[rows, :] = cells.astype(BF) * mask_ref[span(ids_ref[0] ^ j, size), :]
                parts.need(4 + j, t)
                whole[rows, :] = u_in[j][t]

            def spread(i):
                part = span(i, size)
                taps_ref[part, :] = spread_taps(g_ref[part, :].astype(F32), cols)
                device = ids_ref[0] ^ i

                @pl.when(label_at(label_ref, ids_ref, device, t) == 1)
                def _():
                    back_ref[i] = dot_nt(taps_ref[part, :], w_ref[t]).astype(BF)

            all_of(4, spread)
            for j in range(4):
                device = ids_ref[0] ^ j

                @pl.when(label_at(label_ref, ids_ref, device, t) == 1)
                def _(j=j, device=device):
                    outs[j][slot_of(label_ref, ids_ref, device, t)] = back_ref[j]

            grads_of_taps(whole, None, taps_ref, flat, lambda r: grads.at[r, t], cols, depth)

        each(tasks_n, task)

    return section_call(
        body,
        [((2, size, channels), BF)] * 4 + [((4, tasks_n, 4, depth, LANES), BF)],
        line,
        list(grad_pieces) + list(fields) + [weights, mask],
        "enc_tasks_back",
        scratch=[
            pltpu.VMEM((size // 2, LANES), F32),
            pltpu.VMEM((pixels, TAPS * LANES), BF),
            pltpu.VMEM((TAPS * channels, LANES), BF),
            pltpu.VMEM((pixels, channels), BF),
            pltpu.VMEM((pixels, LANES), BF),
            pltpu.VMEM((4, size, channels), BF),
        ],
        only=0,
        split_in=range(4, 9),
        smem=[labels],
    )


def dec_task_layer(line, fields, weights, enc_feats, cols, name):
    tasks_n, channels, _ = weights.shape
    size = fields.shape[1] // 4

    def body(ids_ref, u_ref, w_ref, *rest, parts):
        outs, all_ref = rest[:4], rest[4]

        def task(t):
            parts.need(1, t)
            parts.need(0, t)

            def convolve(i):
                value = dot(u_ref[t, span(i, size), :], w_ref[t])
                all_ref[i] = fold_taps(value, cols).astype(BF)

            all_of(4, convolve)
            for j in range(4):
                outs[j][t] = all_ref[j]

        each(tasks_n, task)

    return section_call(
        body,
        [((tasks_n, size, LANES), BF)] * 4,
        line,
        [fields, weights],
        name,
        scratch=[pltpu.VMEM((4, size, LANES), BF)],
        only=1,
        other=enumerate(enc_feats),
        split_in=(0, 1),
    )


def heads_reverse(line, labels, x_pieces, carried, mask, du_pieces, att, cols, name, only, other=None):
    size = x_pieces[0].shape[0] // 4
    channels = att.shape[1]
    tasks_n = att.shape[0] // 2
    carry = carried is not None

    def body(ids_ref, label_ref, *refs):
        x_in, rest = refs[:4], refs[4:]
        if carry:
            q_in, mask_ref, rest = rest[:4], rest[4], rest[5:]
        du_in, att_ref, rest = rest[:4], rest[4], rest[5:]
        outs, (x_ref, s_ref, ds_ref, da_ref, pairs_ref) = rest[:-5], rest[-5:]
        dx_ref, g_ref, grads = outs[0], outs[1], outs[2:6]
        for j in range(4):
            x_ref[:, span(ids_ref[0] ^ j, LANES)] = x_in[j][span(ids_ref[0], size), :]

        def task(t):
            x_low = x_ref[...]
            x = x_low.astype(F32)
            slot = slot_of(label_ref, ids_ref, ids_ref[0], t)
            if carry:
                own = mask_ref[span(ids_ref[0], size), :]
                for j in range(4):
                    kept = q_in[j][t, span(ids_ref[0], size // 4), :].astype(F32)
                    cells = spread_pairs(kept, pairs_ref, cols)
                    s_ref[:, span(ids_ref[0] ^ j, LANES)] = cells.astype(BF) * own
                mixture = (x + s_ref[...].astype(F32)).astype(BF)
            else:
                mixture = x_low
            inner, active, gate = attend(x, mixture, att_ref[t], att_ref[tasks_n + t])
            du = (
                (du_in[0][slot].astype(F32) + du_in[1][slot].astype(F32))
                + (du_in[2][slot].astype(F32) + du_in[3][slot].astype(F32))
            )
            gated = du * gate
            do = (gated * x * (1.0 - gate)).astype(BF)
            sig = jax.nn.sigmoid(inner)
            dk = (dot(do, att_ref[tasks_n + t]) * (sig * (1.0 + inner * (1.0 - sig)))).astype(BF)
            ds = dot_nt(dk, att_ref[t])
            dx_ref[t] = gated + ds
            if carry:
                ds_ref[...] = ds
                for j in range(4):
                    kept = ds_ref[:, span(ids_ref[0] ^ j, LANES)] * own.astype(F32)
                    outs[6 + j][t] = pool_pairs(kept, pairs_ref, cols).astype(BF)
            for row, value in ((t, dot_tn(mixture, dk)), (tasks_n + t, dot_tn(do, active))):
                da_ref[...] = value
                for j in range(4):
                    grads[j][row] = da_ref[span(ids_ref[0] ^ j, LANES), :].astype(BF)

        def no_task(t):
            dx_ref[t] = jnp.zeros((size, channels), F32)
            for j in range(4):
                if carry:
                    outs[6 + j][t] = jnp.zeros((size // 4, LANES), BF)
                grads[j][t] = jnp.zeros((LANES, LANES), BF)
                grads[j][tasks_n + t] = jnp.zeros((LANES, LANES), BF)

        def either(t):
            label = label_at(label_ref, ids_ref, ids_ref[0], t)
            pl.when(label == 1)(functools.partial(task, t))
            pl.when(label != 1)(functools.partial(no_task, t))

        each(tasks_n, either)
        row = 0
        g_ref[...] = jnp.zeros_like(g_ref)
        for a in range(tasks_n):
            for b in range(a, tasks_n):
                line_sum = jnp.sum(dx_ref[a] * dx_ref[b], axis=0, keepdims=True)
                folded = line_sum[:, :LANES]
                for part in range(1, channels // LANES):
                    folded = folded + line_sum[:, part * LANES : (part + 1) * LANES]
                g_ref[row : row + 1, :] = folded
                row += 1

    outs = [((tasks_n, size, channels), F32), ((8, LANES), F32)]
    outs += [((2 * tasks_n, LANES, LANES), BF)] * 4
    if carry:
        outs += [((tasks_n, size // 4, LANES), BF)] * 4
    return section_call(
        body,
        outs,
        line,
        list(x_pieces) + (list(carried) + [mask] if carry else []) + list(du_pieces) + [att],
        name,
        scratch=[
            pltpu.VMEM((size, channels), BF),
            pltpu.VMEM((size, channels), BF),
            pltpu.VMEM((size, channels), F32),
            pltpu.VMEM((channels, LANES), F32),
            pltpu.VMEM((size // 2, LANES), F32),
        ],
        only=only,
        other=other,
        smem=[labels],
    )


def nash_values(lines, tasks_n):
    def full(row):
        return jnp.broadcast_to(jnp.sum(lines[row : row + 1, :], axis=1, keepdims=True), (8, LANES))

    gram = [[None] * tasks_n for _ in range(tasks_n)]
    row = 0
    for a in range(tasks_n):
        for b in range(a, tasks_n):
            gram[a][b] = gram[b][a] = full(row)
            row += 1
    trace_mean = (gram[0][0] + gram[1][1] + gram[2][2]) / 3.0 + 1e-06
    norm = [[gram[a][b] / trace_mean for b in range(3)] for a in range(3)]
    alpha = [lax.rsqrt(norm[a][a] + 1e-06) for a in range(3)]
    for _ in range(NASH_ITERS):
        right = [
            norm[a][0] * alpha[0] + norm[a][1] * alpha[1] + norm[a][2] * alpha[2] - 1.0 / alpha[a]
            for a in range(3)
        ]
        matrix = [
            [norm[a][b] + 1.0 / (alpha[a] * alpha[a]) if a == b else norm[a][b] for b in range(3)]
            for a in range(3)
        ]
        cof = [[None] * 3 for _ in range(3)]
        for a in range(3):
            for b in range(3):
                a1, a2, b1, b2 = (a + 1) % 3, (a + 2) % 3, (b + 1) % 3, (b + 2) % 3
                cof[a][b] = matrix[a1][b1] * matrix[a2][b2] - matrix[a1][b2] * matrix[a2][b1]
        determinant = (
            matrix[0][0] * cof[0][0] + matrix[0][1] * cof[0][1] + matrix[0][2] * cof[0][2]
        )
        update = [
            (cof[0][b] * right[0] + cof[1][b] * right[1] + cof[2][b] * right[2]) / determinant
            for b in range(3)
        ]
        alpha = [alpha[a] * jnp.exp(-0.5 * jnp.tanh(update[a] / alpha[a])) for a in range(3)]
    return alpha


def weigh(line, dx, w_or_lines, solve, name):
    tasks_n, size, channels = dx.shape

    def body(ids_ref, *refs):
        given, dx_ref, outs, total = refs[: len(w_or_lines)], refs[len(w_or_lines)], refs[-6:-1], refs[-1]
        if solve:
            lines = (given[0][0] + given[0][1]) + (given[0][2] + given[0][3])
            alpha = nash_values(lines, tasks_n)
            outs[0][...] = jnp.concatenate(
                [alpha[t][:1] for t in range(3)] + [jnp.zeros((5, LANES), F32)], axis=0
            )
        else:
            outs[0][...] = given[0][...]
        acc = None
        for t in range(tasks_n):
            scale = jnp.tile(outs[0][t : t + 1, :], (1, channels // LANES))
            term = dx_ref[t] * scale
            acc = term if acc is None else acc + term
        total[...] = acc
        for j in range(4):
            outs[1 + j][...] = total[:, span(ids_ref[0] ^ j, LANES)].astype(BF)

    return kernel_call(
        body,
        [((8, LANES), F32)] + [((size, LANES), BF)] * 4,
        line,
        list(w_or_lines) + [dx],
        name,
        scratch=[pltpu.VMEM((size, channels), F32)],
    )


def trunk_reverse(
    line, pieces, by_image, cells, mask, normed, inverse, norms, layer, weight, cols, parts, other, name, only
):
    pixels = normed.shape[0]
    size = pixels // 4
    channels = weight.shape[1]
    takes, gives = cells is not None, "cells" in parts
    shapes = {"slices": (pixels, LANES), "images": (size, channels), "cells": (size, LANES)}

    def body(ids_ref, *refs):
        given, rest = refs[:4], refs[4:]
        if takes:
            cells_in, rest = rest[:4], rest[4:]
        if takes or gives:
            mask_ref, rest = rest[0], rest[1:]
        (n_ref, inv_ref, norm_ref, w_ref), rest = rest[:4], rest[4:]
        if other is not None:
            other_in, rest = rest[:4], rest[4:]
        outs, (acc_ref, back_ref, pairs_ref) = rest[:-3], rest[-3:]
        gain = norm_ref[layer : layer + 1, :]

        @pl.when(ids_ref[2] == only)
        def _():
            if by_image:
                for j in range(4):
                    acc_ref[span(ids_ref[0] ^ j, size), :] = given[j][...].astype(F32)
            else:
                acc_ref[...] = (given[0][...].astype(F32) + given[1][...].astype(F32)) + (
                    given[2][...].astype(F32) + given[3][...].astype(F32)
                )
            grad = acc_ref[...]
            if takes:
                start = (cells_in[0][...].astype(F32) + cells_in[1][...].astype(F32)) + (
                    cells_in[2][...].astype(F32) + cells_in[3][...].astype(F32)
                )
                start = start.astype(BF).astype(F32)
                grad = grad + spread_pairs(start, pairs_ref, cols) * mask_ref[...].astype(F32)
            normed_value = n_ref[...]
            preact = gain * normed_value + norm_ref[2 + layer : 3 + layer, :]
            sig = jax.nn.sigmoid(preact)
            dp = grad * (sig * (1.0 + preact * (1.0 - sig)))
            bias_total = jnp.sum(dp, axis=0, keepdims=True)
            gain_total = jnp.sum(dp * normed_value, axis=0, keepdims=True)
            outs[1][...] = jnp.concatenate(
                [gain_total, bias_total, jnp.zeros((6, LANES), F32)], axis=0
            )
            scale = inv_ref[0:1, :] * gain
            dv = scale * (dp - bias_total / pixels - normed_value * (gain_total / pixels))
            outs[0][...] = dv.astype(BF)
            acc_ref[...] = dv.astype(BF).astype(F32)

            def convolve(i):
                part = span(i, size)
                back_ref[part, :] = dot_nt(spread_taps(acc_ref[part, :], cols), w_ref[0])

            all_of(4, convolve)
            for at, kind in enumerate(parts):
                for j in range(4):
                    peer = ids_ref[0] ^ j
                    out = outs[2 + 4 * at + j]
                    if kind == "images":
                        out[...] = back_ref[span(peer, size), :].astype(BF)
                    elif kind == "slices":
                        out[...] = back_ref[:, span(peer, LANES)].astype(BF)
                    else:
                        kept = back_ref[:, span(peer, LANES)] * mask_ref[...].astype(F32)
                        out[...] = pool_pairs(kept, pairs_ref, cols).astype(BF)

        if other is not None:

            @pl.when(ids_ref[2] != only)
            def _():
                for j in range(4):
                    outs[2 + 4 * parts.index("images") + j][...] = other_in[j][...]

    outs = [((pixels, LANES), BF), ((8, LANES), F32)]
    for kind in parts:
        outs += [(shapes[kind], BF)] * 4
    extra = list(cells) if takes else []
    if takes or gives:
        extra.append(mask)
    return kernel_call(
        body,
        outs,
        line,
        list(pieces) + extra + [normed, inverse, norms, weight] + list(other or []),
        name,
        scratch=[
            pltpu.VMEM((pixels, LANES), F32),
            pltpu.VMEM((pixels, channels), F32),
            pltpu.VMEM((pixels // 2, LANES), F32),
        ],
    )


def plane_device(
    x_in,
    pool_index,
    task_mask,
    task_cot,
    trunk_conv,
    norm_gain,
    norm_bias,
    att_down,
    attention_up_weights,
    task_conv,
):
    micro_count, _, rows_n, cols, channels = x_in.shape
    tasks_n = task_cot.shape[0]
    strip = rows_n * cols
    size = strip * micro_count
    depth = trunk_conv.shape[2]
    part = att_down.shape[2]
    section = lax.axis_index("pipe")
    decoder = section == 1
    row_at = lax.axis_index("rows")
    line = Line(jnp.stack([lax.axis_index("dp"), row_at, section]).astype(jnp.int32))
    ENC, DEC, BOTH = (0,), (1,), (0, 1)

    norm_own = jnp.concatenate([norm_gain[0], norm_bias[0]], axis=0)
    own_lanes = jnp.arange(LANES) // part == row_at
    norm_own = jnp.where(own_lanes[None], jnp.tile(norm_own, (1, LANES // part)), 0).astype(BF)
    norm_own = jnp.pad(norm_own, ((0, 12), (0, 0)))
    att_own = jnp.concatenate(
        [att_down[0], jnp.swapaxes(attention_up_weights[0], 1, 2)], axis=0
    ).reshape(2 * tasks_n * part, LANES)

    trunk_cut = trade(cut_weights(line, [(trunk_conv[0], [0, 1])], "cut_trunk"), "dp", BOTH)

    labels = lax.all_gather(task_mask, "dp").reshape(-1)

    picked = pool_index[:, 0, :, None, :, None]
    place = jnp.arange(2)[:, None, None] * 2 + jnp.arange(2)[None, None, :]
    cells = (picked == place[None, None]).astype(BF)
    cells = jnp.broadcast_to(cells.reshape(micro_count, strip, 1), (micro_count, strip, LANES))
    strips = x_in.reshape(micro_count, strip, channels)

    def cut_input(ids_ref, x_ref, m_ref, *outs):
        for j in range(4):
            outs[j][:, :channels] = x_ref[ids_ref[1] ^ j]
            outs[j][:, channels:] = m_ref[ids_ref[1] ^ j]

    strips = kernel_call(
        cut_input, [((strip, channels + LANES), BF)] * 4, line, [strips, cells], "cut_input"
    )
    strips = trade(strips, "rows", BOTH)

    trunk_block = stack_weights(line, trunk_cut, [[0, 1]], [[norm_own, att_own]], "stack_trunk")[0]
    trunk_all = lax.all_gather(trunk_block, "rows")

    def place_input(ids_ref, a, b, c, e, o_ref):
        for j, piece in enumerate((a, b, c, e)):
            o_ref[span(ids_ref[1] ^ j, strip), :] = piece[...]

    x_image = kernel_call(
        place_input, [((size, channels + LANES), BF)], line, strips, "place_input"
    )[0]
    x_images = trade([x_image] * 4, "dp", ENC)
    task_cut = trade(
        cut_weights(line, [(task_conv[0], range(tasks_n))], "cut_tasks"), "dp", BOTH
    )
    anchor(line, x_images, "input_there")
    task_block = stack_weights(line, task_cut, [list(range(tasks_n))], [[]], "stack_tasks")[0]
    task_all = lax.all_gather(task_block, "rows")

    half = channels // 2

    def cut_cot(ids_ref, mask_ref, c_ref, *outs):
        for j in range(4):
            micro = ids_ref[1] ^ j
            for t in range(tasks_n):
                labelled = mask_ref[micro * tasks_n + t].astype(F32)
                value = c_ref[t, micro, :, span(ids_ref[2], half)].astype(F32)
                outs[j][t] = (value * labelled).astype(BF)

    cot_strips = kernel_call(
        cut_cot,
        [((tasks_n, strip, half), BF)] * 4,
        line,
        [task_cot.reshape(tasks_n, micro_count, strip, channels)],
        "cut_cotangents",
        smem=[task_mask.reshape(-1)],
    )
    cot_strips = trade(cot_strips, "rows", BOTH)

    def place_cot(ids_ref, _, a, b, c, e, o_ref):
        for j, piece in enumerate((a, b, c, e)):
            for t in range(tasks_n):
                o_ref[t, span(ids_ref[1] ^ j, strip), :] = piece[t]

    cot_half = kernel_call(
        place_cot, [((tasks_n, size, half), BF)], line, cot_strips, "place_cotangents", smem=[labels]
    )[0]
    cot_other = swap_sections([cot_half])[0]

    def slice_cot(ids_ref, own_ref, other_ref, *rest):
        outs, image = rest[:4], rest[4]
        image[:, :, :half] = other_ref[...]
        image[:, :, half:] = own_ref[...]
        for j in range(4):
            outs[j][...] = image[:, :, span(ids_ref[0] ^ j, LANES)]

    cots = kernel_call(
        slice_cot,
        [((tasks_n, size, LANES), BF)] * 4,
        line,
        [cot_half, cot_other],
        "slice_cotangents",
        scratch=[pltpu.VMEM((tasks_n, size, channels), BF)],
    )
    cots = trade(cots, "dp", DEC)
    first_w, second_w, norms, att_rows = place_weights(
        line, trunk_all, 2, depth, "place_trunk", norm_own.shape[0], att_own.shape[0]
    )
    enc_h0, enc_n1, enc_i1, enc_h, mask = trunk_layer(
        line, x_images, first_w, norms, 0, cols, eps, "images", False, None, "enc_layer1", 0
    )
    enc_hs = trade([enc_h] * 4, "dp", BOTH)
    dec_mask = swap_sections([mask])[0]
    att = place_attention(line, trade([att_rows] * 4, "dp", BOTH), 2 * tasks_n, part)
    anchor(line, cots, "cotangents_there")
    enc_h1, enc_n2, enc_i2, enc_x, z = trunk_layer(
        line, enc_hs, second_w, norms, 1, cols, eps, "slices", True, mask, "enc_layer2", 0
    )
    z_pieces = swap_sections([z] * 4)
    enc_xs = trade([enc_x] * 4, "dp", ENC)

    dec_h0, dec_n1, dec_i1, dec_h = trunk_layer(
        line, z_pieces, first_w, norms, 0, cols, eps, "cells", False, dec_mask, "dec_layer1", 1
    )
    dec_hs = trade([dec_h] * 4, "dp", DEC)

    dec_h1, dec_n2, dec_i2, dec_x = trunk_layer(
        line, dec_hs, second_w, norms, 1, cols, eps, "slices", True, None, "dec_layer2", 1
    )
    dec_xs = trade([dec_x] * 4, "dp", BOTH)

    gathered = task_all.reshape(4, tasks_n, 4 * depth, LANES)
    enc_us, enc_feats, kept, du, task_w = section_tasks(
        line, labels, enc_xs, att, gathered, depth, mask, cots, cols
    )
    anchor(line, dec_xs, "decoder_there")
    dec_du = trade(du, "dp", DEC)
    q_cells = swap_sections([kept] * 4)

    dec_dx, lines, *rest = heads_reverse(
        line, labels, dec_xs, q_cells, dec_mask, dec_du, att, cols, "dec_heads", 1
    )
    dec_att, ds = rest[:4], rest[4:]
    ds = swap_sections(ds)
    lines = jnp.sum(lax.all_gather(lines, "dp"), axis=0)
    terms = lax.all_gather(lines, "rows")
    dec_w, *dh = weigh(line, dec_dx, [terms], True, "bargain")
    dh = trade(dh, "dp", BOTH)
    enc_w = swap_sections([dec_w])[0]
    nash_w = jnp.where(decoder, dec_w, enc_w)

    anchor(line, dh, "bargain_there")
    *du, enc_dw = enc_tasks_reverse(
        line, labels, ds, enc_us, task_w, mask, depth, cols
    )
    enc_du = trade(du, "dp", ENC)
    dec_dv2, dec_s2, *dh = trunk_reverse(
        line, dh, True, None, None, dec_n2, dec_i2, norms, 1, second_w, cols, ["slices"], None, "dec_back2", 1
    )
    dh = trade(dh, "dp", DEC)
    dec_u, task_dw = dec_task_grads(
        line, dec_xs, q_cells, dec_mask, att, cots, enc_dw, depth, cols
    )
    task_dw = lax.psum_scatter(task_dw, "rows", scatter_dimension=0, tiled=True)
    dec_dv1, dec_s1, *rest = trunk_reverse(
        line, dh, False, None, dec_mask, dec_n1, dec_i1, norms, 0, first_w, cols, ["cells", "images"], None, "dec_back1", 1
    )
    dec_start, dec_dz = swap_sections(rest[:4]), rest[4:]
    enc_dx, _, *att_parts = heads_reverse(
        line, labels, enc_xs, None, None, enc_du, att, cols, "enc_heads_back", 0, {k + 2: a for k, a in enumerate(dec_att)}
    )
    _, *dh = weigh(line, enc_dx, [enc_w], False, "enc_weigh")
    dh = trade(dh, "dp", BOTH)
    att_parts = trade(att_parts, "dp", BOTH)

    feats = dec_task_layer(line, dec_u, task_w, enc_feats, cols, "dec_tasks")
    feats = trade(feats, "dp", BOTH)
    enc_dv2, enc_s2, *dh = trunk_reverse(
        line, dh, True, dec_start, mask, enc_n2, enc_i2, norms, 1, second_w, cols, ["slices"], None, "enc_back2", 0
    )
    dh = trade(dh, "dp", BOTH)

    enc_dv1, enc_s1, *dz = trunk_reverse(
        line, dh, False, None, None, enc_n1, enc_i1, norms, 0, first_w, cols, ["images"], dec_dz, "enc_back1", 0
    )
    dz = trade(dz, "dp", BOTH)
    trunk_dw = trunk_grads(
        line,
        [(enc_h0, enc_dv1), (enc_h1, enc_dv2)],
        [(dec_h0, dec_dv1), (dec_h1, dec_dv2)],
        depth,
        cols,
        "trunk_grads",
    )
    trunk_dw = lax.psum_scatter(trunk_dw, "rows", scatter_dimension=0, tiled=True)


    def cut_shares(sums, name):
        count = sums.shape[1]

        def cut(ids_ref, g_ref, *outs):
            for j in range(4):
                for n in range(count):
                    outs[j][n] = g_ref[0, n, ids_ref[0] ^ j]

        return kernel_call(cut, [((count, depth, LANES), BF)] * 4, line, [sums], name)

    def join(layers, scale, name):
        counts = [pieces[0].shape[0] for pieces in layers]

        def body(ids_ref, *refs):
            o_ref, at = refs[-1], 0
            for m, count in enumerate(counts):
                for n in range(count):
                    for j in range(4):
                        value = refs[4 * m + j][n].astype(F32)
                        if scale is not None:
                            value = value * refs[4 * len(counts)][n : n + 1, :]
                        o_ref[at, :, span(ids_ref[0] ^ j, LANES)] = value
                    at += 1

        return kernel_call(
            body,
            [((sum(counts), depth, channels), F32)],
            line,
            [piece for pieces in layers for piece in pieces] + ([] if scale is None else [scale]),
            name,
        )[0]

    def cut_att(ids_ref, a, b, c, e, *rest):
        outs, total = rest[:4], rest[4]
        total[...] = (a[...].astype(F32) + b[...].astype(F32)) + (
            c[...].astype(F32) + e[...].astype(F32)
        )
        for j in range(4):
            outs[j][...] = total[:, span(ids_ref[1] ^ j, part), :].astype(BF)

    att_parts = kernel_call(
        cut_att,
        [((2 * tasks_n, part, LANES), BF)] * 4,
        line,
        att_parts,
        "cut_attention",
        scratch=[pltpu.VMEM((2 * tasks_n, LANES, LANES), F32)],
    )
    att_parts = trade(att_parts, "rows", BOTH)

    def cut_feats(ids_ref, a, b, c, e, *rest):
        outs, image = rest[:4], rest[4]
        for j, piece in enumerate((a, b, c, e)):
            image[:, :, span(ids_ref[0] ^ j, LANES)] = piece[...]
        for j in range(4):
            outs[j][...] = image[:, span(ids_ref[1] ^ j, strip), :]

    feats = kernel_call(
        cut_feats,
        [((tasks_n, strip, channels), BF)] * 4,
        line,
        feats,
        "cut_features",
        scratch=[pltpu.VMEM((tasks_n, size, channels), BF)],
    )
    feats = trade(feats, "rows", BOTH)

    sums = jnp.where(
        decoder, jnp.concatenate([dec_s1, dec_s2]), jnp.concatenate([enc_s1, enc_s2])
    )
    sums = trade([sums] * 4, "rows", BOTH)
    sums = (sums[0] + sums[1]) + (sums[2] + sums[3])
    sums = lax.dynamic_slice_in_dim(sums, row_at * part, part, axis=1)
    gain_out = jnp.stack([sums[0], sums[8]])
    bias_out = jnp.stack([sums[1], sums[9]])

    def cut_start(ids_ref, a, b, c, e, *rest):
        outs, image = rest[:4], rest[4]
        image[...] = (a[...].astype(F32) + b[...].astype(F32)) + (
            c[...].astype(F32) + e[...].astype(F32)
        )
        for j in range(4):
            outs[j][...] = image[span(ids_ref[1] ^ j, strip), :].astype(BF)

    starts = kernel_call(
        cut_start,
        [((strip, channels), BF)] * 4,
        line,
        dz,
        "cut_start",
        scratch=[pltpu.VMEM((size, channels), F32)],
    )
    starts = trade(starts, "rows", BOTH)

    task_parts = trade(cut_shares(task_dw, "share_tasks"), "dp", BOTH)

    def join_att(ids_ref, a, b, c, e, w_ref, o_ref):
        total = (a[...].astype(F32) + b[...].astype(F32)) + (
            c[...].astype(F32) + e[...].astype(F32)
        )
        for t in range(2 * tasks_n):
            at = t % tasks_n
            o_ref[t] = total[t] * w_ref[at : at + 1, :]

    att_out = kernel_call(
        join_att,
        [((2 * tasks_n, part, LANES), F32)],
        line,
        att_parts + [nash_w],
        "join_attention",
    )[0]

    task_out = join([task_parts], nash_w, "join_tasks")
    trunk_parts = trade(cut_shares(trunk_dw, "share_trunk"), "dp", BOTH)

    def place_feats(ids_ref, a, b, c, e, o_ref):
        for j, piece in enumerate((a, b, c, e)):
            for t in range(tasks_n):
                o_ref[t, ids_ref[1] ^ j] = piece[t]

    feats_out = kernel_call(
        place_feats, [((tasks_n, micro_count, strip, channels), BF)], line, feats, "place_features"
    )[0]

    def place_start(ids_ref, a, b, c, e, o_ref):
        for j, piece in enumerate((a, b, c, e)):
            o_ref[ids_ref[1] ^ j] = piece[...].astype(F32)

    start_out = kernel_call(
        place_start, [((micro_count, strip, channels), F32)], line, starts, "place_start"
    )[0]
    trunk_out = join([trunk_parts], None, "join_trunk")

    return (
        feats_out.reshape(1, tasks_n, micro_count, 1, rows_n, cols, channels),
        start_out.reshape(1, micro_count, 1, rows_n, cols, channels),
        trunk_out[None],
        gain_out[None],
        bias_out[None],
        att_out[:tasks_n][None],
        jnp.swapaxes(att_out[tasks_n:], 1, 2)[None],
        task_out[None],
        nash_w[:3, 0],
    )


def by_planes(x_in, task_cot):
    peers, planes = lax.axis_size("dp"), lax.axis_size("rows")
    micro, samples, _, _, channels = x_in.shape
    return (
        peers == 4
        and planes == 4
        and micro == planes
        and samples == 1
        and channels == peers * LANES
        and task_cot.shape[0] == 3
    )


def section_device(*arrays):
    if by_planes(arrays[0], arrays[3]):
        return plane_device(*arrays)
    return on_device(*arrays)


def solution(mesh):
    in_specs = (
        P(None, "dp", "rows", None, None),
        P(None, "dp", "rows", None),
        P(None, "dp", None),
        P(None, None, "dp", "rows", None, None),
        P("pipe", None, ("dp", "rows"), None),
        P("pipe", None, ("dp", "rows")),
        P("pipe", None, ("dp", "rows")),
        P("pipe", None, ("dp", "rows"), None),
        P("pipe", None, None, ("dp", "rows")),
        P("pipe", None, ("dp", "rows"), None),
    )
    out_specs = (
        P("pipe", None, None, "dp", "rows", None, None),
        P("pipe", None, "dp", "rows", None, None),
        P("pipe", None, ("dp", "rows"), None),
        P("pipe", None, ("dp", "rows")),
        P("pipe", None, ("dp", "rows")),
        P("pipe", None, ("dp", "rows"), None),
        P("pipe", None, None, ("dp", "rows")),
        P("pipe", None, ("dp", "rows"), None),
        P(),
    )
    return jax.shard_map(
        section_device, mesh=mesh, in_specs=in_specs, out_specs=out_specs, check_vma=False
    )
```
